32 devices in a mesh: dp: 16 (over z, y, x), fsdp: 2 (over core).
Axes of the slice: x: 2, y: 2, z: 4, core: 2. Of those that a mesh axis runs over, the one named last changes fastest.
Arguments:
- tokens_in: bfloat16 [4096, 768], P(('dp', 'fsdp')), may hold values from -6 to 6
- cotangent: bfloat16 [4096, 768], P(('dp', 'fsdp')), may hold values from -6 to 6
- seq_lengths: int32 [16, 3], P('dp'), may hold values from 0 to 256, as said below
- w_qkv: float32 [768, 2304], P(None, ('dp', 'fsdp')), may hold values from -0.21875 to 0.21875
- w_out: float32 [768, 768], P(None, ('dp', 'fsdp')), may hold values from -0.625 to 0.625
- w_up: float32 [768, 3072], P(None, ('dp', 'fsdp')), may hold values from -0.21875 to 0.21875
- w_down: float32 [3072, 768], P(('dp', 'fsdp')), may hold values from -0.109375 to 0.109375
- vectors: float32 [12, 768], P(None, ('dp', 'fsdp')), may hold values from -1.2 to 1.4, as said below
- mom_qkv: float32 [768, 2304], P(None, ('dp', 'fsdp')), may hold values from -192 to 192
- mom_out: float32 [768, 768], P(None, ('dp', 'fsdp')), may hold values from -192 to 192
- mom_up: float32 [768, 3072], P(None, ('dp', 'fsdp')), may hold values from -192 to 192
- mom_down: float32 [3072, 768], P(('dp', 'fsdp')), may hold values from -192 to 192
- adam_first: float32 [12, 768], P(None, ('dp', 'fsdp')), may hold values from -40 to 40
- adam_second: float32 [12, 768], P(None, ('dp', 'fsdp')), may hold values from 4.096 to 16.384
Outputs:
- output: bfloat16 [4096, 768], P(('dp', 'fsdp'))
- d_tokens: float32 [4096, 768], P(('dp', 'fsdp'))
- grad_qkv: float32 [768, 2304], P(None, ('dp', 'fsdp'))
- grad_out: float32 [768, 768], P(None, ('dp', 'fsdp'))
- grad_up: float32 [768, 3072], P(None, ('dp', 'fsdp'))
- grad_down: float32 [3072, 768], P(('dp', 'fsdp'))
- grad_vectors: float32 [12, 768], P(None, ('dp', 'fsdp'))
- new_mom_qkv: float32 [768, 2304], P(None, ('dp', 'fsdp'))
- new_mom_out: float32 [768, 768], P(None, ('dp', 'fsdp'))
- new_mom_up: float32 [768, 3072], P(None, ('dp', 'fsdp'))
- new_mom_down: float32 [3072, 768], P(('dp', 'fsdp'))
- new_w_qkv: float32 [768, 2304], P(None, ('dp', 'fsdp'))
- new_w_out: float32 [768, 768], P(None, ('dp', 'fsdp'))
- new_w_up: float32 [768, 3072], P(None, ('dp', 'fsdp'))
- new_w_down: float32 [3072, 768], P(('dp', 'fsdp'))
- new_first: float32 [12, 768], P(None, ('dp', 'fsdp'))
- new_second: float32 [12, 768], P(None, ('dp', 'fsdp'))
- new_vectors: float32 [12, 768], P(None, ('dp', 'fsdp'))
The draws below stay inside these ranges and needn't reach their ends.
Inputs may be any that keep to these rules, and one draw needn't show every extreme that they name: `seq_lengths`: row g holds the lengths of the 3 sequences of group g, laid end to end from its first position; the first is more than 128; a row sums to at most 256, the rest being padding; in some row the first length is 256. `vectors`: rows 0 and 2 (the norms' gains) lie between 0.6 and 1.4.
All inputs are finite; a program needn't handle non-finite values.
Results may differ from the reference program's by a relative error of at most 0.013.
The reference program's roundings to bfloat16 on the way count: a program that leaves them out, or rounds other values in their place, can miss the bound.
Values may be sent and summed in bfloat16 or wider, within the bound.
No kernel may reach another device: no remote copies, remote signals or barrier semaphores. Data moves between devices by JAX's collectives and lax.ppermute only.
A program may use at most 128 MiB of HBM per device.

```python
import math
import jax
import jax.numpy as jnp
from jax import lax

D = 768
H = 12
HD = 64
FF = 3072
TOK_DEV = 128
NSEQ = 3
NS_ITERS = 2
STEP = 10
GROUP = 256
TOKENS = 4096
VEC = 12
N_DP = 16


def draw_seq_lengths(key, part):
    key = jax.random.fold_in(key, 11)
    key_list = jax.random.split(key, 4)
    first_len = jax.random.randint(key_list[0], (N_DP,), TOK_DEV + 1, GROUP + 1)
    full_group = jax.random.randint(key_list[1], (), 0, N_DP)
    first_len = jnp.where(jnp.arange(N_DP) == full_group, GROUP, first_len)
    remaining = GROUP - first_len
    second_len = jax.random.randint(key_list[2], (N_DP,), 0, remaining + 1)
    third_len = jax.random.randint(key_list[3], (N_DP,), 0, remaining - second_len + 1)
    return jnp.stack([first_len, second_len, third_len], axis=1).astype(jnp.int32)


def draw_vectors(key, part):
    key = jax.random.fold_in(key, 23)
    key_gain, key_bias = jax.random.split(key)
    gains = jax.random.uniform(key_gain, (VEC, D), jnp.float32, 0.7, 1.3)
    biases = jnp.clip(0.3 * jax.random.normal(key_bias, (VEC, D), jnp.float32), -1.2, 1.2)
    row_index = jnp.arange(VEC)[:, None]
    return jnp.where((row_index == 0) | (row_index == 2), gains, biases)


def strengthened(result, stream_key, source, target, blocks, factor):
    def block_of(axis_at):
        return (jnp.arange(result.shape[axis_at]) // (result.shape[axis_at] // blocks)).reshape((-1,) + (1,) * (result.ndim - 1 - axis_at))

    one_side = jax.random.permutation(stream_key, blocks)[block_of(target)]
    second = (block_of(target) + blocks // 2) % blocks
    return jnp.where((block_of(source) == one_side) | (block_of(source) == second), factor * result, result)


def shard_levels(rng, dims, shards, low, high):
    def one(axis_at, parts):
        steps = jax.random.uniform(jax.random.fold_in(jax.random.fold_in(rng, 6), axis_at), (parts,), jnp.float32, low / len(shards), high / len(shards))
        return jnp.repeat(jnp.exp(steps), dims[axis_at] // parts).reshape((-1,) + (1,) * (len(dims) - axis_at - 1))

    factor_of = one(*shards[0])
    for cut in shards[1:]:
        factor_of = factor_of * one(*cut)
    return factor_of


def gaussian(rng, shape, width, bound, pieces=(), held_as=jnp.bfloat16):
    level = shard_levels(rng, shape, pieces, -0.22, 0.18) if pieces else 1.0
    drawn = jax.random.normal(rng, shape, jnp.float32) * width * level
    return jnp.minimum(jnp.maximum(drawn, -bound), bound).astype(held_as)


def bell_draw_with(own_key, shape, width, most, shards, heavy, held_as=jnp.bfloat16):
    result = width * jax.random.normal(own_key, shape, jnp.float32)
    if shards:
        result = result * shard_levels(own_key, shape, shards, -0.22, 0.18)
    return jnp.clip(strengthened(result, jax.random.fold_in(own_key, 3), *heavy), -most, most).astype(held_as)


def setup_inputs(seed: int = 0) -> dict:
    keys = jax.random.split(jax.random.key(seed), 15)
    return {
        "tokens_in": gaussian(keys[0], (TOKENS, D), 1.0, 6.0, ((0, 32),)),
        "cotangent": bell_draw_with(keys[1], (TOKENS, D), 1.0, 6.0, ((0, 32),), (0, 1, 32, 2.75)),
        "seq_lengths": draw_seq_lengths(jax.random.fold_in(keys[14], 71), 0),
        "w_qkv": gaussian(keys[3], (D, 3 * D), D ** -0.5, 0.21875, ((1, 32),), jnp.float32),
        "w_out": gaussian(keys[4], (D, D), (D // 8) ** -0.5, 0.625, ((1, 32),), jnp.float32),
        "w_up": gaussian(keys[5], (D, FF), D ** -0.5, 0.21875, ((1, 32),), jnp.float32),
        "w_down": gaussian(keys[6], (FF, D), FF ** -0.5, 0.109375, ((0, 32),), jnp.float32),
        "vectors": draw_vectors(jax.random.fold_in(keys[14], 71), 0),
        "mom_qkv": gaussian(keys[8], (D, 3 * D), (0.5 * TOKENS ** 0.5), 192.0, ((1, 32),), jnp.float32),
        "mom_out": gaussian(keys[9], (D, D), (0.5 * TOKENS ** 0.5), 192.0, ((1, 32),), jnp.float32),
        "mom_up": gaussian(keys[10], (D, FF), (0.5 * TOKENS ** 0.5), 192.0, ((1, 32),), jnp.float32),
        "mom_down": gaussian(keys[11], (FF, D), (0.5 * TOKENS ** 0.5), 192.0, ((0, 32),), jnp.float32),
        "adam_first": gaussian(keys[12], (VEC, D), (TOKENS ** 0.5 / 9), 40.0, ((1, 32),), jnp.float32),
        "adam_second": jnp.clip(jnp.exp(math.log(16.384) - 1.3862944 * jax.random.uniform(keys[13], (VEC, D), jnp.float32) ** shard_levels(keys[13], (VEC, D), ((1, 32),), -0.2, 0.2)), 4.096, 16.384),
    }


high_precision = lax.Precision.HIGHEST
poly_one = 3.4445
poly_three = -4.775
poly_five = 2.0315
momentum_decay = 0.95
muon_rate = 0.3
muon_decay = 0.01
adam_rate = 0.2
beta_one = 0.9
beta_two = 0.999
adam_epsilon = 1e-08
norm_epsilon = 1e-05
ortho_epsilon = 1e-07
masked_score = -1e+30

@jax.custom_vjp
def low(v):
    return lax.optimization_barrier(v.astype(jnp.bfloat16)).astype(jnp.float32)

@jax.custom_vjp
def low_back(v):
    return v

def low_keep(v):
    return (low(v), None)

def low_pass(kept, grad):
    return (grad,)

def back_keep(v):
    return (v, None)

def back_low(kept, grad):
    return (low(grad),)
low.defvjp(low_keep, low_pass)
low_back.defvjp(back_keep, back_low)

def rounded(values):
    return lax.optimization_barrier(values.astype(jnp.bfloat16)).astype(jnp.float32)

def matmul_high(left, right):
    return jnp.dot(left, right, precision=high_precision, preferred_element_type=jnp.float32)

def layer_norm(values, gain, shift):
    center = values - lax.optimization_barrier(jnp.mean(values, axis=-1, keepdims=True))
    spread = lax.optimization_barrier(jnp.mean(center * center, axis=-1, keepdims=True))
    return center * lax.rsqrt(spread + norm_epsilon) * gain + shift

def gelu_exact(values):
    return 0.5 * values * (1.0 + lax.erf(values * 0.7071067811865476))

def segment_ids(lengths):
    bounds = jnp.cumsum(lengths).astype(jnp.int32)
    places = jnp.arange(GROUP, dtype=jnp.int32)
    return lax.optimization_barrier(jnp.sum((places[:, None] >= bounds[None, :]).astype(jnp.int32), axis=1)).astype(jnp.int32)

def attend(query_rows, key_rows, value_rows, segments):
    scores = jnp.einsum('ihd,jhd->hij', query_rows, key_rows, precision=high_precision) * HD ** (-0.5)
    scores = low_back(scores)
    allowed = segments[:, None] == segments[None, :]
    scores = jnp.where(allowed[None], scores, masked_score)
    row_max = lax.optimization_barrier(jnp.max(scores, axis=-1, keepdims=True))
    exp_scores = jnp.exp(scores - row_max)
    probs = exp_scores / lax.optimization_barrier(jnp.sum(exp_scores, axis=-1, keepdims=True))
    return jnp.einsum('hij,jhd->ihd', low(probs), value_rows, precision=high_precision)

def forward(tokens_f, w_qkv, w_out, w_up, w_down, vectors, segments):
    w_qkv = low(w_qkv)
    w_out = low(w_out)
    w_up = low(w_up)
    w_down = low(w_down)
    vectors = low(vectors)
    zero_bias = jnp.zeros((D,), jnp.float32)
    projected = matmul_high(tokens_f, w_qkv) + jnp.concatenate([vectors[4], zero_bias, vectors[5]])
    projected = low(low_back(projected))
    shaped = projected.reshape(N_DP, GROUP, 3, H, HD)

    def one_group(inputs):
        block = inputs[0]
        return jax.checkpoint(attend)(block[:, 0], block[:, 1], block[:, 2], inputs[1])
    context = lax.map(one_group, (shaped, segments))
    context = low(low_back(context.reshape(TOKENS, D)))
    attended = low_back(matmul_high(context, w_out) + vectors[6])
    normed = layer_norm(tokens_f + attended, vectors[0], vectors[1])
    pre_up = low_back(matmul_high(low(normed), w_up) + vectors[8:].reshape(FF))
    activated = low(gelu_exact(pre_up))
    lowered = low_back(matmul_high(activated, w_down) + vectors[7])
    return layer_norm(normed + lowered, vectors[2], vectors[3])

def orthogonal(moment):
    low_x = rounded(moment)
    current = moment
    for iteration in range(NS_ITERS):
        if iteration > 0:
            low_x = rounded(current)
        gram_mat = matmul_high(low_x, low_x.T)
        factor = 1.0
        if iteration == 0:
            factor = 1.0 / (jnp.sqrt(jnp.trace(gram_mat)) + ortho_epsilon)
            gram_mat = gram_mat * (factor * factor)
            current = low_x * factor
        low_gram = rounded(gram_mat)
        mixing = poly_three * gram_mat + poly_five * matmul_high(low_gram, low_gram)
        current = poly_one * current + matmul_high(rounded(mixing), low_x) * factor
    return current

def reference(tokens_in, cotangent, seq_lengths, w_qkv, w_out, w_up, w_down, vectors, mom_qkv, mom_out, mom_up, mom_down, adam_first, adam_second):
    segments = jax.vmap(segment_ids)(seq_lengths)
    live_rows = (segments < NSEQ).astype(jnp.float32).reshape(TOKENS, 1)

    def wrapped(tokens_f, w_one, w_two, w_three, w_four, vector_rows):
        return forward(tokens_f, w_one, w_two, w_three, w_four, vector_rows, segments)
    final, pull_back = jax.vjp(wrapped, tokens_in.astype(jnp.float32), w_qkv, w_out, w_up, w_down, vectors)
    gradients = pull_back(cotangent.astype(jnp.float32) * live_rows)
    d_tokens, grad_qkv, grad_out, grad_up, grad_down, grad_vectors = gradients
    new_mom_qkv = momentum_decay * mom_qkv + grad_qkv
    new_mom_out = momentum_decay * mom_out + grad_out
    new_mom_up = momentum_decay * mom_up + grad_up
    new_mom_down = momentum_decay * mom_down + grad_down
    ortho_qkv = rounded(orthogonal(new_mom_qkv))
    ortho_out = rounded(orthogonal(new_mom_out))
    ortho_up = rounded(orthogonal(new_mom_up))
    ortho_down = rounded(orthogonal(new_mom_down.T)).T
    new_w_qkv = w_qkv - muon_rate * (0.2 * math.sqrt(max(D, 3 * D)) * ortho_qkv + muon_decay * w_qkv)
    new_w_out = w_out - muon_rate * (0.2 * math.sqrt(D) * ortho_out + muon_decay * w_out)
    new_w_up = w_up - muon_rate * (0.2 * math.sqrt(max(D, FF)) * ortho_up + muon_decay * w_up)
    new_w_down = w_down - muon_rate * (0.2 * math.sqrt(max(D, FF)) * ortho_down + muon_decay * w_down)
    new_first = beta_one * adam_first + (1.0 - beta_one) * grad_vectors
    new_second = beta_two * adam_second + (1.0 - beta_two) * grad_vectors * grad_vectors
    first_hat = new_first / (1.0 - beta_one ** STEP)
    second_hat = new_second / (1.0 - beta_two ** STEP)
    new_vectors = vectors - adam_rate * first_hat / (jnp.sqrt(second_hat) + adam_epsilon)
    return (final.astype(jnp.bfloat16), d_tokens, grad_qkv, grad_out, grad_up, grad_down, grad_vectors, new_mom_qkv, new_mom_out, new_mom_up, new_mom_down, new_w_qkv, new_w_out, new_w_up, new_w_down, new_first, new_second, new_vectors)
```

```python
import math

import jax
import jax.numpy as jnp
from jax import lax
from jax.sharding import PartitionSpec as P

HD = 64
NS_ITERS = 2
STEP = 10

poly_one = 3.4445
poly_three = -4.775
poly_five = 2.0315
momentum_decay = 0.95
muon_rate = 0.3
muon_decay = 0.01
adam_rate = 0.2
beta_one = 0.9
beta_two = 0.999
adam_epsilon = 1e-08
norm_epsilon = 1e-05
ortho_epsilon = 1e-07
masked_score = -1e30
PLANES = 4
LOW = jnp.bfloat16
WIDE = jnp.float32


def xor_trade(block, distance):
    count = lax.axis_size("dp")
    return lax.ppermute(block, "dp", [(i, i ^ distance) for i in range(count)])


def core_trade(block):
    return lax.ppermute(block, "fsdp", [(0, 1), (1, 0)])


def bit_of(rank, place):
    return (rank >> place) & 1


def pick(block, index, axis):
    return lax.dynamic_index_in_dim(block, index, axis, keepdims=False)


def pair(mine, other, bit, axis):
    first = jnp.where(bit == 0, mine, other)
    second = jnp.where(bit == 0, other, mine)
    return jnp.stack([first, second], axis)


def gather_natural(block, order):
    rank, core = lax.axis_index("dp"), lax.axis_index("fsdp")
    tail = block.shape
    done = []
    for place in order:
        axis = sum(1 for other in done if other > place)
        block = pair(block, xor_trade(block, 1 << place), bit_of(rank, place), axis)
        done.append(place)
    block = pair(block, core_trade(block), core, len(done))
    return block.reshape((-1,) + tail)


def gather_relative(block, order):
    tail = block.shape
    done = []
    for place in order:
        axis = sum(1 for other in done if other > place)
        block = jnp.stack([block, xor_trade(block, 1 << place)], axis)
        done.append(place)
    block = block.reshape((-1,) + tail[1:])
    return block, core_trade(block)


def scatter_natural(block, order):
    rank, core = lax.axis_index("dp"), lax.axis_index("fsdp")
    bits = len(order)
    total = block.reshape((2,) * (bits + 1) + block.shape[1:])
    received = core_trade(pick(total, 1 - core, bits))
    total = pick(total, core, bits).astype(WIDE) + received.astype(WIDE)
    left = list(range(bits))
    for place in order:
        axis = sum(1 for other in left if other > place)
        bit = bit_of(rank, place)
        received = xor_trade(pick(total, 1 - bit, axis).astype(LOW), 1 << place)
        total = pick(total, bit, axis) + received.astype(WIDE)
        left.remove(place)
    return total


def scatter_relative(own, other, order):
    bits = len(order)
    total = own.astype(WIDE) + core_trade(other).astype(WIDE)
    total = total.reshape((2,) * bits + (-1,) + own.shape[1:])
    left = list(range(bits))
    for place in order:
        axis = sum(1 for entry in left if entry > place)
        sent = lax.index_in_dim(total, 1, axis, keepdims=False).astype(LOW)
        total = lax.index_in_dim(total, 0, axis, keepdims=False) + xor_trade(
            sent, 1 << place
        ).astype(WIDE)
        left.remove(place)
    return total


def xor_order(block, rank, bits):
    tail = block.shape[1:]
    block = block.reshape((2,) * bits + tail)
    for place in range(bits):
        axis = bits - 1 - place
        block = jnp.where(bit_of(rank, place) == 0, block, jnp.flip(block, axis))
    return block.reshape((-1,) + tail)


def layer_norm(values, gain, shift):
    center = values - jnp.mean(values, axis=-1, keepdims=True)
    spread = jnp.mean(center * center, axis=-1, keepdims=True)
    return center * lax.rsqrt(spread + norm_epsilon) * gain + shift


def gelu_exact(values):
    return 0.5 * values * (1.0 + lax.erf(values * 0.7071067811865476))


def rows_by_cols(left, right):
    return jnp.einsum("td,fd->tf", left, right, preferred_element_type=WIDE)


def plain(left, right):
    return jnp.dot(left, right, preferred_element_type=WIDE)


def over_tokens(left, right):
    return jnp.einsum("ta,tb->ab", left, right, preferred_element_type=WIDE).astype(LOW)


def plane_sum(gram, low_bits):
    core = lax.axis_index("fsdp")
    size = gram.shape[0]
    gram = gram.reshape(2, size // 2, size)
    half = pick(gram, core, 0) + core_trade(pick(gram, 1 - core, 0).astype(LOW)).astype(WIDE)
    quarter = size // 4
    parts = [half[:quarter], half[quarter:]]
    for step in range(len(low_bits)):
        for way in range(2):
            place = low_bits[(step + way) % len(low_bits)]
            moved = xor_trade(parts[way].astype(LOW), 1 << place)
            parts[way] = parts[way] + moved.astype(WIDE)
    half = jnp.concatenate(parts, axis=0).astype(LOW)
    return pair(half, core_trade(half), core, 0).reshape(size, size).astype(WIDE)


def orthogonal(low_x, low_bits):
    gram_mat = plane_sum(
        jnp.einsum("kd,ke->de", low_x, low_x, preferred_element_type=WIDE), low_bits
    )
    factor = 1.0 / (jnp.sqrt(jnp.trace(gram_mat)) + ortho_epsilon)
    gram_mat = gram_mat * (factor * factor)
    current = low_x.astype(WIDE) * factor
    for iteration in range(NS_ITERS):
        low_gram = gram_mat.astype(LOW)
        mixing = poly_three * gram_mat + poly_five * plain(low_gram, low_gram)
        low_mixing = mixing.astype(LOW)
        scale = factor if iteration == 0 else 1.0
        source = low_x if iteration == 0 else current.astype(LOW)
        current = poly_one * current + plain(source, low_mixing) * scale
        if iteration < NS_ITERS - 1:
            product = plain(low_mixing, low_gram)
            gram_mat = (
                (poly_one * poly_one) * gram_mat
                + (2.0 * poly_one) * product
                + plain(low_mixing, product.astype(LOW))
            )
    return current.astype(LOW)


def per_device(
    tokens_in,
    cotangent,
    seq_lengths,
    w_qkv,
    w_out,
    w_up,
    w_down,
    vectors,
    mom_qkv,
    mom_out,
    mom_up,
    mom_down,
    adam_first,
    adam_second,
):
    tok_rows, width = tokens_in.shape
    side = width // 2
    heads = width // HD
    group_len = tok_rows * 2
    dp_count = lax.axis_size("dp")
    bits = dp_count.bit_length() - 1
    rank, core = lax.axis_index("dp"), lax.axis_index("fsdp")
    up_order = list(range(bits))
    down_order = [1, 0] + list(range(2, bits))
    qkv_cols, out_cols, up_cols = w_qkv.shape[1], w_out.shape[1], w_up.shape[1]
    vec_rows, vec_cols = vectors.shape
    vec_size = vec_rows * vec_cols
    devices = 2 * dp_count

    attn_pack = jnp.concatenate([w_qkv.T, w_out.T], axis=0).astype(LOW)
    vec_flat = jnp.pad(vectors.astype(LOW).reshape(1, vec_size), ((0, 7), (0, side - vec_size)))
    pack_one = jnp.concatenate([attn_pack[:, :side], vec_flat], axis=0)
    pack_two = attn_pack[:, side:]
    all_one = gather_natural(pack_one, up_order[::-1])
    all_two = gather_natural(pack_two, down_order[::-1])
    up_own, up_other = gather_relative(w_up.T.astype(LOW), up_order[::-1])
    down_own, down_other = gather_relative(w_down.astype(LOW), down_order[::-1])
    qkv_sides = [part[:, :qkv_cols].reshape(-1, side) for part in (all_one, all_two)]
    out_sides = [
        part[:, qkv_cols : qkv_cols + out_cols].reshape(-1, side) for part in (all_one, all_two)
    ]
    vec_full = (
        all_one[:, qkv_cols + out_cols, :vec_size]
        .reshape(devices, vec_rows, vec_cols)
        .transpose(1, 0, 2)
        .reshape(vec_rows, width)
        .astype(WIDE)
    )
    up_bias = xor_order(vec_full[8:].reshape(dp_count, 2, up_cols), rank, bits)
    bias_own = pick(up_bias, core, 1).reshape(-1)
    bias_other = pick(up_bias, 1 - core, 1).reshape(-1)

    bounds = jnp.cumsum(seq_lengths[0])
    places = jnp.arange(group_len, dtype=jnp.int32)
    places = jnp.where(core == 0, places, (places + tok_rows) % group_len)
    seg_group = jnp.sum((places[:, None] >= bounds[None, :]).astype(jnp.int32), axis=1)
    seg_local = seg_group[:tok_rows]
    live_rows = (seg_local < seq_lengths.shape[1]).astype(WIDE)[:, None]
    allowed = seg_local[:, None] == seg_group[None, :]
    score_scale = HD ** (-0.5)

    zero_bias = jnp.zeros((width,), WIDE)
    qkv_bias = jnp.concatenate([vec_full[4], zero_bias, vec_full[5]])
    projected = (
        rows_by_cols(tokens_in[:, :side], qkv_sides[0])
        + rows_by_cols(tokens_in[:, side:], qkv_sides[1])
        + qkv_bias
    )
    projected_low = projected.astype(LOW)
    queries = projected_low[:, :width].reshape(tok_rows, heads, HD)
    own_kv = projected_low[:, width:]
    keys_values = jnp.concatenate([own_kv, core_trade(own_kv)], axis=0)
    key_rows = keys_values[:, :width].reshape(group_len, heads, HD)
    value_rows = keys_values[:, width:].reshape(group_len, heads, HD)

    def score_block():
        raw_scores = (
            jnp.einsum("ihd,jhd->hij", queries, key_rows, preferred_element_type=WIDE)
            * score_scale
        )
        return jnp.where(allowed[None], raw_scores, masked_score)

    scores = score_block()
    row_max = jnp.max(scores, axis=-1, keepdims=True)
    exp_scores = jnp.exp(scores - row_max)
    totals = jnp.sum(exp_scores, axis=-1, keepdims=True)
    probs_low = (exp_scores / totals).astype(LOW)
    log_total = row_max + jnp.log(totals)
    context = jnp.einsum("hij,jhd->ihd", probs_low, value_rows, preferred_element_type=WIDE)
    context_low = context.reshape(tok_rows, width).astype(LOW)
    attended = (
        rows_by_cols(context_low[:, :side], out_sides[0])
        + rows_by_cols(context_low[:, side:], out_sides[1])
        + vec_full[6]
    )
    normed, norm_one_pull = jax.vjp(
        layer_norm, tokens_in.astype(WIDE) + attended, vec_full[0], vec_full[1]
    )
    normed_low = normed.astype(LOW)

    act_low, gelu_pulls = [], []
    for matrix, bias in ((up_own, bias_own), (up_other, bias_other)):
        activated, gelu_pull = jax.vjp(gelu_exact, rows_by_cols(normed_low, matrix) + bias)
        act_low.append(activated.astype(LOW))
        gelu_pulls.append(gelu_pull)
    lowered = plain(act_low[0], down_own) + plain(act_low[1], down_other) + vec_full[7]
    final, norm_two_pull = jax.vjp(layer_norm, normed + lowered, vec_full[2], vec_full[3])
    output = final.astype(LOW)
    top_grad = cotangent.astype(WIDE) * live_rows
    d_resid_two, g_gain_two, g_shift_two = norm_two_pull(top_grad)
    d_lowered = d_resid_two.astype(LOW)
    g_bias_down = jnp.sum(d_lowered.astype(WIDE), axis=0)
    g_down = [over_tokens(part, d_lowered) for part in act_low]
    grad_down = scatter_relative(g_down[0], g_down[1], down_order)
    d_pre_low = [
        pull(rows_by_cols(d_lowered, matrix))[0].astype(LOW)
        for pull, matrix in zip(gelu_pulls, (down_own, down_other))
    ]
    g_up = [over_tokens(part, normed_low) for part in d_pre_low]
    grad_up_t = scatter_relative(g_up[0], g_up[1], up_order)
    g_bias_up = [jnp.sum(part.astype(WIDE), axis=0).reshape(dp_count, up_cols) for part in d_pre_low]
    g_bias_up = xor_order(pair(g_bias_up[0], g_bias_up[1], core, 1), rank, bits)
    d_normed = plain(d_pre_low[0], up_own) + plain(d_pre_low[1], up_other) + d_resid_two
    d_resid_one, g_gain_one, g_shift_one = norm_one_pull(d_normed)
    d_attended = d_resid_one.astype(LOW)
    g_bias_out = jnp.sum(d_attended.astype(WIDE), axis=0)

    g_out = [
        over_tokens(d_attended, part) for part in (context_low[:, :side], context_low[:, side:])
    ]
    d_context = jnp.concatenate([plain(d_attended, part) for part in out_sides], axis=1)
    d_context = d_context.astype(LOW).reshape(tok_rows, heads, HD)
    probs = jnp.exp(score_block() - log_total)
    d_probs = jnp.einsum("ihd,jhd->hij", d_context, value_rows, preferred_element_type=WIDE)
    inner_sum = jnp.sum(probs * d_probs, axis=-1, keepdims=True)
    d_scores = (probs * (d_probs - inner_sum)).astype(LOW)
    d_queries = (
        jnp.einsum("hij,jhd->ihd", d_scores, key_rows, preferred_element_type=WIDE) * score_scale
    )
    key_part = (
        jnp.einsum("hij,ihd->jhd", d_scores, queries, preferred_element_type=WIDE) * score_scale
    )
    value_part = jnp.einsum(
        "hij,ihd->jhd", probs.astype(LOW), d_context, preferred_element_type=WIDE
    )
    d_kv = jnp.concatenate(
        [key_part.reshape(group_len, width), value_part.reshape(group_len, width)], axis=1
    )
    d_kv = d_kv[:tok_rows] + core_trade(d_kv[tok_rows:].astype(LOW)).astype(WIDE)
    d_qkv = jnp.concatenate([d_queries.reshape(tok_rows, width), d_kv], axis=1).astype(LOW)
    qkv_sums = jnp.sum(d_qkv.astype(WIDE), axis=0)
    g_vec_local = jnp.concatenate(
        [
            jnp.stack(
                [
                    g_gain_one,
                    g_shift_one,
                    g_gain_two,
                    g_shift_two,
                    qkv_sums[:width],
                    qkv_sums[2 * width :],
                    g_bias_out,
                    g_bias_down,
                ]
            ),
            g_bias_up.reshape(-1, width),
        ],
        axis=0,
    )
    g_vec_pack = (
        g_vec_local.reshape(vec_rows, devices, vec_cols)
        .transpose(1, 0, 2)
        .reshape(devices, 1, vec_size)
    )
    g_vec_pack = jnp.pad(g_vec_pack, ((0, 0), (0, 7), (0, side - vec_size))).astype(LOW)
    g_sides = []
    for index in range(2):
        columns = slice(index * side, (index + 1) * side)
        pieces = [
            over_tokens(d_qkv, tokens_in[:, columns]).reshape(devices, qkv_cols, side),
            g_out[index].reshape(devices, out_cols, side),
        ]
        if index == 0:
            pieces.append(g_vec_pack)
        g_sides.append(jnp.concatenate(pieces, axis=1))
    sum_one = scatter_natural(g_sides[0], up_order)
    sum_two = scatter_natural(g_sides[1], down_order)
    d_tokens = d_resid_one + jnp.concatenate([plain(d_qkv, part) for part in qkv_sides], axis=1)

    attn_rows = qkv_cols + out_cols
    grad_attn_t = jnp.concatenate([sum_one[:attn_rows], sum_two], axis=1)
    grad_qkv_t, grad_out_t = grad_attn_t[:qkv_cols], grad_attn_t[qkv_cols:]
    grad_vectors = sum_one[attn_rows, :vec_size].reshape(vec_rows, vec_cols)

    piece_rows = max(qkv_cols, up_cols)
    moments_t = [
        momentum_decay * moment + grad
        for moment, grad in (
            (mom_qkv.T, grad_qkv_t),
            (mom_out.T, grad_out_t),
            (mom_up.T, grad_up_t),
            (mom_down, grad_down),
        )
    ]
    new_mom_qkv, new_mom_out, new_mom_up = [moment.T for moment in moments_t[:3]]
    new_mom_down = moments_t[3]
    stacked = jnp.stack(
        [
            jnp.pad(moment.astype(LOW), ((0, piece_rows - moment.shape[0]), (0, 0)))
            for moment in moments_t
        ]
    )
    plane_step = dp_count // PLANES
    plane = rank // plane_step
    mine = [pick(stacked, plane, 0)]
    for offset in range(1, PLANES):
        mine.append(xor_trade(pick(stacked, plane ^ offset, 0), offset * plane_step))
    turned = orthogonal(jnp.concatenate(mine, axis=0), list(range(bits - 2)))
    turned = turned.reshape(PLANES, piece_rows, width)
    back = [turned[0]]
    for offset in range(1, PLANES):
        back.append(xor_trade(turned[offset], offset * plane_step))
    back = jnp.stack(back)
    ortho_t = [
        pick(back, plane ^ index, 0)[: moment.shape[0]].astype(WIDE)
        for index, moment in enumerate(moments_t)
    ]

    def updated(weight, ortho, longest):
        return weight - muon_rate * (0.2 * math.sqrt(longest) * ortho + muon_decay * weight)

    hidden = up_cols * devices
    new_w_qkv = updated(w_qkv, ortho_t[0].T, 3 * width)
    new_w_out = updated(w_out, ortho_t[1].T, width)
    new_w_up = updated(w_up, ortho_t[2].T, max(width, hidden))
    new_w_down = updated(w_down, ortho_t[3], max(width, hidden))

    new_first = beta_one * adam_first + (1.0 - beta_one) * grad_vectors
    new_second = beta_two * adam_second + (1.0 - beta_two) * grad_vectors * grad_vectors
    first_hat = new_first / (1.0 - beta_one**STEP)
    second_hat = new_second / (1.0 - beta_two**STEP)
    new_vectors = vectors - adam_rate * first_hat / (jnp.sqrt(second_hat) + adam_epsilon)
    return (
        output,
        d_tokens,
        grad_qkv_t.T,
        grad_out_t.T,
        grad_up_t.T,
        grad_down,
        grad_vectors,
        new_mom_qkv,
        new_mom_out,
        new_mom_up,
        new_mom_down,
        new_w_qkv,
        new_w_out,
        new_w_up,
        new_w_down,
        new_first,
        new_second,
        new_vectors,
    )


def solution(mesh):
    in_specs = (
        P(("dp", "fsdp"), None),
        P(("dp", "fsdp"), None),
        P("dp", None),
        P(None, ("dp", "fsdp")),
        P(None, ("dp", "fsdp")),
        P(None, ("dp", "fsdp")),
        P(("dp", "fsdp"), None),
        P(None, ("dp", "fsdp")),
        P(None, ("dp", "fsdp")),
        P(None, ("dp", "fsdp")),
        P(None, ("dp", "fsdp")),
        P(("dp", "fsdp"), None),
        P(None, ("dp", "fsdp")),
        P(None, ("dp", "fsdp")),
    )
    out_specs = (
        P(("dp", "fsdp"), None),
        P(("dp", "fsdp"), None),
        P(None, ("dp", "fsdp")),
        P(None, ("dp", "fsdp")),
        P(None, ("dp", "fsdp")),
        P(("dp", "fsdp"), None),
        P(None, ("dp", "fsdp")),
        P(None, ("dp", "fsdp")),
        P(None, ("dp", "fsdp")),
        P(None, ("dp", "fsdp")),
        P(("dp", "fsdp"), None),
        P(None, ("dp", "fsdp")),
        P(None, ("dp", "fsdp")),
        P(None, ("dp", "fsdp")),
        P(("dp", "fsdp"), None),
        P(None, ("dp", "fsdp")),
        P(None, ("dp", "fsdp")),
        P(None, ("dp", "fsdp")),
    )
    return jax.shard_map(
        per_device, mesh=mesh, in_specs=in_specs, out_specs=out_specs, check_vma=False
    )
```

```python
import math

import jax
import jax.numpy as jnp
from jax import lax
from jax.experimental import pallas as pl
from jax.experimental.pallas import tpu as pltpu
from jax.sharding import PartitionSpec as P

HD = 64
NS_ITERS = 2
STEP = 10

poly_one = 3.4445
poly_three = -4.775
poly_five = 2.0315
momentum_decay = 0.95
muon_rate = 0.3
muon_decay = 0.01
adam_rate = 0.2
beta_one = 0.9
beta_two = 0.999
adam_epsilon = 1e-08
norm_epsilon = 1e-05
ortho_epsilon = 1e-07
masked_score = -1e30
PLANES = 4
LOW = jnp.bfloat16
WIDE = jnp.float32


def xor_trade(block, distance):
    count = lax.axis_size("dp")
    return lax.ppermute(block, "dp", [(i, i ^ distance) for i in range(count)])


def core_trade(block):
    return lax.ppermute(block, "fsdp", [(0, 1), (1, 0)])


def bit_of(rank, place):
    return (rank >> place) & 1


def pick(block, index, axis):
    return lax.dynamic_index_in_dim(block, index, axis, keepdims=False)


def pair(mine, other, bit, axis):
    first = jnp.where(bit == 0, mine, other)
    second = jnp.where(bit == 0, other, mine)
    return jnp.stack([first, second], axis)


def higher(places, place):
    return sum(1 for other in places if other > place)


def gather_relative(block, order, done):
    for index, place in enumerate(order):
        axis = higher(done + order[:index], place)
        block = jnp.stack([block, xor_trade(block, 1 << place)], axis)
    return block


def tie(*values):
    return lax.optimization_barrier(values)


def halves(total, order):
    axis = higher(order, order[0])
    sent = lax.index_in_dim(total, 1, axis, keepdims=False).astype(LOW)
    return lax.index_in_dim(total, 0, axis, keepdims=False), sent


def scatter_relative(total, order):
    for index in range(len(order)):
        kept, sent = halves(total, order[index:])
        total = kept + xor_trade(sent, 1 << order[index]).astype(WIDE)
    return total


def xor_order(block, rank, bits):
    tail = block.shape[1:]
    block = block.reshape((2,) * bits + tail)
    for place in range(bits):
        axis = bits - 1 - place
        block = jnp.where(bit_of(rank, place) == 0, block, jnp.flip(block, axis))
    return block.reshape((-1,) + tail)


def nt(left, right):
    return lax.dot_general(left, right, (((1,), (1,)), ((), ())), preferred_element_type=WIDE)


def nn(left, right):
    return lax.dot_general(left, right, (((1,), (0,)), ((), ())), preferred_element_type=WIDE)


def tn(left, right):
    return lax.dot_general(left, right, (((0,), (0,)), ((), ())), preferred_element_type=WIDE)


def run_kernel(body, results, operands, scratch=(), scalars=0):
    places = [pltpu.SMEM] * scalars + [pltpu.VMEM] * (len(operands) - scalars)
    return pl.pallas_call(
        body,
        out_shape=[jax.ShapeDtypeStruct(shape, kind) for shape, kind in results],
        in_specs=[pl.BlockSpec(memory_space=place) for place in places],
        out_specs=[pl.BlockSpec(memory_space=pltpu.VMEM)] * len(results),
        scratch_shapes=[pltpu.VMEM(shape, kind) for shape, kind in scratch],
        compiler_params=pltpu.CompilerParams(vmem_limit_bytes=48 * 1024 * 1024),
        cost_estimate=pl.CostEstimate(flops=1000, bytes_accessed=1000, transcendentals=0),
    )(*operands)


def gate(value, *needed):
    anywhere = pl.BlockSpec(memory_space=pl.ANY)
    return pl.pallas_call(
        lambda *refs: None,
        out_shape=jax.ShapeDtypeStruct(value.shape, value.dtype),
        in_specs=[anywhere] * (1 + len(needed)),
        out_specs=anywhere,
        input_output_aliases={0: 0},
        cost_estimate=pl.CostEstimate(flops=0, bytes_accessed=0, transcendentals=0),
    )(value, *needed)


def mean_of(values):
    return jnp.sum(values, axis=-1, keepdims=True) * (1.0 / values.shape[-1])


def normalized(values):
    center = values - mean_of(values)
    scale = lax.rsqrt(mean_of(center * center) + norm_epsilon)
    return center * scale, scale


def norm_back(grad, unit, scale, gain):
    inner = grad * gain
    return scale * (inner - mean_of(inner) - unit * mean_of(inner * unit))


def head_probs(query, keys, allowed):
    scores = nt(query, keys) * (HD ** (-0.5))
    scores = jnp.where(allowed, scores, masked_score)
    exp_scores = jnp.exp(scores - jnp.max(scores, axis=-1, keepdims=True))
    return exp_scores / jnp.sum(exp_scores, axis=-1, keepdims=True)


def head_parts(head, width, own_ref, other_ref):
    at = slice(head * HD, (head + 1) * HD)
    keys = jnp.concatenate([own_ref[:, width:][:, at], other_ref[:, :width][:, at]], axis=0)
    values = jnp.concatenate([own_ref[:, 2 * width :][:, at], other_ref[:, width:][:, at]], axis=0)
    return own_ref[:, at], keys, values


def attend_body(
    own_ref, other_ref, seg_col, seg_row, one_ref, two_ref, tokens_ref, vec_ref,
    context_ref, normed_ref, low_ref, unit_ref, scale_ref,
):
    width = tokens_ref.shape[1]
    side = width // 2
    allowed = seg_col[...] == seg_row[...]
    for start in range(0, width // HD, 2):
        found = []
        for head in (start, start + 1):
            query, keys, values = head_parts(head, width, own_ref, other_ref)
            found.append(nn(head_probs(query, keys, allowed).astype(LOW), values))
        context_ref[:, start * HD : (start + 2) * HD] = jnp.concatenate(found, axis=1).astype(LOW)
    attended = (
        nt(context_ref[:, :side], one_ref[...])
        + nt(context_ref[:, side:], two_ref[...])
        + vec_ref[6:7, :]
    )
    unit, scale = normalized(tokens_ref[...].astype(WIDE) + attended)
    normed = unit * vec_ref[0:1, :] + vec_ref[1:2, :]
    normed_ref[...] = normed
    low_ref[...] = normed.astype(LOW)
    unit_ref[...] = unit
    scale_ref[...] = scale


def attend_back_body(
    d_normed_ref, own_ref, other_ref, seg_col, seg_row, one_ref, two_ref, unit_ref, scale_ref, vec_ref,
    resid_ref, attended_ref, query_ref, own_grad_ref, other_grad_ref, rows_ref,
):
    tok_rows, width = d_normed_ref.shape
    allowed = seg_col[...] == seg_row[...]
    grad, unit = d_normed_ref[...], unit_ref[...]
    resid = norm_back(grad, unit, scale_ref[...], vec_ref[0:1, :])
    low = resid.astype(LOW)
    resid_ref[...] = resid
    attended_ref[...] = low
    rows_ref[0:1, :] = jnp.sum(grad * unit, axis=0, keepdims=True)
    rows_ref[1:2, :] = jnp.sum(grad, axis=0, keepdims=True)
    rows_ref[2:3, :] = jnp.sum(low.astype(WIDE), axis=0, keepdims=True)
    d_context = jnp.concatenate([nn(low, one_ref[...]), nn(low, two_ref[...])], axis=1).astype(LOW)
    factor = HD ** (-0.5)
    for start in range(0, width // HD, 2):
        found = []
        for head in (start, start + 1):
            query, keys, values = head_parts(head, width, own_ref, other_ref)
            grad_head = d_context[:, head * HD : (head + 1) * HD]
            probs = head_probs(query, keys, allowed)
            d_probs = nt(grad_head, values)
            inner = jnp.sum(probs * d_probs, axis=-1, keepdims=True)
            d_scores = (probs * (d_probs - inner)).astype(LOW)
            found.append(
                (nn(d_scores, keys) * factor, tn(d_scores, query) * factor,
                 tn(probs.astype(LOW), grad_head))
            )
        d_query, d_keys, d_values = [
            jnp.concatenate([first, second], axis=1) for first, second in zip(*found)
        ]
        at = slice(start * HD, (start + 2) * HD)
        shifted = slice(width + start * HD, width + (start + 2) * HD)
        query_ref[:, at] = d_query.astype(LOW)
        own_grad_ref[:, at] = d_keys[:tok_rows]
        own_grad_ref[:, shifted] = d_values[:tok_rows]
        other_grad_ref[:, at] = d_keys[tok_rows:].astype(LOW)
        other_grad_ref[:, shifted] = d_values[tok_rows:].astype(LOW)


def hidden_body(
    normed_ref, low_ref, cotangent_ref, live_ref, vec_ref,
    up_own, up_other, down_own, down_other, bias_own, bias_other,
    output_ref, grad_ref, g_up_own, g_up_other, g_down_own, g_down_other,
    g_bias_own, g_bias_other, rows_ref, act_ref, slope_ref,
):
    low = low_ref[...]
    hidden = up_own.shape[0]
    step = hidden // 3
    lowered = vec_ref[7:8, :] + jnp.zeros(normed_ref.shape, WIDE)
    for part, (up, bias, down) in enumerate(
        ((up_own, bias_own, down_own), (up_other, bias_other, down_other))
    ):
        for start in range(0, hidden, step):
            at = slice(start, start + step)
            pre = nt(low, up[at, :]) + bias[:, at]
            cdf = 0.5 * (1.0 + lax.erf(pre * 0.7071067811865476))
            slope = cdf + pre * jnp.exp(-0.5 * pre * pre) * 0.3989422804014327
            act = (pre * cdf).astype(LOW)
            act_ref[part, :, at] = act
            slope_ref[part, :, at] = slope
            lowered = lowered + nn(act, down[at, :])
    unit, scale = normalized(normed_ref[...] + lowered)
    output_ref[...] = (unit * vec_ref[2:3, :] + vec_ref[3:4, :]).astype(LOW)
    top = cotangent_ref[...].astype(WIDE) * live_ref[...]
    resid = norm_back(top, unit, scale, vec_ref[2:3, :])
    d_lowered = resid.astype(LOW)
    rows_ref[0:1, :] = jnp.sum(top * unit, axis=0, keepdims=True)
    rows_ref[1:2, :] = jnp.sum(top, axis=0, keepdims=True)
    rows_ref[2:3, :] = jnp.sum(d_lowered.astype(WIDE), axis=0, keepdims=True)
    total = resid
    for part, (up, down, g_up, g_down, g_bias) in enumerate(
        ((up_own, down_own, g_up_own, g_down_own, g_bias_own),
         (up_other, down_other, g_up_other, g_down_other, g_bias_other))
    ):
        for start in range(0, hidden, step):
            at = slice(start, start + step)
            g_down[at, :] = tn(act_ref[part, :, at], d_lowered).astype(LOW)
            d_pre = (nt(d_lowered, down[at, :]) * slope_ref[part, :, at]).astype(LOW)
            g_bias[:, at] = jnp.sum(d_pre.astype(WIDE), axis=0, keepdims=True)
            g_up[at, :] = tn(d_pre, low).astype(LOW)
            total = total + nn(d_pre, up[at, :])
    grad_ref[...] = total


def unpack_body(
    index_ref, own_one, other_one, own_two, other_two, tokens_ref,
    projected_ref, qkv_one, qkv_two, out_one, out_two, vec_ref,
):
    rank, core = index_ref[0], index_ref[1]
    count, rows, side = own_one.shape
    width = 2 * side
    qkv_cols = qkv_one.shape[0] // (2 * count)
    out_cols = out_one.shape[0] // (2 * count)
    split = qkv_cols + 8
    total = []
    for own, other, qkv, out in (
        (own_one, other_one, qkv_one, out_one), (own_two, other_two, qkv_two, out_two)
    ):
        vec = jnp.zeros((16, side), WIDE)
        for place in range(count):
            slot = jnp.bitwise_xor(rank, place)
            mine, theirs = own[slot].astype(WIDE), other[slot].astype(WIDE)
            first = jnp.where(core == 0, mine, theirs)
            second = jnp.where(core == 0, theirs, mine)
            both = jnp.concatenate([first[:qkv_cols], second[:qkv_cols]], axis=0)
            qkv[2 * qkv_cols * place : 2 * qkv_cols * (place + 1), :] = both.astype(LOW)
            both = [part[split : split + out_cols] for part in (first, second)]
            both = jnp.concatenate(both, axis=0)
            out[2 * out_cols * place : 2 * out_cols * (place + 1), :] = both.astype(LOW)
            vec = vec + jnp.concatenate(
                [mine[qkv_cols:split] + theirs[qkv_cols:split], mine[rows - 8 :] + theirs[rows - 8 :]],
                axis=0,
            )
        total.append(vec)
    vec = jnp.concatenate(total, axis=1)
    vec_ref[...] = vec
    for part, bias in enumerate((vec[4:5], None, vec[5:6])):
        at = slice(part * width, (part + 1) * width)
        block = nt(tokens_ref[:, :side], qkv_one[at, :]) + nt(tokens_ref[:, side:], qkv_two[at, :])
        projected_ref[:, at] = (block if bias is None else block + bias).astype(LOW)


def pack_body(
    index_ref, query_ref, own_ref, got_ref, tokens_ref, attended_ref, context_ref, rows_ref,
    d_qkv_ref, kept_one, sent_one, kept_two, sent_two, wide_ref, out_ref,
):
    rank, core = index_ref[0], index_ref[1]
    count, rows, side = kept_one.shape
    width = 2 * side
    qkv_cols = wide_ref.shape[0] // (2 * count)
    out_cols = out_ref.shape[0] // (2 * count)
    d_qkv_ref[:, :width] = query_ref[...]
    d_qkv_ref[:, width:] = (own_ref[...] + got_ref[...].astype(WIDE)).astype(LOW)
    for index, (kept, sent) in enumerate(((kept_one, sent_one), (kept_two, sent_two))):
        at = slice(index * side, (index + 1) * side)
        for part in range(3):
            block = slice(part * width, (part + 1) * width)
            wide_ref[block, :] = tn(d_qkv_ref[:, block], tokens_ref[:, at])
        out_ref[...] = tn(attended_ref[...], context_ref[:, at])
        sums = [
            jnp.sum(d_qkv_ref[:, block].astype(WIDE), axis=0, keepdims=True)[:, at]
            for block in (slice(0, width), slice(2 * width, 3 * width))
        ]
        low_rows = jnp.concatenate([rows_ref[:4, at], sums[0], sums[1], rows_ref[6:8, at]], axis=0)
        high_rows = rows_ref[8:, at]
        for place in range(count):
            slot = jnp.bitwise_xor(rank, place)
            blocks = []
            for chunk in (2 * place, 2 * place + 1):
                blocks.append(
                    jnp.concatenate(
                        [
                            wide_ref[qkv_cols * chunk : qkv_cols * (chunk + 1), :],
                            low_rows,
                            out_ref[out_cols * chunk : out_cols * (chunk + 1), :],
                            high_rows,
                        ],
                        axis=0,
                    )
                )
            kept[slot] = jnp.where(core == 0, blocks[0], blocks[1]).astype(LOW)
            sent[slot] = jnp.where(core == 0, blocks[1], blocks[0]).astype(LOW)


def rows_by_cols(left, right):
    return jnp.einsum("td,fd->tf", left, right, preferred_element_type=WIDE)


def plain(left, right):
    return jnp.dot(left, right, preferred_element_type=WIDE)


def over_tokens(left, right):
    return jnp.einsum("ta,tb->ab", left, right, preferred_element_type=WIDE).astype(LOW)


def plane_sum(gram, low_bits):
    core = lax.axis_index("fsdp")
    size = gram.shape[0]
    gram = gram.reshape(2, size // 2, size)
    half = pick(gram, core, 0) + core_trade(pick(gram, 1 - core, 0).astype(LOW)).astype(WIDE)
    quarter = size // 4
    parts = [half[:quarter], half[quarter:]]
    for step in range(len(low_bits)):
        for way in range(2):
            place = low_bits[(step + way) % len(low_bits)]
            moved = xor_trade(parts[way].astype(LOW), 1 << place)
            parts[way] = parts[way] + moved.astype(WIDE)
    half = jnp.concatenate(parts, axis=0).astype(LOW)
    return pair(half, core_trade(half), core, 0).reshape(size, size).astype(WIDE)


def orthogonal(low_x, low_bits):
    gram_mat = plane_sum(
        jnp.einsum("kd,ke->de", low_x, low_x, preferred_element_type=WIDE), low_bits
    )
    factor = 1.0 / (jnp.sqrt(jnp.trace(gram_mat)) + ortho_epsilon)
    gram_mat = gram_mat * (factor * factor)
    current = low_x.astype(WIDE) * factor
    for iteration in range(NS_ITERS):
        low_gram = gram_mat.astype(LOW)
        mixing = poly_three * gram_mat + poly_five * plain(low_gram, low_gram)
        low_mixing = mixing.astype(LOW)
        scale = factor if iteration == 0 else 1.0
        source = low_x if iteration == 0 else current.astype(LOW)
        current = poly_one * current + plain(source, low_mixing) * scale
        if iteration < NS_ITERS - 1:
            product = plain(low_mixing, low_gram)
            gram_mat = (
                (poly_one * poly_one) * gram_mat
                + (2.0 * poly_one) * product
                + plain(low_mixing, product.astype(LOW))
            )
    return current.astype(LOW)


def per_device(
    tokens_in,
    cotangent,
    seq_lengths,
    w_qkv,
    w_out,
    w_up,
    w_down,
    vectors,
    mom_qkv,
    mom_out,
    mom_up,
    mom_down,
    adam_first,
    adam_second,
):
    tok_rows, width = tokens_in.shape
    side = width // 2
    group_len = tok_rows * 2
    dp_count = lax.axis_size("dp")
    bits = dp_count.bit_length() - 1
    rank, core = lax.axis_index("dp"), lax.axis_index("fsdp")
    up_order = list(range(bits))
    down_order = [1, 0] + list(range(2, bits))
    qkv_cols, out_cols, up_cols = w_qkv.shape[1], w_out.shape[1], w_up.shape[1]
    vec_rows, vec_cols = vectors.shape
    devices = 2 * dp_count

    index = jnp.stack([rank, core]).astype(jnp.int32)
    first_col = vec_cols * (2 * rank + core)
    vec_wide = lax.dynamic_update_slice(
        jnp.zeros((16, width), LOW), vectors.astype(LOW), (0, first_col)
    )
    split = -(-(qkv_cols + 8) // 16) * 16
    rows = split + -(-(out_cols + 8) // 16) * 16
    exact = qkv_cols % 8 == 0 and out_cols % 8 == 0 and split == qkv_cols + 8 and rows == split + out_cols + 8
    pack = jnp.concatenate(
        [
            jnp.pad(w_qkv.T.astype(LOW), ((0, split - 8 - qkv_cols), (0, 0))),
            vec_wide[:8],
            jnp.pad(w_out.T.astype(LOW), ((0, rows - split - 8 - out_cols), (0, 0))),
            vec_wide[8:],
        ],
        axis=0,
    )
    pack_one, pack_two = pack[:, :side], pack[:, side:]
    far = up_order[2:][::-1]
    near_one, near_two = [1, 0], [0, 1]
    near_axis = bits - 2
    all_one = gather_relative(pack_one, far, [])
    all_two = gather_relative(pack_two, far, [])
    up_part, down_part = w_up.T.astype(LOW), w_down.astype(LOW)
    all_one, all_two, up_part, down_part = tie(all_one, all_two, up_part, down_part)
    all_one = gather_relative(all_one, near_one, far)
    all_two = gather_relative(all_two, near_two, far)
    up_part = gather_relative(up_part, far, [])
    down_part = gather_relative(down_part, far, [])
    all_one, all_two, up_part, down_part = tie(all_one, all_two, up_part, down_part)
    up_got = xor_trade(up_part, 1 << near_one[0])
    down_got = xor_trade(down_part, 1 << near_two[0])
    own_packs = [part.reshape((dp_count, rows, side)) for part in (all_one, all_two)]
    other_packs = [core_trade(part) for part in own_packs]
    packs = (own_packs[0], other_packs[0], own_packs[1], other_packs[1])
    wide_side, out_side = (devices * qkv_cols, side), (devices * out_cols, side)
    if exact:
        projected_low, *sides, vec_full = run_kernel(
            unpack_body,
            [((tok_rows, 3 * width), LOW), (wide_side, LOW), (wide_side, LOW)]
            + [(out_side, LOW), (out_side, LOW), ((16, width), WIDE)],
            (index, *packs, tokens_in),
            scalars=1,
        )
        qkv_sides, out_sides = sides[:2], sides[2:]
    else:
        natural = [
            xor_order(pair(own, other, core, 1), rank, bits).reshape(devices, rows, side)
            for own, other in zip(own_packs, other_packs)
        ]
        qkv_sides = [part[:, :qkv_cols].reshape(wide_side) for part in natural]
        out_sides = [part[:, split : split + out_cols].reshape(out_side) for part in natural]
        vec_full = jnp.concatenate(natural, axis=2).astype(WIDE)
        vec_full = jnp.concatenate([vec_full[:, split - 8 : split], vec_full[:, rows - 8 :]], axis=1)
        vec_full = jnp.sum(vec_full, axis=0)
        qkv_bias = jnp.concatenate([vec_full[4], jnp.zeros((width,), WIDE), vec_full[5]])
        projected = rows_by_cols(tokens_in[:, :side], qkv_sides[0])
        projected = projected + rows_by_cols(tokens_in[:, side:], qkv_sides[1])
        projected_low = (projected + qkv_bias).astype(LOW)
    up_bias = xor_order(vec_full[8:12].reshape(dp_count, 2, up_cols), rank, bits)
    bias_own = pick(up_bias, core, 1).reshape(1, -1)
    bias_other = pick(up_bias, 1 - core, 1).reshape(1, -1)

    bounds = jnp.cumsum(seq_lengths[0])
    places = jnp.arange(group_len, dtype=jnp.int32)
    places = jnp.where(core == 0, places, (places + tok_rows) % group_len)
    seg_group = jnp.sum((places[:, None] >= bounds[None, :]).astype(jnp.int32), axis=1)
    seg_local = seg_group[:tok_rows]
    live_rows = (seg_local < seq_lengths.shape[1]).astype(WIDE)[:, None]
    seg_col, seg_row = seg_local[:, None], seg_group[None, :]

    own_kv = projected_low[:, width:]
    up_got, down_got, own_kv = tie(up_got, down_got, own_kv)
    up_part = jnp.stack([up_part, up_got], near_axis)
    down_part = jnp.stack([down_part, down_got], near_axis)
    up_got = xor_trade(up_part, 1 << near_one[1])
    down_got = xor_trade(down_part, 1 << near_two[1])
    other_kv = core_trade(own_kv)
    square = (tok_rows, width)
    context_low, normed, normed_low, unit, scale = run_kernel(
        attend_body,
        [(square, LOW), (square, WIDE), (square, LOW), (square, WIDE), ((tok_rows, 1), WIDE)],
        (projected_low, other_kv, seg_col, seg_row, *out_sides, tokens_in, vec_full),
    )
    up_got, down_got, normed_low = tie(up_got, down_got, normed_low)
    up_part = jnp.stack([up_part, up_got], near_axis + 1)
    down_part = jnp.stack([down_part, down_got], near_axis)
    up_own, down_own = up_part.reshape(-1, width), down_part.reshape(-1, width)
    up_other, down_other = core_trade(up_own), core_trade(down_own)
    hidden_rows = up_own.shape[0]
    output, d_normed, *grads, rows_two = run_kernel(
        hidden_body,
        [(square, LOW), (square, WIDE)]
        + [((hidden_rows, width), LOW)] * 4
        + [((1, hidden_rows), WIDE)] * 2
        + [((3, width), WIDE)],
        (normed, normed_low, cotangent, live_rows, vec_full)
        + (up_own, up_other, down_own, down_other, bias_own, bias_other),
        [((2, tok_rows, hidden_rows), LOW), ((2, tok_rows, hidden_rows), WIDE)],
    )
    g_up, g_down, g_bias_up = grads[:2], grads[2:4], grads[4:]
    bit_shape = (2,) * bits + (-1, width)
    grad_down = (g_down[0].astype(WIDE) + core_trade(g_down[1]).astype(WIDE)).reshape(bit_shape)
    grad_up_t = (g_up[0].astype(WIDE) + core_trade(g_up[1]).astype(WIDE)).reshape(bit_shape)
    g_bias_up = [part.reshape(dp_count, up_cols) for part in g_bias_up]
    g_bias_up = xor_order(pair(g_bias_up[0], g_bias_up[1], core, 1), rank, bits)
    d_resid_one, d_attended, d_query, own_grad, other_grad, rows_one = run_kernel(
        attend_back_body,
        [(square, WIDE), (square, LOW), (square, LOW)]
        + [((tok_rows, 2 * width), WIDE), ((tok_rows, 2 * width), LOW), ((3, width), WIDE)],
        (d_normed, projected_low, other_kv, seg_col, seg_row, *out_sides, unit, scale, vec_full),
    )
    down_kept, down_sent = halves(grad_down, down_order)
    up_kept, up_sent = halves(grad_up_t, up_order)
    down_got = xor_trade(down_sent, 1 << down_order[0])
    up_got = xor_trade(up_sent, 1 << up_order[0])
    other_grad = gate(other_grad, down_sent, up_sent)
    g_rows = jnp.concatenate(
        [
            rows_one[:2],
            rows_two[:2],
            jnp.zeros((2, width), WIDE),
            rows_one[2:],
            rows_two[2:],
            g_bias_up.reshape(-1, width),
            jnp.zeros((16 - vec_rows, width), WIDE),
        ],
        axis=0,
    )
    got_grad = core_trade(other_grad)
    if exact:
        block = ((dp_count, rows, side), LOW)
        d_qkv, *g_sides = run_kernel(
            pack_body,
            [((tok_rows, 3 * width), LOW), block, block, block, block],
            (index, d_query, own_grad, got_grad, tokens_in, d_attended, context_low, g_rows),
            [(wide_side, WIDE), (out_side, WIDE)],
            scalars=1,
        )
    else:
        d_kv = own_grad + got_grad.astype(WIDE)
        d_qkv = jnp.concatenate([d_query, d_kv.astype(LOW)], axis=1)
        sums = jnp.sum(d_qkv.astype(WIDE), axis=0)
        g_rows = g_rows.at[4].set(sums[:width]).at[5].set(sums[2 * width :]).astype(LOW)
        g_sides = []
        for part in range(2):
            at = slice(part * side, (part + 1) * side)
            whole = jnp.broadcast_to(g_rows[None, :, at], (devices, 16, side))
            g_qkv = over_tokens(d_qkv, tokens_in[:, at]).reshape(devices, qkv_cols, side)
            g_out = over_tokens(d_attended, context_low[:, at]).reshape(devices, out_cols, side)
            whole = jnp.concatenate(
                [
                    jnp.pad(g_qkv, ((0, 0), (0, split - 8 - qkv_cols), (0, 0))),
                    whole[:, :8],
                    jnp.pad(g_out, ((0, 0), (0, rows - split - 8 - out_cols), (0, 0))),
                    whole[:, 8:],
                ],
                axis=1,
            )
            whole = xor_order(whole.reshape(dp_count, 2, rows, side), rank, bits)
            g_sides += [pick(whole, core, 1), pick(whole, 1 - core, 1)]
    grad_down = down_kept + gate(down_got, *g_sides).astype(WIDE)
    grad_up_t = up_kept + gate(up_got, *g_sides).astype(WIDE)
    grad_down = scatter_relative(grad_down, down_order[1:])
    grad_up_t = scatter_relative(grad_up_t, up_order[1:])
    sums = []
    for kept, sent, order in (g_sides[:2] + [up_order], g_sides[2:] + [down_order]):
        total = kept.astype(WIDE) + core_trade(sent).astype(WIDE)
        sums.append(scatter_relative(total.reshape((2,) * bits + (rows, side)), order))
    d_tokens = d_resid_one + jnp.concatenate([plain(d_qkv, part) for part in qkv_sides], axis=1)

    grad_attn_t = jnp.concatenate([part.reshape(rows, side) for part in sums], axis=1)
    grad_qkv_t, grad_out_t = grad_attn_t[:qkv_cols], grad_attn_t[split : split + out_cols]
    grad_vectors = jnp.concatenate([grad_attn_t[split - 8 : split], grad_attn_t[rows - 8 :]], axis=0)
    grad_vectors = lax.dynamic_slice(grad_vectors, (0, first_col), (vec_rows, vec_cols))

    piece_rows = max(qkv_cols, up_cols)
    moments_t = [
        momentum_decay * moment + grad
        for moment, grad in (
            (mom_qkv.T, grad_qkv_t),
            (mom_out.T, grad_out_t),
            (mom_up.T, grad_up_t),
            (mom_down, grad_down),
        )
    ]
    new_mom_qkv, new_mom_out, new_mom_up = [moment.T for moment in moments_t[:3]]
    new_mom_down = moments_t[3]
    stacked = jnp.stack(
        [
            jnp.pad(moment.astype(LOW), ((0, piece_rows - moment.shape[0]), (0, 0)))
            for moment in moments_t
        ]
    )
    plane_step = dp_count // PLANES
    plane = rank // plane_step
    mine = [pick(stacked, plane, 0)]
    for offset in range(1, PLANES):
        mine.append(xor_trade(pick(stacked, plane ^ offset, 0), offset * plane_step))
    turned = orthogonal(jnp.concatenate(mine, axis=0), list(range(bits - 2)))
    turned = turned.reshape(PLANES, piece_rows, width)
    back = [turned[0]]
    for offset in range(1, PLANES):
        back.append(xor_trade(turned[offset], offset * plane_step))
    back = jnp.stack(back)
    ortho_t = [
        pick(back, plane ^ index, 0)[: moment.shape[0]].astype(WIDE)
        for index, moment in enumerate(moments_t)
    ]

    def updated(weight, ortho, longest):
        return weight - muon_rate * (0.2 * math.sqrt(longest) * ortho + muon_decay * weight)

    hidden = up_cols * devices
    new_w_qkv = updated(w_qkv, ortho_t[0].T, 3 * width)
    new_w_out = updated(w_out, ortho_t[1].T, width)
    new_w_up = updated(w_up, ortho_t[2].T, max(width, hidden))
    new_w_down = updated(w_down, ortho_t[3], max(width, hidden))

    new_first = beta_one * adam_first + (1.0 - beta_one) * grad_vectors
    new_second = beta_two * adam_second + (1.0 - beta_two) * grad_vectors * grad_vectors
    first_hat = new_first / (1.0 - beta_one**STEP)
    second_hat = new_second / (1.0 - beta_two**STEP)
    new_vectors = vectors - adam_rate * first_hat / (jnp.sqrt(second_hat) + adam_epsilon)
    return (
        output,
        d_tokens,
        grad_qkv_t.T,
        grad_out_t.T,
        grad_up_t.T,
        grad_down,
        grad_vectors,
        new_mom_qkv,
        new_mom_out,
        new_mom_up,
        new_mom_down,
        new_w_qkv,
        new_w_out,
        new_w_up,
        new_w_down,
        new_first,
        new_second,
        new_vectors,
    )


def solution(mesh):
    in_specs = (
        P(("dp", "fsdp"), None),
        P(("dp", "fsdp"), None),
        P("dp", None),
        P(None, ("dp", "fsdp")),
        P(None, ("dp", "fsdp")),
        P(None, ("dp", "fsdp")),
        P(("dp", "fsdp"), None),
        P(None, ("dp", "fsdp")),
        P(None, ("dp", "fsdp")),
        P(None, ("dp", "fsdp")),
        P(None, ("dp", "fsdp")),
        P(("dp", "fsdp"), None),
        P(None, ("dp", "fsdp")),
        P(None, ("dp", "fsdp")),
    )
    out_specs = (
        P(("dp", "fsdp"), None),
        P(("dp", "fsdp"), None),
        P(None, ("dp", "fsdp")),
        P(None, ("dp", "fsdp")),
        P(None, ("dp", "fsdp")),
        P(("dp", "fsdp"), None),
        P(None, ("dp", "fsdp")),
        P(None, ("dp", "fsdp")),
        P(None, ("dp", "fsdp")),
        P(None, ("dp", "fsdp")),
        P(("dp", "fsdp"), None),
        P(None, ("dp", "fsdp")),
        P(None, ("dp", "fsdp")),
        P(None, ("dp", "fsdp")),
        P(("dp", "fsdp"), None),
        P(None, ("dp", "fsdp")),
        P(None, ("dp", "fsdp")),
        P(None, ("dp", "fsdp")),
    )
    return jax.shard_map(
        per_device, mesh=mesh, in_specs=in_specs, out_specs=out_specs, check_vma=False
    )
```

```python
import functools
import math

import jax
import jax.numpy as jnp
from jax import lax
from jax.experimental import pallas as pl
from jax.experimental.pallas import tpu as pltpu
from jax.sharding import PartitionSpec as P

HD = 64
NS_ITERS = 2
STEP = 10

poly_one = 3.4445
poly_three = -4.775
poly_five = 2.0315
momentum_decay = 0.95
muon_rate = 0.3
muon_decay = 0.01
adam_rate = 0.2
beta_one = 0.9
beta_two = 0.999
adam_epsilon = 1e-08
norm_epsilon = 1e-05
ortho_epsilon = 1e-07
masked_score = -1e30
PLANES = 4
LOW = jnp.bfloat16
WIDE = jnp.float32


def xor_trade(block, distance):
    count = lax.axis_size("dp")
    return lax.ppermute(block, "dp", [(i, i ^ distance) for i in range(count)])


def core_trade(block):
    return lax.ppermute(block, "fsdp", [(0, 1), (1, 0)])


def bit_of(rank, place):
    return (rank >> place) & 1


def pick(block, index, axis):
    return lax.dynamic_index_in_dim(block, index, axis, keepdims=False)


def pair(mine, other, bit, axis):
    first = jnp.where(bit == 0, mine, other)
    second = jnp.where(bit == 0, other, mine)
    return jnp.stack([first, second], axis)


def higher(places, place):
    return sum(1 for other in places if other > place)


def gather_relative(block, order, done):
    for index, place in enumerate(order):
        axis = higher(done + order[:index], place)
        block = jnp.stack([block, xor_trade(block, 1 << place)], axis)
    return block


def tie(*values):
    return lax.optimization_barrier(values)


def xor_order(block, rank, bits):
    tail = block.shape[1:]
    block = block.reshape((2,) * bits + tail)
    for place in range(bits):
        axis = bits - 1 - place
        block = jnp.where(bit_of(rank, place) == 0, block, jnp.flip(block, axis))
    return block.reshape((-1,) + tail)


def nt(left, right):
    return lax.dot_general(left, right, (((1,), (1,)), ((), ())), preferred_element_type=WIDE)


def nn(left, right):
    return lax.dot_general(left, right, (((1,), (0,)), ((), ())), preferred_element_type=WIDE)


def tn(left, right):
    return lax.dot_general(left, right, (((0,), (0,)), ((), ())), preferred_element_type=WIDE)


def run_kernel(body, results, operands, scratch=(), scalars=0, room=10):
    places = [pltpu.SMEM] * scalars + [pltpu.VMEM] * (len(operands) - scalars)
    return pl.pallas_call(
        body,
        out_shape=[jax.ShapeDtypeStruct(shape, kind) for shape, kind in results],
        in_specs=[pl.BlockSpec(memory_space=place) for place in places],
        out_specs=[pl.BlockSpec(memory_space=pltpu.VMEM)] * len(results),
        scratch_shapes=[pltpu.VMEM(shape, kind) for shape, kind in scratch],
        compiler_params=pltpu.CompilerParams(vmem_limit_bytes=room * 1024 * 1024),
        cost_estimate=pl.CostEstimate(flops=1000, bytes_accessed=1000, transcendentals=0),
    )(*operands)


def gate(values, *needed):
    anywhere = pl.BlockSpec(memory_space=pl.ANY)
    return pl.pallas_call(
        lambda *refs: None,
        out_shape=[jax.ShapeDtypeStruct(value.shape, value.dtype) for value in values],
        in_specs=[anywhere] * (len(values) + len(needed)),
        out_specs=[anywhere] * len(values),
        input_output_aliases={place: place for place in range(len(values))},
        compiler_params=pltpu.CompilerParams(vmem_limit_bytes=1024 * 1024),
        cost_estimate=pl.CostEstimate(flops=0, bytes_accessed=0, transcendentals=0),
    )(*values, *needed)


MARK = ((8, 128), WIDE)


def step_body(count, splits, *refs):
    kept, got = refs[:count], refs[count : 2 * count]
    results = list(refs[2 * count + 1 :])
    results.pop()[...] = jnp.zeros(MARK[0], WIDE)
    for kept_ref, got_ref in zip(kept, got):
        if splits:
            for half in range(2):
                part = kept_ref[:, half].astype(WIDE) + got_ref[:, half].astype(WIDE)
                result = results.pop(0)
                result[...] = part.astype(result.dtype)
        else:
            result = results.pop(0)
            result[...] = (kept_ref[...].astype(WIDE) + got_ref[...].astype(WIDE)).astype(result.dtype)


def summed(kept, got, mark, kind):
    results = [(part.shape, kind) for part in kept] + [MARK]
    body = functools.partial(step_body, len(kept), False)
    *totals, mark = run_kernel(body, results, (*kept, *got, mark))
    return totals, mark


def stepped(kept, got, mark, orders, tail):
    results, operands = [], []
    for part, order in zip(kept, orders):
        above = higher(order, order[0])
        shape = (2**above, 2 ** (len(order) - 1 - above)) + tail
        operands.append((shape[0], 2) + shape[1:])
        results += [(shape, WIDE), (shape, LOW)]
    body = functools.partial(step_body, len(kept), True)
    parts = [part.reshape(shape) for part, shape in zip((*kept, *got), operands * 2)]
    *halves, mark = run_kernel(body, results + [MARK], (*parts, mark))
    return halves[::2], halves[1::2], mark


def mean_of(values):
    return jnp.sum(values, axis=-1, keepdims=True) * (1.0 / values.shape[-1])


def normalized(values):
    center = values - mean_of(values)
    scale = lax.rsqrt(mean_of(center * center) + norm_epsilon)
    return center * scale, scale


def norm_back(grad, unit, scale, gain):
    inner = grad * gain
    return scale * (inner - mean_of(inner) - unit * mean_of(inner * unit))


def head_probs(query, keys, allowed):
    scores = nt(query, keys) * (HD ** (-0.5))
    scores = jnp.where(allowed, scores, masked_score)
    exp_scores = jnp.exp(scores - jnp.max(scores, axis=-1, keepdims=True))
    return exp_scores / jnp.sum(exp_scores, axis=-1, keepdims=True)


def head_parts(head, width, own_ref, other_ref):
    at = slice(head * HD, (head + 1) * HD)
    keys = jnp.concatenate([own_ref[:, width:][:, at], other_ref[:, :width][:, at]], axis=0)
    values = jnp.concatenate([own_ref[:, 2 * width :][:, at], other_ref[:, width:][:, at]], axis=0)
    return own_ref[:, at], keys, values


def segments(index_ref, lengths_ref, places):
    half = places.size // 2 if places.shape[0] == 1 else places.shape[0]
    places = jnp.where(index_ref[1] == 0, places, (places + half) & (2 * half - 1))
    result, bound = jnp.zeros(places.shape, jnp.int32), 0
    for entry in range(lengths_ref.shape[1]):
        bound = bound + lengths_ref[0, entry]
        result = result + jnp.where(places >= bound, 1, 0)
    return result


def own_segments(index_ref, lengths_ref, tok_rows):
    return segments(index_ref, lengths_ref, lax.broadcasted_iota(jnp.int32, (tok_rows, 1), 0))


def allowed_pairs(index_ref, lengths_ref, tok_rows):
    every = lax.broadcasted_iota(jnp.int32, (1, 2 * tok_rows), 1)
    return own_segments(index_ref, lengths_ref, tok_rows) == segments(index_ref, lengths_ref, every)


def attend_body(
    index_ref, lengths_ref, own_ref, other_ref, one_ref, two_ref, tokens_ref, vec_ref,
    context_ref, normed_ref, low_ref, unit_ref, scale_ref,
):
    width = tokens_ref.shape[1]
    side = width // 2
    allowed = allowed_pairs(index_ref, lengths_ref, tokens_ref.shape[0])
    for start in range(0, width // HD, 2):
        found = []
        for head in (start, start + 1):
            query, keys, values = head_parts(head, width, own_ref, other_ref)
            found.append(nn(head_probs(query, keys, allowed).astype(LOW), values))
        context_ref[:, start * HD : (start + 2) * HD] = jnp.concatenate(found, axis=1).astype(LOW)
    attended = (
        nt(context_ref[:, :side], one_ref[...])
        + nt(context_ref[:, side:], two_ref[...])
        + vec_ref[6:7, :]
    )
    unit, scale = normalized(tokens_ref[...].astype(WIDE) + attended)
    normed = unit * vec_ref[0:1, :] + vec_ref[1:2, :]
    normed_ref[...] = normed
    low_ref[...] = normed.astype(LOW)
    unit_ref[...] = unit
    scale_ref[...] = scale


def attend_back_body(
    index_ref, lengths_ref, d_normed_ref, own_ref, other_ref, one_ref, two_ref, unit_ref, scale_ref, vec_ref,
    resid_ref, attended_ref, query_ref, own_grad_ref, other_grad_ref, rows_ref,
):
    tok_rows, width = d_normed_ref.shape
    allowed = allowed_pairs(index_ref, lengths_ref, tok_rows)
    grad, unit = d_normed_ref[...], unit_ref[...]
    resid = norm_back(grad, unit, scale_ref[...], vec_ref[0:1, :])
    low = resid.astype(LOW)
    resid_ref[...] = resid
    attended_ref[...] = low
    rows_ref[0:1, :] = jnp.sum(grad * unit, axis=0, keepdims=True)
    rows_ref[1:2, :] = jnp.sum(grad, axis=0, keepdims=True)
    rows_ref[2:3, :] = jnp.sum(low.astype(WIDE), axis=0, keepdims=True)
    d_context = jnp.concatenate([nn(low, one_ref[...]), nn(low, two_ref[...])], axis=1).astype(LOW)
    factor = HD ** (-0.5)
    for start in range(0, width // HD, 2):
        found = []
        for head in (start, start + 1):
            query, keys, values = head_parts(head, width, own_ref, other_ref)
            grad_head = d_context[:, head * HD : (head + 1) * HD]
            probs = head_probs(query, keys, allowed)
            d_probs = nt(grad_head, values)
            inner = jnp.sum(probs * d_probs, axis=-1, keepdims=True)
            d_scores = (probs * (d_probs - inner)).astype(LOW)
            found.append(
                (nn(d_scores, keys) * factor, tn(d_scores, query) * factor,
                 tn(probs.astype(LOW), grad_head))
            )
        d_query, d_keys, d_values = [
            jnp.concatenate([first, second], axis=1) for first, second in zip(*found)
        ]
        at = slice(start * HD, (start + 2) * HD)
        shifted = slice(width + start * HD, width + (start + 2) * HD)
        query_ref[:, at] = d_query.astype(LOW)
        own_grad_ref[:, at] = d_keys[:tok_rows]
        own_grad_ref[:, shifted] = d_values[:tok_rows]
        other_grad_ref[:, at] = d_keys[tok_rows:].astype(LOW)
        other_grad_ref[:, shifted] = d_values[tok_rows:].astype(LOW)


def hidden_body(
    index_ref, lengths_ref, normed_ref, low_ref, cotangent_ref, vec_ref, bias_ref, *refs
):
    up, down = refs[:4], refs[4:8]
    output_ref, grad_ref, g_bias, rows_ref = refs[8:12]
    g_up, g_down = refs[12:16], refs[16:20]
    act_ref, slope_ref = refs[20:]
    low = low_ref[...]
    lowered = vec_ref[7:8, :] + jnp.zeros(normed_ref.shape, WIDE)
    blocks = [(core, high, lower) for core in range(2) for high in range(2) for lower in range(2)]
    for place, (core, high, lower) in enumerate(blocks):
        pre = nt(low, up[2 * core + lower][high]) + bias_ref[place : place + 1, :]
        cdf = 0.5 * (1.0 + lax.erf(pre * 0.7071067811865476))
        act = (pre * cdf).astype(LOW)
        act_ref[place] = act
        slope_ref[place] = cdf + pre * jnp.exp(-0.5 * pre * pre) * 0.3989422804014327
        lowered = lowered + nn(act, down[2 * core + high][lower])
    unit, scale = normalized(normed_ref[...] + lowered)
    output_ref[...] = (unit * vec_ref[2:3, :] + vec_ref[3:4, :]).astype(LOW)
    segment = own_segments(index_ref, lengths_ref, low.shape[0])
    live = jnp.where(segment < lengths_ref.shape[1], 1.0, 0.0)
    top = cotangent_ref[...].astype(WIDE) * live
    resid = norm_back(top, unit, scale, vec_ref[2:3, :])
    d_lowered = resid.astype(LOW)
    rows_ref[0:1, :] = jnp.sum(top * unit, axis=0, keepdims=True)
    rows_ref[1:2, :] = jnp.sum(top, axis=0, keepdims=True)
    rows_ref[2:3, :] = jnp.sum(d_lowered.astype(WIDE), axis=0, keepdims=True)
    total = resid
    for place, (core, high, lower) in enumerate(blocks):
        g_down[2 * core + high][lower] = tn(act_ref[place], d_lowered).astype(LOW)
        d_pre = (nt(d_lowered, down[2 * core + high][lower]) * slope_ref[place]).astype(LOW)
        g_bias[place : place + 1, :] = jnp.sum(d_pre.astype(WIDE), axis=0, keepdims=True)
        g_up[2 * core + lower][high] = tn(d_pre, low).astype(LOW)
        total = total + nn(d_pre, up[2 * core + lower][high])
    grad_ref[...] = total


def chunk_slot(rank, core, chunk, far):
    place = jnp.bitwise_xor(rank, chunk // 2)
    block = 4 * jnp.bitwise_xor(core, chunk % 2) + jnp.bitwise_and(place, 3)
    return far * block + lax.shift_right_logical(place, 2)


def unpack_body(
    index_ref, own_one, other_one, own_two, other_two, tokens_ref,
    projected_ref, qkv_one, qkv_two, out_one, out_two, vec_ref, bias_ref, chunk_ref,
):
    rank, core = index_ref[0], index_ref[1]
    count, rows, side = own_one.shape
    width = 2 * side
    qkv_cols = qkv_one.shape[0] // (2 * count)
    out_cols = out_one.shape[0] // (2 * count)
    split = qkv_cols + 8
    total = []
    for own, other, qkv, out in (
        (own_one, other_one, qkv_one, out_one), (own_two, other_two, qkv_two, out_two)
    ):
        vec = jnp.zeros((16, side), WIDE)
        for place in range(count):
            slot = jnp.bitwise_xor(rank, place)
            mine, theirs = own[slot].astype(WIDE), other[slot].astype(WIDE)
            first = jnp.where(core == 0, mine, theirs)
            second = jnp.where(core == 0, theirs, mine)
            both = jnp.concatenate([first[:qkv_cols], second[:qkv_cols]], axis=0)
            qkv[2 * qkv_cols * place : 2 * qkv_cols * (place + 1), :] = both.astype(LOW)
            both = [part[split : split + out_cols] for part in (first, second)]
            both = jnp.concatenate(both, axis=0)
            out[2 * out_cols * place : 2 * out_cols * (place + 1), :] = both.astype(LOW)
            vec = vec + jnp.concatenate(
                [mine[qkv_cols:split] + theirs[qkv_cols:split], mine[rows - 8 :] + theirs[rows - 8 :]],
                axis=0,
            )
        total.append(vec)
    vec = jnp.concatenate(total, axis=1)
    vec_ref[...] = vec
    far, cols = count // 4, chunk_ref.shape[1]
    per_row = width // cols
    for chunk in range(2 * count):
        at = slice((chunk % per_row) * cols, (chunk % per_row + 1) * cols)
        row = 8 + chunk // per_row
        chunk_ref[pl.ds(chunk_slot(rank, core, chunk, far), 1), :] = vec[row : row + 1, at]
    for block in range(8):
        parts = [chunk_ref[far * block + part : far * block + part + 1, :] for part in range(far)]
        bias_ref[block : block + 1, :] = jnp.concatenate(parts, axis=1)
    for part, bias in enumerate((vec[4:5], None, vec[5:6])):
        at = slice(part * width, (part + 1) * width)
        block = nt(tokens_ref[:, :side], qkv_one[at, :]) + nt(tokens_ref[:, side:], qkv_two[at, :])
        projected_ref[:, at] = (block if bias is None else block + bias).astype(LOW)


def pack_body(
    index_ref, query_ref, own_ref, got_ref, tokens_ref, attended_ref, context_ref,
    one_ref, two_ref, g_bias_ref,
    d_qkv_ref, kept_one, sent_one, kept_two, sent_two, wide_ref, out_ref, chunk_ref, rows_ref,
):
    rank, core = index_ref[0], index_ref[1]
    count, rows, side = kept_one.shape
    width = 2 * side
    qkv_cols = wide_ref.shape[0] // (2 * count)
    out_cols = out_ref.shape[0] // (2 * count)
    d_qkv_ref[:, :width] = query_ref[...]
    d_qkv_ref[:, width:] = (own_ref[...] + got_ref[...].astype(WIDE)).astype(LOW)
    far, cols = count // 4, chunk_ref.shape[1]
    for block in range(8):
        for part in range(far):
            at = slice(part * cols, (part + 1) * cols)
            chunk_ref[far * block + part : far * block + part + 1, :] = g_bias_ref[block : block + 1, at]
    rows_ref[...] = jnp.zeros(rows_ref.shape, WIDE)
    rows_ref[0:2, :] = one_ref[:2]
    rows_ref[2:4, :] = two_ref[:2]
    rows_ref[6:7, :] = one_ref[2:]
    rows_ref[7:8, :] = two_ref[2:]
    for part, row in ((0, 4), (2, 5)):
        block = slice(part * width, (part + 1) * width)
        rows_ref[row : row + 1, :] = jnp.sum(d_qkv_ref[:, block].astype(WIDE), axis=0, keepdims=True)
    per_row = width // cols
    for chunk in range(2 * count):
        at = slice((chunk % per_row) * cols, (chunk % per_row + 1) * cols)
        row = 8 + chunk // per_row
        rows_ref[row : row + 1, at] = chunk_ref[pl.ds(chunk_slot(rank, core, chunk, far), 1), :]
    for index, (kept, sent) in enumerate(((kept_one, sent_one), (kept_two, sent_two))):
        at = slice(index * side, (index + 1) * side)
        for part in range(3):
            block = slice(part * width, (part + 1) * width)
            wide_ref[block, :] = tn(d_qkv_ref[:, block], tokens_ref[:, at])
        out_ref[...] = tn(attended_ref[...], context_ref[:, at])
        low_rows = rows_ref[:8, at]
        high_rows = rows_ref[8:, at]
        for place in range(count):
            slot = jnp.bitwise_xor(rank, place)
            blocks = []
            for chunk in (2 * place, 2 * place + 1):
                blocks.append(
                    jnp.concatenate(
                        [
                            wide_ref[qkv_cols * chunk : qkv_cols * (chunk + 1), :],
                            low_rows,
                            out_ref[out_cols * chunk : out_cols * (chunk + 1), :],
                            high_rows,
                        ],
                        axis=0,
                    )
                )
            kept[slot] = jnp.where(core == 0, blocks[0], blocks[1]).astype(LOW)
            sent[slot] = jnp.where(core == 0, blocks[1], blocks[0]).astype(LOW)


def rows_by_cols(left, right):
    return jnp.einsum("td,fd->tf", left, right, preferred_element_type=WIDE)


def plain(left, right):
    return jnp.dot(left, right, preferred_element_type=WIDE)


def over_tokens(left, right):
    return jnp.einsum("ta,tb->ab", left, right, preferred_element_type=WIDE).astype(LOW)


def moment_body(index_ref, *refs):
    kept_one, kept_two, got_one, got_two, kept_up, kept_down, got_up, got_down = refs[:8]
    moments, pieces, grads, results = refs[8:12], refs[12:16], refs[16:20], refs[20:24]
    vec_ref, stack_ref = refs[24:]
    attn = jnp.concatenate(
        [kept_one[...] + got_one[...].astype(WIDE), kept_two[...] + got_two[...].astype(WIDE)], axis=1
    )
    qkv_cols, out_cols = moments[0].shape[0], moments[1].shape[0]
    split = qkv_cols + 8
    vec_ref[...] = jnp.concatenate([attn[qkv_cols:split], attn[split + out_cols :]], axis=0)
    sums = (
        attn[:qkv_cols],
        attn[split : split + out_cols],
        kept_up[...] + got_up[...].astype(WIDE),
        kept_down[...] + got_down[...].astype(WIDE),
    )
    for place, (moment, total, grad, result) in enumerate(zip(moments, sums, grads, results)):
        grad[...] = total
        updated = momentum_decay * moment[...] + total
        result[...] = updated
        missing = stack_ref.shape[1] - updated.shape[0]
        if missing:
            updated = jnp.concatenate([updated, jnp.zeros((missing, updated.shape[1]), WIDE)], axis=0)
        stack_ref[place] = updated.astype(LOW)
    plane = index_ref[2]
    for offset, piece in enumerate(pieces):
        piece[...] = stack_ref[jnp.bitwise_xor(plane, offset)]


def gram_body(index_ref, *refs):
    rows, kept_ref, sent_ref = refs[:-2], refs[-2], refs[-1]
    gram = tn(rows[0][...], rows[0][...])
    for part in rows[1:]:
        gram = gram + tn(part[...], part[...])
    third = gram.shape[0] // 3
    first = gram[:third]
    second = jnp.concatenate([gram[third : 2 * third, third:], gram[2 * third :, 2 * third :]], axis=1)
    kept_ref[...] = jnp.where(index_ref[1] == 0, first, second)
    sent_ref[...] = jnp.where(index_ref[1] == 0, second, first).astype(LOW)


def orthogonal_body(index_ref, own_ref, other_ref, *refs):
    count = (len(refs) - 1) // 2
    rows, results, gram_ref = refs[:count], refs[count : 2 * count], refs[-1]
    third = own_ref.shape[0]
    own, other = own_ref[...].astype(WIDE), other_ref[...].astype(WIDE)
    first = jnp.where(index_ref[1] == 0, own, other)
    second = jnp.where(index_ref[1] == 0, other, own)
    gram_ref[:third, :] = first
    gram_ref[third : 2 * third, third:] = second[:, : 2 * third]
    gram_ref[2 * third :, 2 * third :] = second[:, 2 * third :]
    gram_ref[third : 2 * third, :third] = first[:, third : 2 * third].T
    gram_ref[2 * third :, :third] = first[:, 2 * third :].T
    gram_ref[2 * third :, third : 2 * third] = second[:, third : 2 * third].T
    trace = jnp.zeros((1, 1), WIDE)
    spot = lax.broadcasted_iota(jnp.int32, (third, third), 0)
    eye = spot == lax.broadcasted_iota(jnp.int32, (third, third), 1)
    for part in range(3):
        at = slice(part * third, (part + 1) * third)
        block = jnp.where(eye, gram_ref[at, at], 0.0)
        trace = trace + jnp.sum(jnp.sum(block, axis=1, keepdims=True), axis=0, keepdims=True)
    factor = 1.0 / (jnp.sqrt(trace) + ortho_epsilon)
    gram_mat = gram_ref[...] * (factor * factor)
    low_x = [part[...] for part in rows]
    current = [part.astype(WIDE) * factor for part in low_x]
    for iteration in range(NS_ITERS):
        low_gram = gram_mat.astype(LOW)
        low_mixing = (poly_three * gram_mat + poly_five * nn(low_gram, low_gram)).astype(LOW)
        scale = factor if iteration == 0 else 1.0
        current = [
            poly_one * part + nn(low, low_mixing) * scale for part, low in zip(current, low_x)
        ]
        low_x = [part.astype(LOW) for part in current]
        if iteration < NS_ITERS - 1:
            product = nn(low_mixing, low_gram)
            gram_mat = (
                (poly_one * poly_one) * gram_mat
                + (2.0 * poly_one) * product
                + nn(low_mixing, product.astype(LOW))
            )
    for result, part in zip(results, low_x):
        result[...] = part


def orthogonal(rows, index, low_bits):
    count, width = rows[0].shape
    third = width // 3
    kept, sent = run_kernel(
        gram_body, [((third, width), WIDE), ((third, width), LOW)], (index, *rows), scalars=1
    )
    total = kept + core_trade(sent).astype(WIDE)
    parts = [total[: third // 2], total[third // 2 :]]
    for step in range(len(low_bits)):
        for way in range(2):
            place = low_bits[(step + way) % len(low_bits)]
            moved = xor_trade(parts[way].astype(LOW), 1 << place)
            parts[way] = parts[way] + moved.astype(WIDE)
    own = jnp.concatenate(parts, axis=0).astype(LOW)
    return run_kernel(
        orthogonal_body,
        [((count, width), LOW)] * len(rows),
        (index, own, core_trade(own), *rows),
        [((width, width), WIDE)],
        scalars=1,
        room=26,
    )


def per_device(
    tokens_in,
    cotangent,
    seq_lengths,
    w_qkv,
    w_out,
    w_up,
    w_down,
    vectors,
    mom_qkv,
    mom_out,
    mom_up,
    mom_down,
    adam_first,
    adam_second,
):
    tok_rows, width = tokens_in.shape
    side = width // 2
    dp_count = lax.axis_size("dp")
    bits = dp_count.bit_length() - 1
    rank, core = lax.axis_index("dp"), lax.axis_index("fsdp")
    up_order = list(range(bits))
    down_order = [1, 0] + list(range(2, bits))
    qkv_cols, out_cols, up_cols = w_qkv.shape[1], w_out.shape[1], w_up.shape[1]
    vec_rows, vec_cols = vectors.shape
    devices = 2 * dp_count

    index = jnp.stack([rank, core, lax.shift_right_logical(rank, bits - 2)]).astype(jnp.int32)
    first_col = vec_cols * (2 * rank + core)
    vec_wide = lax.dynamic_update_slice(
        jnp.zeros((16, width), LOW), vectors.astype(LOW), (0, first_col)
    )
    split = -(-(qkv_cols + 8) // 16) * 16
    rows = split + -(-(out_cols + 8) // 16) * 16
    exact = qkv_cols % 8 == 0 and out_cols % 8 == 0 and split == qkv_cols + 8 and rows == split + out_cols + 8
    pack = jnp.concatenate(
        [
            jnp.pad(w_qkv.T.astype(LOW), ((0, split - 8 - qkv_cols), (0, 0))),
            vec_wide[:8],
            jnp.pad(w_out.T.astype(LOW), ((0, rows - split - 8 - out_cols), (0, 0))),
            vec_wide[8:],
        ],
        axis=0,
    )
    pack_one, pack_two = pack[:, :side], pack[:, side:]
    far = up_order[2:][::-1]
    near_one, near_two = [1, 0], [0, 1]
    all_one = gather_relative(pack_one, far, [])
    all_two = gather_relative(pack_two, far, [])
    hidden_low = (w_up.T.astype(LOW), w_down.astype(LOW))
    all_one, all_two, *hidden_low = tie(all_one, all_two, *hidden_low)
    all_one = gather_relative(all_one, near_one, far)
    all_two = gather_relative(all_two, near_two, far)
    hidden_far = [gather_relative(part, far, []).reshape(-1, width) for part in hidden_low]
    all_one, all_two, *hidden_far = tie(all_one, all_two, *hidden_far)
    hidden_near = [
        jnp.stack([part, xor_trade(part, 1 << near[0])])
        for part, near in zip(hidden_far, (near_one, near_two))
    ]
    own_packs = [part.reshape((dp_count, rows, side)) for part in (all_one, all_two)]
    other_packs = [core_trade(part) for part in own_packs]
    packs = (own_packs[0], other_packs[0], own_packs[1], other_packs[1])
    far_count = dp_count // 4
    hidden_rows = far_count * up_cols
    wide_side, out_side = (devices * qkv_cols, side), (devices * out_cols, side)
    if exact:
        projected_low, *sides, vec_full, up_bias = run_kernel(
            unpack_body,
            [((tok_rows, 3 * width), LOW), (wide_side, LOW), (wide_side, LOW)]
            + [(out_side, LOW), (out_side, LOW), ((16, width), WIDE), ((8, hidden_rows), WIDE)],
            (index, *packs, tokens_in),
            [((devices, up_cols), WIDE)],
            scalars=1,
            room=18,
        )
        qkv_sides, out_sides = sides[:2], sides[2:]
    else:
        natural = [
            xor_order(pair(own, other, core, 1), rank, bits).reshape(devices, rows, side)
            for own, other in zip(own_packs, other_packs)
        ]
        qkv_sides = [part[:, :qkv_cols].reshape(wide_side) for part in natural]
        out_sides = [part[:, split : split + out_cols].reshape(out_side) for part in natural]
        vec_full = jnp.concatenate(natural, axis=2).astype(WIDE)
        vec_full = jnp.concatenate([vec_full[:, split - 8 : split], vec_full[:, rows - 8 :]], axis=1)
        vec_full = jnp.sum(vec_full, axis=0)
        qkv_bias = jnp.concatenate([vec_full[4], jnp.zeros((width,), WIDE), vec_full[5]])
        projected = rows_by_cols(tokens_in[:, :side], qkv_sides[0])
        projected = projected + rows_by_cols(tokens_in[:, side:], qkv_sides[1])
        projected_low = (projected + qkv_bias).astype(LOW)
        up_bias = xor_order(vec_full[8:12].reshape(dp_count, 2, up_cols), rank, bits)
        up_bias = up_bias.reshape(far_count, 2, 2, 2, up_cols).transpose(3, 1, 2, 0, 4)
        up_bias = up_bias.reshape(2, 4, hidden_rows)
        up_bias = jnp.where(core == 0, up_bias, up_bias[::-1]).reshape(8, hidden_rows)
    own_kv = projected_low[:, width:]
    other_kv = core_trade(own_kv)
    square = (tok_rows, width)
    context_low, normed, normed_low, unit, scale = run_kernel(
        attend_body,
        [(square, LOW), (square, WIDE), (square, LOW), (square, WIDE), ((tok_rows, 1), WIDE)],
        (index, seq_lengths, projected_low, other_kv, *out_sides, tokens_in, vec_full),
        scalars=2,
    )
    hidden_got = [xor_trade(part, 1 << near[1]) for part, near in zip(hidden_near, (near_one, near_two))]
    hidden_got = gate(hidden_got, scale)
    pieces = []
    for part, got in zip(hidden_near, hidden_got):
        pieces += [part, got, core_trade(part), core_trade(got)]
    piece = hidden_near[0].shape
    output, d_normed, g_bias_up, rows_two, *grads = run_kernel(
        hidden_body,
        [(square, LOW), (square, WIDE), ((8, hidden_rows), WIDE), ((3, width), WIDE)]
        + [(piece, LOW)] * 8,
        (index, seq_lengths, normed, normed_low, cotangent, vec_full, up_bias, *pieces),
        [((8, tok_rows, hidden_rows), LOW), ((8, tok_rows, hidden_rows), WIDE)],
        room=18,
        scalars=2,
    )
    hidden_orders = (up_order, [1] + up_order[2:] + [0])
    hidden_left = [[bits] + up_order[2:], up_order[2:] + [bits]]
    mark = jnp.zeros(*MARK)
    hidden_sent, mark = summed(
        (grads[1], grads[5]), (core_trade(grads[3]), core_trade(grads[7])), mark, LOW
    )
    hidden_kept, _ = summed(
        (grads[0], grads[4]), (core_trade(grads[2]), core_trade(grads[6])), mark, WIDE
    )
    d_resid_one, d_attended, d_query, own_grad, other_grad, rows_one = run_kernel(
        attend_back_body,
        [(square, WIDE), (square, LOW), (square, LOW)]
        + [((tok_rows, 2 * width), WIDE), ((tok_rows, 2 * width), LOW), ((3, width), WIDE)],
        (index, seq_lengths, d_normed, projected_low, other_kv, *out_sides, unit, scale, vec_full),
        scalars=2,
    )
    (other_grad,) = gate((other_grad,), mark)
    got_grad = core_trade(other_grad)
    if exact:
        block = ((dp_count, rows, side), LOW)
        d_qkv, *g_sides = run_kernel(
            pack_body,
            [((tok_rows, 3 * width), LOW), block, block, block, block],
            (index, d_query, own_grad, got_grad, tokens_in, d_attended, context_low)
            + (rows_one, rows_two, g_bias_up),
            [(wide_side, WIDE), (out_side, WIDE), ((devices, up_cols), WIDE), ((16, width), WIDE)],
            scalars=1,
            room=20,
        )
    else:
        d_kv = own_grad + got_grad.astype(WIDE)
        d_qkv = jnp.concatenate([d_query, d_kv.astype(LOW)], axis=1)
        sums = jnp.sum(d_qkv.astype(WIDE), axis=0, keepdims=True)
        g_bias_up = g_bias_up.reshape(2, 4, hidden_rows)
        g_bias_up = jnp.where(core == 0, g_bias_up, g_bias_up[::-1])
        g_bias_up = g_bias_up.reshape(2, 2, 2, far_count, up_cols).transpose(3, 1, 2, 0, 4)
        g_bias_up = xor_order(g_bias_up.reshape(dp_count, 2, up_cols), rank, bits)
        g_rows = [rows_one[:2], rows_two[:2], sums[:, :width], sums[:, 2 * width :]]
        g_rows += [rows_one[2:], rows_two[2:], g_bias_up.reshape(-1, width)]
        g_rows = jnp.concatenate(g_rows + [jnp.zeros((4, width), WIDE)], axis=0).astype(LOW)
        g_sides = []
        for part in range(2):
            at = slice(part * side, (part + 1) * side)
            whole = jnp.broadcast_to(g_rows[None, :, at], (devices, 16, side))
            g_qkv = over_tokens(d_qkv, tokens_in[:, at]).reshape(devices, qkv_cols, side)
            g_out = over_tokens(d_attended, context_low[:, at]).reshape(devices, out_cols, side)
            whole = jnp.concatenate(
                [
                    jnp.pad(g_qkv, ((0, 0), (0, split - 8 - qkv_cols), (0, 0))),
                    whole[:, :8],
                    jnp.pad(g_out, ((0, 0), (0, rows - split - 8 - out_cols), (0, 0))),
                    whole[:, 8:],
                ],
                axis=1,
            )
            whole = xor_order(whole.reshape(dp_count, 2, rows, side), rank, bits)
            g_sides += [pick(whole, core, 1), pick(whole, 1 - core, 1)]
    attn_orders = (up_order, down_order)
    attn_kept = g_sides[::2]
    attn_got = [core_trade(part) for part in g_sides[1::2]]
    for step in range(bits):
        got = [xor_trade(sent, 1 << order[step]) for sent, order in zip(hidden_sent, hidden_orders)]
        if step < bits - 1:
            left = [order[step:] for order in hidden_left]
            hidden_kept, hidden_sent, mark = stepped(hidden_kept, got, mark, left, (up_cols, width))
        left = [order[step:] for order in attn_orders]
        attn_kept, attn_sent, _ = stepped(attn_kept, attn_got, mark, left, (rows, side))
        attn_got = [
            xor_trade(sent, 1 << order[step]) for sent, order in zip(attn_sent, attn_orders)
        ]
    last = [part.reshape(rows, side) for part in (*attn_kept, *attn_got)]
    last += [part.reshape(up_cols, width) for part in (*hidden_kept, *got)]
    d_tokens = d_resid_one + jnp.concatenate([plain(d_qkv, part) for part in qkv_sides], axis=1)

    piece_rows = max(qkv_cols, up_cols)
    moments = (mom_qkv.T, mom_out.T, mom_up.T, mom_down)
    plane_step = dp_count // PLANES
    if exact:
        shapes = [(moment.shape, WIDE) for moment in moments]
        results = run_kernel(
            moment_body,
            [((piece_rows, width), LOW)] * PLANES + shapes + shapes + [((16, width), WIDE)],
            (index, *last, *moments),
            [((PLANES, piece_rows, width), LOW)],
            scalars=1,
        )
        pieces = results[:PLANES]
        grads_t, moments_t = results[PLANES : 2 * PLANES], results[2 * PLANES : 3 * PLANES]
        vec_sums = results[-1]
    else:
        plane = lax.shift_right_logical(rank, bits - 2)
        attn = [kept.astype(WIDE) + part.astype(WIDE) for kept, part in zip(last[:2], last[2:4])]
        attn = jnp.concatenate(attn, axis=1)
        grads_t = [attn[:qkv_cols], attn[split : split + out_cols]]
        grads_t += [kept + part.astype(WIDE) for kept, part in zip(last[4:6], last[6:8])]
        vec_sums = jnp.concatenate([attn[split - 8 : split], attn[rows - 8 :]], axis=0)
        moments_t = [momentum_decay * moment + grad for moment, grad in zip(moments, grads_t)]
        stacked = [
            jnp.pad(moment.astype(LOW), ((0, piece_rows - moment.shape[0]), (0, 0)))
            for moment in moments_t
        ]
        stacked = jnp.stack(stacked)
        pieces = [pick(stacked, plane ^ offset, 0) for offset in range(PLANES)]
    grad_qkv_t, grad_out_t, grad_up_t, grad_down = grads_t
    grad_vectors = lax.dynamic_slice(vec_sums, (0, first_col), (vec_rows, vec_cols))
    new_mom_qkv, new_mom_out, new_mom_up = [moment.T for moment in moments_t[:3]]
    new_mom_down = moments_t[3]
    mine = [pieces[0]]
    for offset in range(1, PLANES):
        mine.append(xor_trade(pieces[offset], offset * plane_step))
    turned = orthogonal(mine, index, list(range(bits - 2)))
    back = [turned[0]]
    for offset in range(1, PLANES):
        back.append(xor_trade(turned[offset], offset * plane_step))
    back = jnp.stack(back)
    plane = lax.shift_right_logical(rank, bits - 2)
    ortho_t = [
        pick(back, plane ^ index, 0)[: moment.shape[0]].astype(WIDE)
        for index, moment in enumerate(moments_t)
    ]

    def updated(weight, ortho, longest):
        return weight - muon_rate * (0.2 * math.sqrt(longest) * ortho + muon_decay * weight)

    hidden = up_cols * devices
    new_w_qkv = updated(w_qkv, ortho_t[0].T, 3 * width)
    new_w_out = updated(w_out, ortho_t[1].T, width)
    new_w_up = updated(w_up, ortho_t[2].T, max(width, hidden))
    new_w_down = updated(w_down, ortho_t[3], max(width, hidden))

    new_first = beta_one * adam_first + (1.0 - beta_one) * grad_vectors
    new_second = beta_two * adam_second + (1.0 - beta_two) * grad_vectors * grad_vectors
    first_hat = new_first / (1.0 - beta_one**STEP)
    second_hat = new_second / (1.0 - beta_two**STEP)
    new_vectors = vectors - adam_rate * first_hat / (jnp.sqrt(second_hat) + adam_epsilon)
    return (
        output,
        d_tokens,
        grad_qkv_t.T,
        grad_out_t.T,
        grad_up_t.T,
        grad_down,
        grad_vectors,
        new_mom_qkv,
        new_mom_out,
        new_mom_up,
        new_mom_down,
        new_w_qkv,
        new_w_out,
        new_w_up,
        new_w_down,
        new_first,
        new_second,
        new_vectors,
    )


def solution(mesh):
    in_specs = (
        P(("dp", "fsdp"), None),
        P(("dp", "fsdp"), None),
        P("dp", None),
        P(None, ("dp", "fsdp")),
        P(None, ("dp", "fsdp")),
        P(None, ("dp", "fsdp")),
        P(("dp", "fsdp"), None),
        P(None, ("dp", "fsdp")),
        P(None, ("dp", "fsdp")),
        P(None, ("dp", "fsdp")),
        P(None, ("dp", "fsdp")),
        P(("dp", "fsdp"), None),
        P(None, ("dp", "fsdp")),
        P(None, ("dp", "fsdp")),
    )
    out_specs = (
        P(("dp", "fsdp"), None),
        P(("dp", "fsdp"), None),
        P(None, ("dp", "fsdp")),
        P(None, ("dp", "fsdp")),
        P(None, ("dp", "fsdp")),
        P(("dp", "fsdp"), None),
        P(None, ("dp", "fsdp")),
        P(None, ("dp", "fsdp")),
        P(None, ("dp", "fsdp")),
        P(None, ("dp", "fsdp")),
        P(("dp", "fsdp"), None),
        P(None, ("dp", "fsdp")),
        P(None, ("dp", "fsdp")),
        P(None, ("dp", "fsdp")),
        P(("dp", "fsdp"), None),
        P(None, ("dp", "fsdp")),
        P(None, ("dp", "fsdp")),
        P(None, ("dp", "fsdp")),
    )
    return jax.shard_map(
        per_device, mesh=mesh, in_specs=in_specs, out_specs=out_specs, check_vma=False
    )
```

```python
import functools
import math

import jax
import jax.numpy as jnp
from jax import lax
from jax.experimental import pallas as pl
from jax.experimental.pallas import tpu as pltpu
from jax.sharding import PartitionSpec as P

HD = 64
NS_ITERS = 2
STEP = 10

poly_one = 3.4445
poly_three = -4.775
poly_five = 2.0315
momentum_decay = 0.95
muon_rate = 0.3
muon_decay = 0.01
adam_rate = 0.2
beta_one = 0.9
beta_two = 0.999
adam_epsilon = 1e-08
norm_epsilon = 1e-05
ortho_epsilon = 1e-07
masked_score = -1e30
PLANES = 4
LOW = jnp.bfloat16
WIDE = jnp.float32


def xor_trade(block, distance):
    count = lax.axis_size("dp")
    return lax.ppermute(block, "dp", [(i, i ^ distance) for i in range(count)])


def core_trade(block):
    return lax.ppermute(block, "fsdp", [(0, 1), (1, 0)])


def bit_of(rank, place):
    return (rank >> place) & 1


def pick(block, index, axis):
    return lax.dynamic_index_in_dim(block, index, axis, keepdims=False)


def pair(mine, other, bit, axis):
    first = jnp.where(bit == 0, mine, other)
    second = jnp.where(bit == 0, other, mine)
    return jnp.stack([first, second], axis)


def higher(places, place):
    return sum(1 for other in places if other > place)


def gather_relative(block, order, done):
    for index, place in enumerate(order):
        axis = higher(done + order[:index], place)
        block = jnp.stack([block, xor_trade(block, 1 << place)], axis)
    return block


def tie(*values):
    return lax.optimization_barrier(values)


def xor_order(block, rank, bits):
    tail = block.shape[1:]
    block = block.reshape((2,) * bits + tail)
    for place in range(bits):
        axis = bits - 1 - place
        block = jnp.where(bit_of(rank, place) == 0, block, jnp.flip(block, axis))
    return block.reshape((-1,) + tail)


def nt(left, right):
    return lax.dot_general(left, right, (((1,), (1,)), ((), ())), preferred_element_type=WIDE)


def nn(left, right):
    return lax.dot_general(left, right, (((1,), (0,)), ((), ())), preferred_element_type=WIDE)


def tn(left, right):
    return lax.dot_general(left, right, (((0,), (0,)), ((), ())), preferred_element_type=WIDE)


def run_kernel(body, results, operands, scratch=(), scalars=0, room=10):
    places = [pltpu.SMEM] * scalars + [pltpu.VMEM] * (len(operands) - scalars)
    return pl.pallas_call(
        body,
        out_shape=[jax.ShapeDtypeStruct(shape, kind) for shape, kind in results],
        in_specs=[pl.BlockSpec(memory_space=place) for place in places],
        out_specs=[pl.BlockSpec(memory_space=pltpu.VMEM)] * len(results),
        scratch_shapes=[pltpu.VMEM(shape, kind) for shape, kind in scratch],
        compiler_params=pltpu.CompilerParams(vmem_limit_bytes=room * 1024 * 1024),
        cost_estimate=pl.CostEstimate(flops=1000, bytes_accessed=1000, transcendentals=0),
    )(*operands)


def gate(values, *needed):
    anywhere = pl.BlockSpec(memory_space=pl.ANY)
    return pl.pallas_call(
        lambda *refs: None,
        out_shape=[jax.ShapeDtypeStruct(value.shape, value.dtype) for value in values],
        in_specs=[anywhere] * (len(values) + len(needed)),
        out_specs=[anywhere] * len(values),
        input_output_aliases={place: place for place in range(len(values))},
        compiler_params=pltpu.CompilerParams(vmem_limit_bytes=1024 * 1024),
        cost_estimate=pl.CostEstimate(flops=0, bytes_accessed=0, transcendentals=0),
    )(*values, *needed)


MARK = ((8, 128), WIDE)


def step_body(count, splits, *refs):
    kept, got = refs[:count], refs[count : 2 * count]
    results = list(refs[2 * count + 1 :])
    results.pop()[...] = jnp.zeros(MARK[0], WIDE)
    for kept_ref, got_ref in zip(kept, got):
        if splits:
            for half in range(2):
                part = kept_ref[:, half].astype(WIDE) + got_ref[:, half].astype(WIDE)
                result = results.pop(0)
                result[...] = part.astype(result.dtype)
        else:
            result = results.pop(0)
            result[...] = (kept_ref[...].astype(WIDE) + got_ref[...].astype(WIDE)).astype(result.dtype)


def summed(kept, got, mark, kind):
    results = [(part.shape, kind) for part in kept] + [MARK]
    body = functools.partial(step_body, len(kept), False)
    *totals, mark = run_kernel(body, results, (*kept, *got, mark))
    return totals, mark


def stepped(kept, got, mark, orders, tail):
    results, operands = [], []
    for part, order in zip(kept, orders):
        above = higher(order, order[0])
        shape = (2**above, 2 ** (len(order) - 1 - above)) + tail
        operands.append((shape[0], 2) + shape[1:])
        results += [(shape, WIDE), (shape, LOW)]
    body = functools.partial(step_body, len(kept), True)
    parts = [part.reshape(shape) for part, shape in zip((*kept, *got), operands * 2)]
    *halves, mark = run_kernel(body, results + [MARK], (*parts, mark))
    return halves[::2], halves[1::2], mark


def mean_of(values):
    return jnp.sum(values, axis=-1, keepdims=True) * (1.0 / values.shape[-1])


def normalized(values):
    center = values - mean_of(values)
    scale = lax.rsqrt(mean_of(center * center) + norm_epsilon)
    return center * scale, scale


def norm_back(grad, unit, scale, gain):
    inner = grad * gain
    return scale * (inner - mean_of(inner) - unit * mean_of(inner * unit))


def head_probs(query, keys, allowed):
    scores = nt(query, keys) * (HD ** (-0.5))
    scores = jnp.where(allowed, scores, masked_score)
    exp_scores = jnp.exp(scores - jnp.max(scores, axis=-1, keepdims=True))
    return exp_scores / jnp.sum(exp_scores, axis=-1, keepdims=True)


def head_parts(head, width, own_ref, other_ref):
    at = slice(head * HD, (head + 1) * HD)
    keys = jnp.concatenate([own_ref[:, width:][:, at], other_ref[:, :width][:, at]], axis=0)
    values = jnp.concatenate([own_ref[:, 2 * width :][:, at], other_ref[:, width:][:, at]], axis=0)
    return own_ref[:, at], keys, values


def segments(index_ref, lengths_ref, places):
    half = places.size // 2 if places.shape[0] == 1 else places.shape[0]
    places = jnp.where(index_ref[1] == 0, places, (places + half) & (2 * half - 1))
    result, bound = jnp.zeros(places.shape, jnp.int32), 0
    for entry in range(lengths_ref.shape[1]):
        bound = bound + lengths_ref[0, entry]
        result = result + jnp.where(places >= bound, 1, 0)
    return result


def own_segments(index_ref, lengths_ref, tok_rows):
    return segments(index_ref, lengths_ref, lax.broadcasted_iota(jnp.int32, (tok_rows, 1), 0))


def allowed_pairs(index_ref, lengths_ref, tok_rows):
    every = lax.broadcasted_iota(jnp.int32, (1, 2 * tok_rows), 1)
    return own_segments(index_ref, lengths_ref, tok_rows) == segments(index_ref, lengths_ref, every)


def attend_body(
    index_ref, lengths_ref, own_ref, other_ref, one_ref, two_ref, tokens_ref, vec_ref,
    context_ref, normed_ref, low_ref, unit_ref, scale_ref,
):
    width = tokens_ref.shape[1]
    side = width // 2
    allowed = allowed_pairs(index_ref, lengths_ref, tokens_ref.shape[0])
    for start in range(0, width // HD, 2):
        found = []
        for head in (start, start + 1):
            query, keys, values = head_parts(head, width, own_ref, other_ref)
            found.append(nn(head_probs(query, keys, allowed).astype(LOW), values))
        context_ref[:, start * HD : (start + 2) * HD] = jnp.concatenate(found, axis=1).astype(LOW)
    attended = (
        nt(context_ref[:, :side], one_ref[...])
        + nt(context_ref[:, side:], two_ref[...])
        + vec_ref[6:7, :]
    )
    unit, scale = normalized(tokens_ref[...].astype(WIDE) + attended)
    normed = unit * vec_ref[0:1, :] + vec_ref[1:2, :]
    normed_ref[...] = normed
    low_ref[...] = normed.astype(LOW)
    unit_ref[...] = unit
    scale_ref[...] = scale


def attend_back_body(
    index_ref, lengths_ref, d_normed_ref, own_ref, other_ref, one_ref, two_ref, unit_ref, scale_ref, vec_ref,
    resid_ref, attended_ref, query_ref, own_grad_ref, other_grad_ref, rows_ref,
):
    tok_rows, width = d_normed_ref.shape
    allowed = allowed_pairs(index_ref, lengths_ref, tok_rows)
    grad, unit = d_normed_ref[...], unit_ref[...]
    resid = norm_back(grad, unit, scale_ref[...], vec_ref[0:1, :])
    low = resid.astype(LOW)
    resid_ref[...] = resid
    attended_ref[...] = low
    rows_ref[0:1, :] = jnp.sum(grad * unit, axis=0, keepdims=True)
    rows_ref[1:2, :] = jnp.sum(grad, axis=0, keepdims=True)
    rows_ref[2:3, :] = jnp.sum(low.astype(WIDE), axis=0, keepdims=True)
    d_context = jnp.concatenate([nn(low, one_ref[...]), nn(low, two_ref[...])], axis=1).astype(LOW)
    factor = HD ** (-0.5)
    for start in range(0, width // HD, 2):
        found = []
        for head in (start, start + 1):
            query, keys, values = head_parts(head, width, own_ref, other_ref)
            grad_head = d_context[:, head * HD : (head + 1) * HD]
            probs = head_probs(query, keys, allowed)
            d_probs = nt(grad_head, values)
            inner = jnp.sum(probs * d_probs, axis=-1, keepdims=True)
            d_scores = (probs * (d_probs - inner)).astype(LOW)
            found.append(
                (nn(d_scores, keys) * factor, tn(d_scores, query) * factor,
                 tn(probs.astype(LOW), grad_head))
            )
        d_query, d_keys, d_values = [
            jnp.concatenate([first, second], axis=1) for first, second in zip(*found)
        ]
        at = slice(start * HD, (start + 2) * HD)
        shifted = slice(width + start * HD, width + (start + 2) * HD)
        query_ref[:, at] = d_query.astype(LOW)
        own_grad_ref[:, at] = d_keys[:tok_rows]
        own_grad_ref[:, shifted] = d_values[:tok_rows]
        other_grad_ref[:, at] = d_keys[tok_rows:].astype(LOW)
        other_grad_ref[:, shifted] = d_values[tok_rows:].astype(LOW)


def hidden_body(
    index_ref, lengths_ref, normed_ref, low_ref, cotangent_ref, vec_ref, bias_ref, *refs
):
    up, down = refs[:4], refs[4:8]
    output_ref, grad_ref, g_bias, rows_ref = refs[8:12]
    g_up, g_down = refs[12:16], refs[16:20]
    act_ref, slope_ref = refs[20:]
    low = low_ref[...]
    lowered = vec_ref[7:8, :] + jnp.zeros(normed_ref.shape, WIDE)
    blocks = [(core, high, lower) for core in range(2) for high in range(2) for lower in range(2)]
    for place, (core, high, lower) in enumerate(blocks):
        pre = nt(low, up[2 * core + lower][high]) + bias_ref[place : place + 1, :]
        cdf = 0.5 * (1.0 + lax.erf(pre * 0.7071067811865476))
        act = (pre * cdf).astype(LOW)
        act_ref[place] = act
        slope_ref[place] = cdf + pre * jnp.exp(-0.5 * pre * pre) * 0.3989422804014327
        lowered = lowered + nn(act, down[2 * core + high][lower])
    unit, scale = normalized(normed_ref[...] + lowered)
    output_ref[...] = (unit * vec_ref[2:3, :] + vec_ref[3:4, :]).astype(LOW)
    segment = own_segments(index_ref, lengths_ref, low.shape[0])
    live = jnp.where(segment < lengths_ref.shape[1], 1.0, 0.0)
    top = cotangent_ref[...].astype(WIDE) * live
    resid = norm_back(top, unit, scale, vec_ref[2:3, :])
    d_lowered = resid.astype(LOW)
    rows_ref[0:1, :] = jnp.sum(top * unit, axis=0, keepdims=True)
    rows_ref[1:2, :] = jnp.sum(top, axis=0, keepdims=True)
    rows_ref[2:3, :] = jnp.sum(d_lowered.astype(WIDE), axis=0, keepdims=True)
    total = resid
    for place, (core, high, lower) in enumerate(blocks):
        g_down[2 * core + high][lower] = tn(act_ref[place], d_lowered).astype(LOW)
        d_pre = (nt(d_lowered, down[2 * core + high][lower]) * slope_ref[place]).astype(LOW)
        g_bias[place : place + 1, :] = jnp.sum(d_pre.astype(WIDE), axis=0, keepdims=True)
        g_up[2 * core + lower][high] = tn(d_pre, low).astype(LOW)
        total = total + nn(d_pre, up[2 * core + lower][high])
    grad_ref[...] = total


def chunk_slot(rank, core, chunk, far):
    place = jnp.bitwise_xor(rank, chunk // 2)
    block = 4 * jnp.bitwise_xor(core, chunk % 2) + jnp.bitwise_and(place, 3)
    return far * block + lax.shift_right_logical(place, 2)


def unpack_body(
    index_ref, own_one, other_one, own_two, other_two, tokens_ref,
    projected_ref, qkv_one, qkv_two, out_one, out_two, vec_ref, bias_ref, chunk_ref,
):
    rank, core = index_ref[0], index_ref[1]
    count, rows, side = own_one.shape
    width = 2 * side
    qkv_cols = qkv_one.shape[0] // (2 * count)
    out_cols = out_one.shape[0] // (2 * count)
    split = qkv_cols + 8
    total = []
    for own, other, qkv, out in (
        (own_one, other_one, qkv_one, out_one), (own_two, other_two, qkv_two, out_two)
    ):
        vec = jnp.zeros((16, side), WIDE)
        for place in range(count):
            slot = jnp.bitwise_xor(rank, place)
            mine, theirs = own[slot].astype(WIDE), other[slot].astype(WIDE)
            first = jnp.where(core == 0, mine, theirs)
            second = jnp.where(core == 0, theirs, mine)
            both = jnp.concatenate([first[:qkv_cols], second[:qkv_cols]], axis=0)
            qkv[2 * qkv_cols * place : 2 * qkv_cols * (place + 1), :] = both.astype(LOW)
            both = [part[split : split + out_cols] for part in (first, second)]
            both = jnp.concatenate(both, axis=0)
            out[2 * out_cols * place : 2 * out_cols * (place + 1), :] = both.astype(LOW)
            vec = vec + jnp.concatenate(
                [mine[qkv_cols:split] + theirs[qkv_cols:split], mine[rows - 8 :] + theirs[rows - 8 :]],
                axis=0,
            )
        total.append(vec)
    vec = jnp.concatenate(total, axis=1)
    vec_ref[...] = vec
    far, cols = count // 4, chunk_ref.shape[1]
    per_row = width // cols
    for chunk in range(2 * count):
        at = slice((chunk % per_row) * cols, (chunk % per_row + 1) * cols)
        row = 8 + chunk // per_row
        chunk_ref[pl.ds(chunk_slot(rank, core, chunk, far), 1), :] = vec[row : row + 1, at]
    for block in range(8):
        parts = [chunk_ref[far * block + part : far * block + part + 1, :] for part in range(far)]
        bias_ref[block : block + 1, :] = jnp.concatenate(parts, axis=1)
    for part, bias in enumerate((vec[4:5], None, vec[5:6])):
        at = slice(part * width, (part + 1) * width)
        block = nt(tokens_ref[:, :side], qkv_one[at, :]) + nt(tokens_ref[:, side:], qkv_two[at, :])
        projected_ref[:, at] = (block if bias is None else block + bias).astype(LOW)


def pack_body(
    index_ref, query_ref, own_ref, got_ref, tokens_ref, attended_ref, context_ref,
    one_ref, two_ref, g_bias_ref,
    d_qkv_ref, kept_one, sent_one, kept_two, sent_two, wide_ref, out_ref, chunk_ref, rows_ref,
):
    rank, core = index_ref[0], index_ref[1]
    count, rows, side = kept_one.shape
    width = 2 * side
    qkv_cols = wide_ref.shape[0] // (2 * count)
    out_cols = out_ref.shape[0] // (2 * count)
    d_qkv_ref[:, :width] = query_ref[...]
    d_qkv_ref[:, width:] = (own_ref[...] + got_ref[...].astype(WIDE)).astype(LOW)
    far, cols = count // 4, chunk_ref.shape[1]
    for block in range(8):
        for part in range(far):
            at = slice(part * cols, (part + 1) * cols)
            chunk_ref[far * block + part : far * block + part + 1, :] = g_bias_ref[block : block + 1, at]
    rows_ref[...] = jnp.zeros(rows_ref.shape, WIDE)
    rows_ref[0:2, :] = one_ref[:2]
    rows_ref[2:4, :] = two_ref[:2]
    rows_ref[6:7, :] = one_ref[2:]
    rows_ref[7:8, :] = two_ref[2:]
    for part, row in ((0, 4), (2, 5)):
        block = slice(part * width, (part + 1) * width)
        rows_ref[row : row + 1, :] = jnp.sum(d_qkv_ref[:, block].astype(WIDE), axis=0, keepdims=True)
    per_row = width // cols
    for chunk in range(2 * count):
        at = slice((chunk % per_row) * cols, (chunk % per_row + 1) * cols)
        row = 8 + chunk // per_row
        rows_ref[row : row + 1, at] = chunk_ref[pl.ds(chunk_slot(rank, core, chunk, far), 1), :]
    for index, (kept, sent) in enumerate(((kept_one, sent_one), (kept_two, sent_two))):
        at = slice(index * side, (index + 1) * side)
        for part in range(3):
            block = slice(part * width, (part + 1) * width)
            wide_ref[block, :] = tn(d_qkv_ref[:, block], tokens_ref[:, at])
        out_ref[...] = tn(attended_ref[...], context_ref[:, at])
        low_rows = rows_ref[:8, at]
        high_rows = rows_ref[8:, at]
        for place in range(count):
            slot = jnp.bitwise_xor(rank, place)
            blocks = []
            for chunk in (2 * place, 2 * place + 1):
                blocks.append(
                    jnp.concatenate(
                        [
                            wide_ref[qkv_cols * chunk : qkv_cols * (chunk + 1), :],
                            low_rows,
                            out_ref[out_cols * chunk : out_cols * (chunk + 1), :],
                            high_rows,
                        ],
                        axis=0,
                    )
                )
            kept[slot] = jnp.where(core == 0, blocks[0], blocks[1]).astype(LOW)
            sent[slot] = jnp.where(core == 0, blocks[1], blocks[0]).astype(LOW)


def rows_by_cols(left, right):
    return jnp.einsum("td,fd->tf", left, right, preferred_element_type=WIDE)


def plain(left, right):
    return jnp.dot(left, right, preferred_element_type=WIDE)


def over_tokens(left, right):
    return jnp.einsum("ta,tb->ab", left, right, preferred_element_type=WIDE).astype(LOW)


def moment_body(index_ref, *refs):
    kept_one, kept_two, got_one, got_two, kept_up, kept_down, got_up, got_down = refs[:8]
    moments, pieces, grads, results = refs[8:12], refs[12:16], refs[16:20], refs[20:24]
    vec_ref, stack_ref = refs[24:]
    attn = jnp.concatenate(
        [kept_one[...] + got_one[...].astype(WIDE), kept_two[...] + got_two[...].astype(WIDE)], axis=1
    )
    qkv_cols, out_cols = moments[0].shape[0], moments[1].shape[0]
    split = qkv_cols + 8
    vec_ref[...] = jnp.concatenate([attn[qkv_cols:split], attn[split + out_cols :]], axis=0)
    sums = (
        attn[:qkv_cols],
        attn[split : split + out_cols],
        kept_up[...] + got_up[...].astype(WIDE),
        kept_down[...] + got_down[...].astype(WIDE),
    )
    for place, (moment, total, grad, result) in enumerate(zip(moments, sums, grads, results)):
        grad[...] = total
        updated = momentum_decay * moment[...] + total
        result[...] = updated
        missing = stack_ref.shape[1] - updated.shape[0]
        if missing:
            updated = jnp.concatenate([updated, jnp.zeros((missing, updated.shape[1]), WIDE)], axis=0)
        stack_ref[place] = updated.astype(LOW)
    plane = index_ref[2]
    for offset, piece in enumerate(pieces):
        piece[...] = stack_ref[jnp.bitwise_xor(plane, offset)]


def weight_update(weight, ortho, longest):
    return weight - muon_rate * (0.2 * math.sqrt(longest) * ortho + muon_decay * weight)


def update_body(sizes, index_ref, *refs):
    stack_ref = refs[-1]
    for offset in range(PLANES):
        stack_ref[offset] = refs[offset][...]
    for place, longest in enumerate(sizes):
        weight, result = refs[PLANES + place], refs[2 * PLANES + place]
        ortho = stack_ref[jnp.bitwise_xor(index_ref[2], place)].astype(WIDE)[: weight.shape[0]]
        result[...] = weight_update(weight[...], ortho, longest)


def gram_body(index_ref, *refs):
    rows, kept_ref, sent_ref = refs[:-2], refs[-2], refs[-1]
    gram = tn(rows[0][...], rows[0][...])
    for part in rows[1:]:
        gram = gram + tn(part[...], part[...])
    third = gram.shape[0] // 3
    first = gram[:third]
    second = jnp.concatenate([gram[third : 2 * third, third:], gram[2 * third :, 2 * third :]], axis=1)
    kept_ref[...] = jnp.where(index_ref[1] == 0, first, second)
    sent_ref[...] = jnp.where(index_ref[1] == 0, second, first).astype(LOW)


def share_body(kept_ref, got_ref, *results):
    half = kept_ref.shape[0] // 2
    for way in range(2):
        at = slice(way * half, (way + 1) * half)
        total = kept_ref[at, :] + got_ref[at, :].astype(WIDE)
        results[way][...] = total
        results[2 + way][...] = total.astype(LOW)


def add_body(*refs):
    for way in range(2):
        total = refs[way][...] + refs[2 + way][...].astype(WIDE)
        refs[4 + way][...] = total
        refs[6 + way][...] = total.astype(LOW)


def join_body(first, second, got_first, got_second, result):
    half = first.shape[0]
    result[:half, :] = (first[...] + got_first[...].astype(WIDE)).astype(LOW)
    result[half:, :] = (second[...] + got_second[...].astype(WIDE)).astype(LOW)


def orthogonal_body(index_ref, own_ref, other_ref, *refs):
    count = (len(refs) - 1) // 2
    rows, results, gram_ref = refs[:count], refs[count : 2 * count], refs[-1]
    third = own_ref.shape[0]
    own, other = own_ref[...].astype(WIDE), other_ref[...].astype(WIDE)
    first = jnp.where(index_ref[1] == 0, own, other)
    second = jnp.where(index_ref[1] == 0, other, own)
    gram_ref[:third, :] = first
    gram_ref[third : 2 * third, third:] = second[:, : 2 * third]
    gram_ref[2 * third :, 2 * third :] = second[:, 2 * third :]
    gram_ref[third : 2 * third, :third] = first[:, third : 2 * third].T
    gram_ref[2 * third :, :third] = first[:, 2 * third :].T
    gram_ref[2 * third :, third : 2 * third] = second[:, third : 2 * third].T
    trace = jnp.zeros((1, 1), WIDE)
    spot = lax.broadcasted_iota(jnp.int32, (third, third), 0)
    eye = spot == lax.broadcasted_iota(jnp.int32, (third, third), 1)
    for part in range(3):
        at = slice(part * third, (part + 1) * third)
        block = jnp.where(eye, gram_ref[at, at], 0.0)
        trace = trace + jnp.sum(jnp.sum(block, axis=1, keepdims=True), axis=0, keepdims=True)
    factor = 1.0 / (jnp.sqrt(trace) + ortho_epsilon)
    gram_mat = gram_ref[...] * (factor * factor)
    low_x = [part[...] for part in rows]
    current = [part.astype(WIDE) * factor for part in low_x]
    for iteration in range(NS_ITERS):
        low_gram = gram_mat.astype(LOW)
        low_mixing = (poly_three * gram_mat + poly_five * nn(low_gram, low_gram)).astype(LOW)
        scale = factor if iteration == 0 else 1.0
        current = [
            poly_one * part + nn(low, low_mixing) * scale for part, low in zip(current, low_x)
        ]
        low_x = [part.astype(LOW) for part in current]
        if iteration < NS_ITERS - 1:
            product = nn(low_mixing, low_gram)
            gram_mat = (
                (poly_one * poly_one) * gram_mat
                + (2.0 * poly_one) * product
                + nn(low_mixing, product.astype(LOW))
            )
    for result, part in zip(results, low_x):
        result[...] = part


def orthogonal(rows, index, low_bits):
    count, width = rows[0].shape
    third = width // 3
    kept, sent = run_kernel(
        gram_body, [((third, width), WIDE), ((third, width), LOW)], (index, *rows), scalars=1
    )
    half = (third // 2, width)
    both = [(half, WIDE)] * 2 + [(half, LOW)] * 2
    *parts, left, right = run_kernel(share_body, both, (kept, core_trade(sent)))
    for step in range(len(low_bits)):
        got = [
            xor_trade(part, 1 << low_bits[(step + way) % len(low_bits)])
            for way, part in enumerate((left, right))
        ]
        if step < len(low_bits) - 1:
            *parts, left, right = run_kernel(add_body, both, (*parts, *got))
    (own,) = run_kernel(join_body, [((third, width), LOW)], (*parts, *got))
    return run_kernel(
        orthogonal_body,
        [((count, width), LOW)] * len(rows),
        (index, own, core_trade(own), *rows),
        [((width, width), WIDE)],
        scalars=1,
        room=26,
    )


def per_device(
    tokens_in,
    cotangent,
    seq_lengths,
    w_qkv,
    w_out,
    w_up,
    w_down,
    vectors,
    mom_qkv,
    mom_out,
    mom_up,
    mom_down,
    adam_first,
    adam_second,
):
    tok_rows, width = tokens_in.shape
    side = width // 2
    dp_count = lax.axis_size("dp")
    bits = dp_count.bit_length() - 1
    rank, core = lax.axis_index("dp"), lax.axis_index("fsdp")
    up_order = list(range(bits))
    qkv_cols, out_cols, up_cols = w_qkv.shape[1], w_out.shape[1], w_up.shape[1]
    vec_rows, vec_cols = vectors.shape
    devices = 2 * dp_count

    masks = [(offset & 1) | (offset & 2) << 1 for offset in range(PLANES)]
    plane_bits = [place for place in range(bits) if place not in (0, 2)]
    plane = bit_of(rank, 0) + 2 * bit_of(rank, 2)
    index = jnp.stack([rank, core, plane]).astype(jnp.int32)
    first_col = (vec_cols * (2 * rank + core)).astype(jnp.uint32)
    top = jnp.uint32(0)
    vec_wide = lax.dynamic_update_slice(
        jnp.zeros((16, width), LOW), vectors.astype(LOW), (top, first_col)
    )
    split = -(-(qkv_cols + 8) // 16) * 16
    rows = split + -(-(out_cols + 8) // 16) * 16
    exact = qkv_cols % 8 == 0 and out_cols % 8 == 0 and split == qkv_cols + 8 and rows == split + out_cols + 8
    pack = jnp.concatenate(
        [
            jnp.pad(w_qkv.T.astype(LOW), ((0, split - 8 - qkv_cols), (0, 0))),
            vec_wide[:8],
            jnp.pad(w_out.T.astype(LOW), ((0, rows - split - 8 - out_cols), (0, 0))),
            vec_wide[8:],
        ],
        axis=0,
    )
    pack_one, pack_two = pack[:, :side], pack[:, side:]
    far = up_order[2:][::-1]
    near_one, near_two = [1, 0], [0, 1]
    all_one = gather_relative(pack_one, far, [])
    all_two = gather_relative(pack_two, far, [])
    hidden_low = (w_up.T.astype(LOW), w_down.astype(LOW))
    all_one, all_two, *hidden_low = tie(all_one, all_two, *hidden_low)
    all_one = gather_relative(all_one, near_one, far)
    all_two = gather_relative(all_two, near_two, far)
    hidden_far = [gather_relative(part, far, []).reshape(-1, width) for part in hidden_low]
    all_one, all_two, *hidden_far = tie(all_one, all_two, *hidden_far)
    hidden_near = [
        jnp.stack([part, xor_trade(part, 1 << near[0])])
        for part, near in zip(hidden_far, (near_one, near_two))
    ]
    own_packs = [part.reshape((dp_count, rows, side)) for part in (all_one, all_two)]
    other_packs = [core_trade(part) for part in own_packs]
    packs = (own_packs[0], other_packs[0], own_packs[1], other_packs[1])
    far_count = dp_count // 4
    hidden_rows = far_count * up_cols
    wide_side, out_side = (devices * qkv_cols, side), (devices * out_cols, side)
    if exact:
        projected_low, *sides, vec_full, up_bias = run_kernel(
            unpack_body,
            [((tok_rows, 3 * width), LOW), (wide_side, LOW), (wide_side, LOW)]
            + [(out_side, LOW), (out_side, LOW), ((16, width), WIDE), ((8, hidden_rows), WIDE)],
            (index, *packs, tokens_in),
            [((devices, up_cols), WIDE)],
            scalars=1,
            room=18,
        )
        qkv_sides, out_sides = sides[:2], sides[2:]
    else:
        natural = [
            xor_order(pair(own, other, core, 1), rank, bits).reshape(devices, rows, side)
            for own, other in zip(own_packs, other_packs)
        ]
        qkv_sides = [part[:, :qkv_cols].reshape(wide_side) for part in natural]
        out_sides = [part[:, split : split + out_cols].reshape(out_side) for part in natural]
        vec_full = jnp.concatenate(natural, axis=2).astype(WIDE)
        vec_full = jnp.concatenate([vec_full[:, split - 8 : split], vec_full[:, rows - 8 :]], axis=1)
        vec_full = jnp.sum(vec_full, axis=0)
        qkv_bias = jnp.concatenate([vec_full[4], jnp.zeros((width,), WIDE), vec_full[5]])
        projected = rows_by_cols(tokens_in[:, :side], qkv_sides[0])
        projected = projected + rows_by_cols(tokens_in[:, side:], qkv_sides[1])
        projected_low = (projected + qkv_bias).astype(LOW)
        up_bias = xor_order(vec_full[8:12].reshape(dp_count, 2, up_cols), rank, bits)
        up_bias = up_bias.reshape(far_count, 2, 2, 2, up_cols).transpose(3, 1, 2, 0, 4)
        up_bias = up_bias.reshape(2, 4, hidden_rows)
        up_bias = jnp.where(core == 0, up_bias, up_bias[::-1]).reshape(8, hidden_rows)
    own_kv = projected_low[:, width:]
    other_kv = core_trade(own_kv)
    square = (tok_rows, width)
    context_low, normed, normed_low, unit, scale = run_kernel(
        attend_body,
        [(square, LOW), (square, WIDE), (square, LOW), (square, WIDE), ((tok_rows, 1), WIDE)],
        (index, seq_lengths, projected_low, other_kv, *out_sides, tokens_in, vec_full),
        scalars=2,
    )
    hidden_got = [xor_trade(part, 1 << near[1]) for part, near in zip(hidden_near, (near_one, near_two))]
    hidden_got = gate(hidden_got, scale)
    pieces = []
    for part, got in zip(hidden_near, hidden_got):
        pieces += [part, got, core_trade(part), core_trade(got)]
    piece = hidden_near[0].shape
    output, d_normed, g_bias_up, rows_two, *grads = run_kernel(
        hidden_body,
        [(square, LOW), (square, WIDE), ((8, hidden_rows), WIDE), ((3, width), WIDE)]
        + [(piece, LOW)] * 8,
        (index, seq_lengths, normed, normed_low, cotangent, vec_full, up_bias, *pieces),
        [((8, tok_rows, hidden_rows), LOW), ((8, tok_rows, hidden_rows), WIDE)],
        room=18,
        scalars=2,
    )
    hidden_orders = (up_order, [1] + up_order[2:] + [0])
    hidden_left = [[bits] + up_order[2:], up_order[2:] + [bits]]
    mark = jnp.zeros(*MARK)
    hidden_sent, mark = summed(
        (grads[1], grads[5]), (core_trade(grads[3]), core_trade(grads[7])), mark, LOW
    )
    hidden_kept, _ = summed(
        (grads[0], grads[4]), (core_trade(grads[2]), core_trade(grads[6])), mark, WIDE
    )
    d_resid_one, d_attended, d_query, own_grad, other_grad, rows_one = run_kernel(
        attend_back_body,
        [(square, WIDE), (square, LOW), (square, LOW)]
        + [((tok_rows, 2 * width), WIDE), ((tok_rows, 2 * width), LOW), ((3, width), WIDE)],
        (index, seq_lengths, d_normed, projected_low, other_kv, *out_sides, unit, scale, vec_full),
        scalars=2,
    )
    (other_grad,) = gate((other_grad,), mark)
    got_grad = core_trade(other_grad)
    if exact:
        block = ((dp_count, rows, side), LOW)
        d_qkv, *g_sides = run_kernel(
            pack_body,
            [((tok_rows, 3 * width), LOW), block, block, block, block],
            (index, d_query, own_grad, got_grad, tokens_in, d_attended, context_low)
            + (rows_one, rows_two, g_bias_up),
            [(wide_side, WIDE), (out_side, WIDE), ((devices, up_cols), WIDE), ((16, width), WIDE)],
            scalars=1,
            room=20,
        )
    else:
        d_kv = own_grad + got_grad.astype(WIDE)
        d_qkv = jnp.concatenate([d_query, d_kv.astype(LOW)], axis=1)
        sums = jnp.sum(d_qkv.astype(WIDE), axis=0, keepdims=True)
        g_bias_up = g_bias_up.reshape(2, 4, hidden_rows)
        g_bias_up = jnp.where(core == 0, g_bias_up, g_bias_up[::-1])
        g_bias_up = g_bias_up.reshape(2, 2, 2, far_count, up_cols).transpose(3, 1, 2, 0, 4)
        g_bias_up = xor_order(g_bias_up.reshape(dp_count, 2, up_cols), rank, bits)
        g_rows = [rows_one[:2], rows_two[:2], sums[:, :width], sums[:, 2 * width :]]
        g_rows += [rows_one[2:], rows_two[2:], g_bias_up.reshape(-1, width)]
        g_rows = jnp.concatenate(g_rows + [jnp.zeros((4, width), WIDE)], axis=0).astype(LOW)
        g_sides = []
        for part in range(2):
            at = slice(part * side, (part + 1) * side)
            whole = jnp.broadcast_to(g_rows[None, :, at], (devices, 16, side))
            g_qkv = over_tokens(d_qkv, tokens_in[:, at]).reshape(devices, qkv_cols, side)
            g_out = over_tokens(d_attended, context_low[:, at]).reshape(devices, out_cols, side)
            whole = jnp.concatenate(
                [
                    jnp.pad(g_qkv, ((0, 0), (0, split - 8 - qkv_cols), (0, 0))),
                    whole[:, :8],
                    jnp.pad(g_out, ((0, 0), (0, rows - split - 8 - out_cols), (0, 0))),
                    whole[:, 8:],
                ],
                axis=1,
            )
            whole = xor_order(whole.reshape(dp_count, 2, rows, side), rank, bits)
            g_sides += [pick(whole, core, 1), pick(whole, 1 - core, 1)]
    attn_orders = (up_order, [2, 0, 1] + up_order[3:])
    attn_kept = g_sides[::2]
    attn_got = [core_trade(part) for part in g_sides[1::2]]
    for step in range(bits):
        left = [order[step:] for order in attn_orders]
        attn_kept, attn_sent, mark = stepped(attn_kept, attn_got, mark, left, (rows, side))
        attn_got = [
            xor_trade(sent, 1 << order[step]) for sent, order in zip(attn_sent, attn_orders)
        ]
        got = [xor_trade(sent, 1 << order[step]) for sent, order in zip(hidden_sent, hidden_orders)]
        if step < bits - 1:
            left = [order[step:] for order in hidden_left]
            hidden_kept, hidden_sent, mark = stepped(hidden_kept, got, mark, left, (up_cols, width))
    last = [part.reshape(rows, side) for part in (*attn_kept, *attn_got)]
    last += [part.reshape(up_cols, width) for part in (*hidden_kept, *got)]
    d_tokens = d_resid_one + jnp.concatenate([plain(d_qkv, part) for part in qkv_sides], axis=1)

    piece_rows = max(qkv_cols, up_cols)
    moments = (mom_qkv.T, mom_out.T, mom_up.T, mom_down)
    if exact:
        shapes = [(moment.shape, WIDE) for moment in moments]
        results = run_kernel(
            moment_body,
            [((piece_rows, width), LOW)] * PLANES + shapes + shapes + [((16, width), WIDE)],
            (index, *last, *moments),
            [((PLANES, piece_rows, width), LOW)],
            scalars=1,
        )
        pieces = results[:PLANES]
        grads_t, moments_t = results[PLANES : 2 * PLANES], results[2 * PLANES : 3 * PLANES]
        vec_sums = results[-1]
    else:
        attn = [kept.astype(WIDE) + part.astype(WIDE) for kept, part in zip(last[:2], last[2:4])]
        attn = jnp.concatenate(attn, axis=1)
        grads_t = [attn[:qkv_cols], attn[split : split + out_cols]]
        grads_t += [kept + part.astype(WIDE) for kept, part in zip(last[4:6], last[6:8])]
        vec_sums = jnp.concatenate([attn[split - 8 : split], attn[rows - 8 :]], axis=0)
        moments_t = [momentum_decay * moment + grad for moment, grad in zip(moments, grads_t)]
        stacked = [
            jnp.pad(moment.astype(LOW), ((0, piece_rows - moment.shape[0]), (0, 0)))
            for moment in moments_t
        ]
        stacked = jnp.stack(stacked)
        pieces = [pick(stacked, plane ^ offset, 0) for offset in range(PLANES)]
    grad_qkv_t, grad_out_t, grad_up_t, grad_down = grads_t
    grad_vectors = lax.dynamic_slice(vec_sums, (top, first_col), (vec_rows, vec_cols))
    new_mom_qkv, new_mom_out, new_mom_up = [moment.T for moment in moments_t[:3]]
    new_mom_down = moments_t[3]
    mine = [pieces[0]]
    for offset in range(1, PLANES):
        mine.append(xor_trade(pieces[offset], masks[offset]))
    turned = orthogonal(mine, index, plane_bits)
    back = [turned[0]]
    for offset in range(1, PLANES):
        back.append(xor_trade(turned[offset], masks[offset]))
    hidden = up_cols * devices
    sizes = (3 * width, width, max(width, hidden), max(width, hidden))
    weights = (w_qkv.T, w_out.T, w_up.T, w_down)
    if exact:
        new_weights = run_kernel(
            functools.partial(update_body, sizes),
            [(weight.shape, WIDE) for weight in weights],
            (index, *back, *weights),
            [((PLANES, piece_rows, width), LOW)],
            scalars=1,
        )
    else:
        back = jnp.stack(back)
        new_weights = [
            weight_update(weight, pick(back, plane ^ place, 0)[: weight.shape[0]].astype(WIDE), longest)
            for place, (weight, longest) in enumerate(zip(weights, sizes))
        ]
    new_w_qkv, new_w_out, new_w_up = [weight.T for weight in new_weights[:3]]
    new_w_down = new_weights[3]

    new_first = beta_one * adam_first + (1.0 - beta_one) * grad_vectors
    new_second = beta_two * adam_second + (1.0 - beta_two) * grad_vectors * grad_vectors
    first_hat = new_first / (1.0 - beta_one**STEP)
    second_hat = new_second / (1.0 - beta_two**STEP)
    new_vectors = vectors - adam_rate * first_hat / (jnp.sqrt(second_hat) + adam_epsilon)
    return (
        output,
        d_tokens,
        grad_qkv_t.T,
        grad_out_t.T,
        grad_up_t.T,
        grad_down,
        grad_vectors,
        new_mom_qkv,
        new_mom_out,
        new_mom_up,
        new_mom_down,
        new_w_qkv,
        new_w_out,
        new_w_up,
        new_w_down,
        new_first,
        new_second,
        new_vectors,
    )


def solution(mesh):
    in_specs = (
        P(("dp", "fsdp"), None),
        P(("dp", "fsdp"), None),
        P("dp", None),
        P(None, ("dp", "fsdp")),
        P(None, ("dp", "fsdp")),
        P(None, ("dp", "fsdp")),
        P(("dp", "fsdp"), None),
        P(None, ("dp", "fsdp")),
        P(None, ("dp", "fsdp")),
        P(None, ("dp", "fsdp")),
        P(None, ("dp", "fsdp")),
        P(("dp", "fsdp"), None),
        P(None, ("dp", "fsdp")),
        P(None, ("dp", "fsdp")),
    )
    out_specs = (
        P(("dp", "fsdp"), None),
        P(("dp", "fsdp"), None),
        P(None, ("dp", "fsdp")),
        P(None, ("dp", "fsdp")),
        P(None, ("dp", "fsdp")),
        P(("dp", "fsdp"), None),
        P(None, ("dp", "fsdp")),
        P(None, ("dp", "fsdp")),
        P(None, ("dp", "fsdp")),
        P(None, ("dp", "fsdp")),
        P(("dp", "fsdp"), None),
        P(None, ("dp", "fsdp")),
        P(None, ("dp", "fsdp")),
        P(None, ("dp", "fsdp")),
        P(("dp", "fsdp"), None),
        P(None, ("dp", "fsdp")),
        P(None, ("dp", "fsdp")),
        P(None, ("dp", "fsdp")),
    )
    return jax.shard_map(
        per_device, mesh=mesh, in_specs=in_specs, out_specs=out_specs, check_vma=False
    )
```

```python
import functools
import math

import jax
import jax.numpy as jnp
from jax import lax
from jax.experimental import pallas as pl
from jax.experimental.pallas import tpu as pltpu
from jax.sharding import PartitionSpec as P

HD = 64
NS_ITERS = 2
STEP = 10

poly_one = 3.4445
poly_three = -4.775
poly_five = 2.0315
momentum_decay = 0.95
muon_rate = 0.3
muon_decay = 0.01
adam_rate = 0.2
beta_one = 0.9
beta_two = 0.999
adam_epsilon = 1e-08
norm_epsilon = 1e-05
ortho_epsilon = 1e-07
masked_score = -1e30
PLANES = 4
LOW = jnp.bfloat16
WIDE = jnp.float32


def xor_trade(block, distance):
    count = lax.axis_size("dp")
    return lax.ppermute(block, "dp", [(i, i ^ distance) for i in range(count)])


def core_trade(block):
    return lax.ppermute(block, "fsdp", [(0, 1), (1, 0)])


def bit_of(rank, place):
    return (rank >> place) & 1


def pick(block, index, axis):
    return lax.dynamic_index_in_dim(block, index, axis, keepdims=False)


def pair(mine, other, bit, axis):
    first = jnp.where(bit == 0, mine, other)
    second = jnp.where(bit == 0, other, mine)
    return jnp.stack([first, second], axis)


def higher(places, place):
    return sum(1 for other in places if other > place)


def gather_relative(block, order, done):
    for index, place in enumerate(order):
        axis = higher(done + order[:index], place)
        block = jnp.stack([block, xor_trade(block, 1 << place)], axis)
    return block


def tie(*values):
    return lax.optimization_barrier(values)


def xor_order(block, rank, bits):
    tail = block.shape[1:]
    block = block.reshape((2,) * bits + tail)
    for place in range(bits):
        axis = bits - 1 - place
        block = jnp.where(bit_of(rank, place) == 0, block, jnp.flip(block, axis))
    return block.reshape((-1,) + tail)


def nt(left, right):
    return lax.dot_general(left, right, (((1,), (1,)), ((), ())), preferred_element_type=WIDE)


def nn(left, right):
    return lax.dot_general(left, right, (((1,), (0,)), ((), ())), preferred_element_type=WIDE)


def tn(left, right):
    return lax.dot_general(left, right, (((0,), (0,)), ((), ())), preferred_element_type=WIDE)


def run_kernel(body, results, operands, scratch=(), scalars=0, room=10):
    places = [pltpu.SMEM] * scalars + [pltpu.VMEM] * (len(operands) - scalars)
    return pl.pallas_call(
        body,
        out_shape=[jax.ShapeDtypeStruct(shape, kind) for shape, kind in results],
        in_specs=[pl.BlockSpec(memory_space=place) for place in places],
        out_specs=[pl.BlockSpec(memory_space=pltpu.VMEM)] * len(results),
        scratch_shapes=[pltpu.VMEM(shape, kind) for shape, kind in scratch],
        compiler_params=pltpu.CompilerParams(vmem_limit_bytes=room * 1024 * 1024),
        cost_estimate=pl.CostEstimate(flops=1000, bytes_accessed=1000, transcendentals=0),
    )(*operands)


def gate(values, *needed):
    anywhere = pl.BlockSpec(memory_space=pl.ANY)
    return pl.pallas_call(
        lambda *refs: None,
        out_shape=[jax.ShapeDtypeStruct(value.shape, value.dtype) for value in values],
        in_specs=[anywhere] * (len(values) + len(needed)),
        out_specs=[anywhere] * len(values),
        input_output_aliases={place: place for place in range(len(values))},
        compiler_params=pltpu.CompilerParams(vmem_limit_bytes=1024 * 1024),
        cost_estimate=pl.CostEstimate(flops=0, bytes_accessed=0, transcendentals=0),
    )(*values, *needed)


MARK = ((8, 128), WIDE)


def step_body(count, splits, *refs):
    kept, got = refs[:count], refs[count : 2 * count]
    results = list(refs[2 * count + 1 :])
    results.pop()[...] = jnp.zeros(MARK[0], WIDE)
    for kept_ref, got_ref in zip(kept, got):
        if splits:
            for half in range(2):
                part = kept_ref[:, half].astype(WIDE) + got_ref[:, half].astype(WIDE)
                result = results.pop(0)
                result[...] = part.astype(result.dtype)
        else:
            result = results.pop(0)
            result[...] = (kept_ref[...].astype(WIDE) + got_ref[...].astype(WIDE)).astype(result.dtype)


def summed(kept, got, mark, kind):
    results = [(part.shape, kind) for part in kept] + [MARK]
    body = functools.partial(step_body, len(kept), False)
    *totals, mark = run_kernel(body, results, (*kept, *got, mark))
    return totals, mark


def stepped(kept, got, mark, orders, tail):
    results, operands = [], []
    for part, order in zip(kept, orders):
        above = higher(order, order[0])
        shape = (2**above, 2 ** (len(order) - 1 - above)) + tail
        operands.append((shape[0], 2) + shape[1:])
        results += [(shape, WIDE), (shape, LOW)]
    body = functools.partial(step_body, len(kept), True)
    parts = [part.reshape(shape) for part, shape in zip((*kept, *got), operands * 2)]
    *halves, mark = run_kernel(body, results + [MARK], (*parts, mark))
    return halves[::2], halves[1::2], mark


def mean_of(values):
    return jnp.sum(values, axis=-1, keepdims=True) * (1.0 / values.shape[-1])


def normalized(values):
    center = values - mean_of(values)
    scale = lax.rsqrt(mean_of(center * center) + norm_epsilon)
    return center * scale, scale


def norm_back(grad, unit, scale, gain):
    inner = grad * gain
    return scale * (inner - mean_of(inner) - unit * mean_of(inner * unit))


def head_probs(query, keys, allowed):
    scores = nt(query, keys) * (HD ** (-0.5))
    scores = jnp.where(allowed, scores, masked_score)
    exp_scores = jnp.exp(scores - jnp.max(scores, axis=-1, keepdims=True))
    return exp_scores / jnp.sum(exp_scores, axis=-1, keepdims=True)


def head_parts(head, width, own_ref, other_ref):
    at = slice(head * HD, (head + 1) * HD)
    keys = jnp.concatenate([own_ref[:, width:][:, at], other_ref[:, :width][:, at]], axis=0)
    values = jnp.concatenate([own_ref[:, 2 * width :][:, at], other_ref[:, width:][:, at]], axis=0)
    return own_ref[:, at], keys, values


def segments(index_ref, lengths_ref, places):
    half = places.size // 2 if places.shape[0] == 1 else places.shape[0]
    places = jnp.where(index_ref[1] == 0, places, (places + half) & (2 * half - 1))
    result, bound = jnp.zeros(places.shape, jnp.int32), 0
    for entry in range(lengths_ref.shape[1]):
        bound = bound + lengths_ref[0, entry]
        result = result + jnp.where(places >= bound, 1, 0)
    return result


def own_segments(index_ref, lengths_ref, tok_rows):
    return segments(index_ref, lengths_ref, lax.broadcasted_iota(jnp.int32, (tok_rows, 1), 0))


def allowed_pairs(index_ref, lengths_ref, tok_rows):
    every = lax.broadcasted_iota(jnp.int32, (1, 2 * tok_rows), 1)
    return own_segments(index_ref, lengths_ref, tok_rows) == segments(index_ref, lengths_ref, every)


def attend_body(
    index_ref, lengths_ref, own_ref, other_ref, one_ref, two_ref, tokens_ref, vec_ref,
    context_ref, normed_ref, low_ref, unit_ref, scale_ref, probs_ref,
):
    width = tokens_ref.shape[1]
    side = width // 2
    allowed = allowed_pairs(index_ref, lengths_ref, tokens_ref.shape[0])
    for start in range(0, width // HD, 2):
        found = []
        for head in (start, start + 1):
            query, keys, values = head_parts(head, width, own_ref, other_ref)
            probs = head_probs(query, keys, allowed)
            probs_ref[head] = probs
            found.append(nn(probs.astype(LOW), values))
        context_ref[:, start * HD : (start + 2) * HD] = jnp.concatenate(found, axis=1).astype(LOW)
    attended = (
        nt(context_ref[:, :side], one_ref[...])
        + nt(context_ref[:, side:], two_ref[...])
        + vec_ref[6:7, :]
    )
    unit, scale = normalized(tokens_ref[...].astype(WIDE) + attended)
    normed = unit * vec_ref[0:1, :] + vec_ref[1:2, :]
    normed_ref[...] = normed
    low_ref[...] = normed.astype(LOW)
    unit_ref[...] = unit
    scale_ref[...] = scale


def attend_back_body(
    d_normed_ref, own_ref, other_ref, probs_ref, one_ref, two_ref, unit_ref, scale_ref, vec_ref,
    resid_ref, attended_ref, query_ref, own_grad_ref, other_grad_ref, rows_ref,
):
    tok_rows, width = d_normed_ref.shape
    grad, unit = d_normed_ref[...], unit_ref[...]
    resid = norm_back(grad, unit, scale_ref[...], vec_ref[0:1, :])
    low = resid.astype(LOW)
    resid_ref[...] = resid
    attended_ref[...] = low
    rows_ref[0:1, :] = jnp.sum(grad * unit, axis=0, keepdims=True)
    rows_ref[1:2, :] = jnp.sum(grad, axis=0, keepdims=True)
    rows_ref[2:3, :] = jnp.sum(low.astype(WIDE), axis=0, keepdims=True)
    d_context = jnp.concatenate([nn(low, one_ref[...]), nn(low, two_ref[...])], axis=1).astype(LOW)
    factor = HD ** (-0.5)
    for start in range(0, width // HD, 2):
        found = []
        for head in (start, start + 1):
            query, keys, values = head_parts(head, width, own_ref, other_ref)
            grad_head = d_context[:, head * HD : (head + 1) * HD]
            probs = probs_ref[head]
            d_probs = nt(grad_head, values)
            inner = jnp.sum(probs * d_probs, axis=-1, keepdims=True)
            d_scores = (probs * (d_probs - inner)).astype(LOW)
            found.append(
                (nn(d_scores, keys) * factor, tn(d_scores, query) * factor,
                 tn(probs.astype(LOW), grad_head))
            )
        d_query, d_keys, d_values = [
            jnp.concatenate([first, second], axis=1) for first, second in zip(*found)
        ]
        at = slice(start * HD, (start + 2) * HD)
        shifted = slice(width + start * HD, width + (start + 2) * HD)
        query_ref[:, at] = d_query.astype(LOW)
        own_grad_ref[:, at] = d_keys[:tok_rows]
        own_grad_ref[:, shifted] = d_values[:tok_rows]
        other_grad_ref[:, at] = d_keys[tok_rows:].astype(LOW)
        other_grad_ref[:, shifted] = d_values[tok_rows:].astype(LOW)


def hidden_body(
    index_ref, lengths_ref, normed_ref, low_ref, cotangent_ref, vec_ref, bias_ref, *refs
):
    up, down = refs[:4], refs[4:8]
    output_ref, grad_ref, g_bias, rows_ref = refs[8:12]
    g_up, g_down = refs[12:16], refs[16:20]
    act_ref, slope_ref = refs[20:]
    low = low_ref[...]
    lowered = vec_ref[7:8, :] + jnp.zeros(normed_ref.shape, WIDE)
    blocks = [(core, high, lower) for core in range(2) for high in range(2) for lower in range(2)]
    for place, (core, high, lower) in enumerate(blocks):
        pre = nt(low, up[2 * core + lower][high]) + bias_ref[place : place + 1, :]
        cdf = 0.5 * (1.0 + lax.erf(pre * 0.7071067811865476))
        act = (pre * cdf).astype(LOW)
        act_ref[place] = act
        slope_ref[place] = cdf + pre * jnp.exp(-0.5 * pre * pre) * 0.3989422804014327
        lowered = lowered + nn(act, down[2 * core + high][lower])
    unit, scale = normalized(normed_ref[...] + lowered)
    output_ref[...] = (unit * vec_ref[2:3, :] + vec_ref[3:4, :]).astype(LOW)
    segment = own_segments(index_ref, lengths_ref, low.shape[0])
    live = jnp.where(segment < lengths_ref.shape[1], 1.0, 0.0)
    top = cotangent_ref[...].astype(WIDE) * live
    resid = norm_back(top, unit, scale, vec_ref[2:3, :])
    d_lowered = resid.astype(LOW)
    rows_ref[0:1, :] = jnp.sum(top * unit, axis=0, keepdims=True)
    rows_ref[1:2, :] = jnp.sum(top, axis=0, keepdims=True)
    rows_ref[2:3, :] = jnp.sum(d_lowered.astype(WIDE), axis=0, keepdims=True)
    total = resid
    for place, (core, high, lower) in enumerate(blocks):
        g_down[2 * core + high][lower] = tn(act_ref[place], d_lowered).astype(LOW)
        d_pre = (nt(d_lowered, down[2 * core + high][lower]) * slope_ref[place]).astype(LOW)
        g_bias[place : place + 1, :] = jnp.sum(d_pre.astype(WIDE), axis=0, keepdims=True)
        g_up[2 * core + lower][high] = tn(d_pre, low).astype(LOW)
        total = total + nn(d_pre, up[2 * core + lower][high])
    grad_ref[...] = total


def chunk_slot(rank, core, chunk, far):
    place = jnp.bitwise_xor(rank, chunk // 2)
    block = 4 * jnp.bitwise_xor(core, chunk % 2) + jnp.bitwise_and(place, 3)
    return far * block + lax.shift_right_logical(place, 2)


def unpack_body(
    index_ref, own_one, other_one, own_two, other_two, tokens_ref,
    projected_ref, qkv_one, qkv_two, out_one, out_two, vec_ref, bias_ref, chunk_ref,
):
    rank, core = index_ref[0], index_ref[1]
    count, rows, side = own_one.shape
    width = 2 * side
    qkv_cols = qkv_one.shape[0] // (2 * count)
    out_cols = out_one.shape[0] // (2 * count)
    split = qkv_cols + 8
    total = []
    for own, other, qkv, out in (
        (own_one, other_one, qkv_one, out_one), (own_two, other_two, qkv_two, out_two)
    ):
        vec = jnp.zeros((16, side), WIDE)
        for place in range(count):
            slot = jnp.bitwise_xor(rank, place)
            mine, theirs = own[slot].astype(WIDE), other[slot].astype(WIDE)
            first = jnp.where(core == 0, mine, theirs)
            second = jnp.where(core == 0, theirs, mine)
            both = jnp.concatenate([first[:qkv_cols], second[:qkv_cols]], axis=0)
            qkv[2 * qkv_cols * place : 2 * qkv_cols * (place + 1), :] = both.astype(LOW)
            both = [part[split : split + out_cols] for part in (first, second)]
            both = jnp.concatenate(both, axis=0)
            out[2 * out_cols * place : 2 * out_cols * (place + 1), :] = both.astype(LOW)
            vec = vec + jnp.concatenate(
                [mine[qkv_cols:split] + theirs[qkv_cols:split], mine[rows - 8 :] + theirs[rows - 8 :]],
                axis=0,
            )
        total.append(vec)
    vec = jnp.concatenate(total, axis=1)
    vec_ref[...] = vec
    far, cols = count // 4, chunk_ref.shape[1]
    per_row = width // cols
    for chunk in range(2 * count):
        at = slice((chunk % per_row) * cols, (chunk % per_row + 1) * cols)
        row = 8 + chunk // per_row
        chunk_ref[pl.ds(chunk_slot(rank, core, chunk, far), 1), :] = vec[row : row + 1, at]
    for block in range(8):
        parts = [chunk_ref[far * block + part : far * block + part + 1, :] for part in range(far)]
        bias_ref[block : block + 1, :] = jnp.concatenate(parts, axis=1)
    for part, bias in enumerate((vec[4:5], None, vec[5:6])):
        at = slice(part * width, (part + 1) * width)
        block = nt(tokens_ref[:, :side], qkv_one[at, :]) + nt(tokens_ref[:, side:], qkv_two[at, :])
        projected_ref[:, at] = (block if bias is None else block + bias).astype(LOW)


def pack_body(
    index_ref, query_ref, own_ref, got_ref, tokens_ref, attended_ref, context_ref,
    one_ref, two_ref, g_bias_ref,
    d_qkv_ref, kept_one, sent_one, kept_two, sent_two, wide_ref, out_ref, chunk_ref, rows_ref,
):
    rank, core = index_ref[0], index_ref[1]
    count, rows, side = kept_one.shape
    width = 2 * side
    qkv_cols = wide_ref.shape[0] // (2 * count)
    out_cols = out_ref.shape[0] // (2 * count)
    d_qkv_ref[:, :width] = query_ref[...]
    d_qkv_ref[:, width:] = (own_ref[...] + got_ref[...].astype(WIDE)).astype(LOW)
    far, cols = count // 4, chunk_ref.shape[1]
    for block in range(8):
        for part in range(far):
            at = slice(part * cols, (part + 1) * cols)
            chunk_ref[far * block + part : far * block + part + 1, :] = g_bias_ref[block : block + 1, at]
    rows_ref[...] = jnp.zeros(rows_ref.shape, WIDE)
    rows_ref[0:2, :] = one_ref[:2]
    rows_ref[2:4, :] = two_ref[:2]
    rows_ref[6:7, :] = one_ref[2:]
    rows_ref[7:8, :] = two_ref[2:]
    for part, row in ((0, 4), (2, 5)):
        block = slice(part * width, (part + 1) * width)
        rows_ref[row : row + 1, :] = jnp.sum(d_qkv_ref[:, block].astype(WIDE), axis=0, keepdims=True)
    per_row = width // cols
    for chunk in range(2 * count):
        at = slice((chunk % per_row) * cols, (chunk % per_row + 1) * cols)
        row = 8 + chunk // per_row
        rows_ref[row : row + 1, at] = chunk_ref[pl.ds(chunk_slot(rank, core, chunk, far), 1), :]
    for index, (kept, sent) in enumerate(((kept_one, sent_one), (kept_two, sent_two))):
        at = slice(index * side, (index + 1) * side)
        for part in range(3):
            block = slice(part * width, (part + 1) * width)
            wide_ref[block, :] = tn(d_qkv_ref[:, block], tokens_ref[:, at])
        out_ref[...] = tn(attended_ref[...], context_ref[:, at])
        low_rows = rows_ref[:8, at]
        high_rows = rows_ref[8:, at]
        for place in range(count):
            slot = jnp.bitwise_xor(rank, place)
            blocks = []
            for chunk in (2 * place, 2 * place + 1):
                blocks.append(
                    jnp.concatenate(
                        [
                            wide_ref[qkv_cols * chunk : qkv_cols * (chunk + 1), :],
                            low_rows,
                            out_ref[out_cols * chunk : out_cols * (chunk + 1), :],
                            high_rows,
                        ],
                        axis=0,
                    )
                )
            kept[slot] = jnp.where(core == 0, blocks[0], blocks[1]).astype(LOW)
            sent[slot] = jnp.where(core == 0, blocks[1], blocks[0]).astype(LOW)


def rows_by_cols(left, right):
    return jnp.einsum("td,fd->tf", left, right, preferred_element_type=WIDE)


def plain(left, right):
    return jnp.dot(left, right, preferred_element_type=WIDE)


def over_tokens(left, right):
    return jnp.einsum("ta,tb->ab", left, right, preferred_element_type=WIDE).astype(LOW)


def moment_body(index_ref, *refs):
    kept_one, kept_two, got_one, got_two, kept_up, kept_down, got_up, got_down = refs[:8]
    moments, pieces, grads, results = refs[8:12], refs[12:16], refs[16:20], refs[20:24]
    vec_ref, stack_ref = refs[24:]
    attn = jnp.concatenate(
        [kept_one[...] + got_one[...].astype(WIDE), kept_two[...] + got_two[...].astype(WIDE)], axis=1
    )
    qkv_cols, out_cols = moments[0].shape[0], moments[1].shape[0]
    split = qkv_cols + 8
    vec_ref[...] = jnp.concatenate([attn[qkv_cols:split], attn[split + out_cols :]], axis=0)
    sums = (
        attn[:qkv_cols],
        attn[split : split + out_cols],
        kept_up[...] + got_up[...].astype(WIDE),
        kept_down[...] + got_down[...].astype(WIDE),
    )
    for place, (moment, total, grad, result) in enumerate(zip(moments, sums, grads, results)):
        grad[...] = total
        updated = momentum_decay * moment[...] + total
        result[...] = updated
        missing = stack_ref.shape[1] - updated.shape[0]
        if missing:
            updated = jnp.concatenate([updated, jnp.zeros((missing, updated.shape[1]), WIDE)], axis=0)
        stack_ref[place] = updated.astype(LOW)
    plane = index_ref[2]
    for offset, piece in enumerate(pieces):
        piece[...] = stack_ref[jnp.bitwise_xor(plane, offset)]


def weight_update(weight, ortho, longest):
    return weight - muon_rate * (0.2 * math.sqrt(longest) * ortho + muon_decay * weight)


def update_body(sizes, index_ref, *refs):
    stack_ref = refs[-1]
    for offset in range(PLANES):
        stack_ref[offset] = refs[offset][...]
    for place, longest in enumerate(sizes):
        weight, result = refs[PLANES + place], refs[2 * PLANES + place]
        ortho = stack_ref[jnp.bitwise_xor(index_ref[2], place)].astype(WIDE)[: weight.shape[0]]
        result[...] = weight_update(weight[...], ortho, longest)


def gram_body(index_ref, *refs):
    rows, kept_ref, sent_ref = refs[:-2], refs[-2], refs[-1]
    gram = tn(rows[0][...], rows[0][...])
    for part in rows[1:]:
        gram = gram + tn(part[...], part[...])
    third = gram.shape[0] // 3
    first = gram[:third]
    second = jnp.concatenate([gram[third : 2 * third, third:], gram[2 * third :, 2 * third :]], axis=1)
    kept_ref[...] = jnp.where(index_ref[1] == 0, first, second)
    sent_ref[...] = jnp.where(index_ref[1] == 0, second, first).astype(LOW)


def share_body(kept_ref, got_ref, *results):
    half = kept_ref.shape[0] // 2
    for way in range(2):
        at = slice(way * half, (way + 1) * half)
        total = kept_ref[at, :] + got_ref[at, :].astype(WIDE)
        results[way][...] = total
        results[2 + way][...] = total.astype(LOW)


def add_body(*refs):
    for way in range(2):
        total = refs[way][...] + refs[2 + way][...].astype(WIDE)
        refs[4 + way][...] = total
        refs[6 + way][...] = total.astype(LOW)


def join_body(first, second, got_first, got_second, result):
    half = first.shape[0]
    result[:half, :] = (first[...] + got_first[...].astype(WIDE)).astype(LOW)
    result[half:, :] = (second[...] + got_second[...].astype(WIDE)).astype(LOW)


def orthogonal_body(index_ref, own_ref, other_ref, *refs):
    count = (len(refs) - 1) // 2
    rows, results, gram_ref = refs[:count], refs[count : 2 * count], refs[-1]
    third = own_ref.shape[0]
    own, other = own_ref[...].astype(WIDE), other_ref[...].astype(WIDE)
    first = jnp.where(index_ref[1] == 0, own, other)
    second = jnp.where(index_ref[1] == 0, other, own)
    gram_ref[:third, :] = first
    gram_ref[third : 2 * third, third:] = second[:, : 2 * third]
    gram_ref[2 * third :, 2 * third :] = second[:, 2 * third :]
    gram_ref[third : 2 * third, :third] = first[:, third : 2 * third].T
    gram_ref[2 * third :, :third] = first[:, 2 * third :].T
    gram_ref[2 * third :, third : 2 * third] = second[:, third : 2 * third].T
    trace = jnp.zeros((1, 1), WIDE)
    spot = lax.broadcasted_iota(jnp.int32, (third, third), 0)
    eye = spot == lax.broadcasted_iota(jnp.int32, (third, third), 1)
    for part in range(3):
        at = slice(part * third, (part + 1) * third)
        block = jnp.where(eye, gram_ref[at, at], 0.0)
        trace = trace + jnp.sum(jnp.sum(block, axis=1, keepdims=True), axis=0, keepdims=True)
    factor = 1.0 / (jnp.sqrt(trace) + ortho_epsilon)
    gram_mat = gram_ref[...] * (factor * factor)
    low_x = [part[...] for part in rows]
    current = [part.astype(WIDE) * factor for part in low_x]
    for iteration in range(NS_ITERS):
        low_gram = gram_mat.astype(LOW)
        low_mixing = (poly_three * gram_mat + poly_five * nn(low_gram, low_gram)).astype(LOW)
        scale = factor if iteration == 0 else 1.0
        current = [
            poly_one * part + nn(low, low_mixing) * scale for part, low in zip(current, low_x)
        ]
        low_x = [part.astype(LOW) for part in current]
        if iteration < NS_ITERS - 1:
            product = nn(low_mixing, low_gram)
            gram_mat = (
                (poly_one * poly_one) * gram_mat
                + (2.0 * poly_one) * product
                + nn(low_mixing, product.astype(LOW))
            )
    for result, part in zip(results, low_x):
        result[...] = part


def orthogonal(rows, index, low_bits):
    count, width = rows[0].shape
    third = width // 3
    kept, sent = run_kernel(
        gram_body, [((third, width), WIDE), ((third, width), LOW)], (index, *rows), scalars=1
    )
    half = (third // 2, width)
    both = [(half, WIDE)] * 2 + [(half, LOW)] * 2
    *parts, left, right = run_kernel(share_body, both, (kept, core_trade(sent)))
    for step in range(len(low_bits)):
        got = [
            xor_trade(part, 1 << low_bits[(step + way) % len(low_bits)])
            for way, part in enumerate((left, right))
        ]
        if step < len(low_bits) - 1:
            *parts, left, right = run_kernel(add_body, both, (*parts, *got))
    (own,) = run_kernel(join_body, [((third, width), LOW)], (*parts, *got))
    return run_kernel(
        orthogonal_body,
        [((count, width), LOW)] * len(rows),
        (index, own, core_trade(own), *rows),
        [((width, width), WIDE)],
        scalars=1,
        room=26,
    )


def per_device(
    tokens_in,
    cotangent,
    seq_lengths,
    w_qkv,
    w_out,
    w_up,
    w_down,
    vectors,
    mom_qkv,
    mom_out,
    mom_up,
    mom_down,
    adam_first,
    adam_second,
):
    tok_rows, width = tokens_in.shape
    side = width // 2
    dp_count = lax.axis_size("dp")
    bits = dp_count.bit_length() - 1
    rank, core = lax.axis_index("dp"), lax.axis_index("fsdp")
    up_order = list(range(bits))
    qkv_cols, out_cols, up_cols = w_qkv.shape[1], w_out.shape[1], w_up.shape[1]
    vec_rows, vec_cols = vectors.shape
    devices = 2 * dp_count

    masks = [(offset & 1) | (offset & 2) << 1 for offset in range(PLANES)]
    plane_bits = [place for place in range(bits) if place not in (0, 2)]
    plane = bit_of(rank, 0) + 2 * bit_of(rank, 2)
    index = jnp.stack([rank, core, plane]).astype(jnp.int32)
    first_col = (vec_cols * (2 * rank + core)).astype(jnp.uint32)
    top = jnp.uint32(0)
    vec_wide = lax.dynamic_update_slice(
        jnp.zeros((16, width), LOW), vectors.astype(LOW), (top, first_col)
    )
    split = -(-(qkv_cols + 8) // 16) * 16
    rows = split + -(-(out_cols + 8) // 16) * 16
    exact = qkv_cols % 8 == 0 and out_cols % 8 == 0 and split == qkv_cols + 8 and rows == split + out_cols + 8
    pack = jnp.concatenate(
        [
            jnp.pad(w_qkv.T.astype(LOW), ((0, split - 8 - qkv_cols), (0, 0))),
            vec_wide[:8],
            jnp.pad(w_out.T.astype(LOW), ((0, rows - split - 8 - out_cols), (0, 0))),
            vec_wide[8:],
        ],
        axis=0,
    )
    pack_one, pack_two = pack[:, :side], pack[:, side:]
    far = up_order[2:][::-1]
    near_one, near_two = [1, 0], [0, 1]
    all_one = gather_relative(pack_one, far, [])
    all_two = gather_relative(pack_two, far, [])
    hidden_low = (w_up.T.astype(LOW), w_down.astype(LOW))
    all_one, all_two, *hidden_low = tie(all_one, all_two, *hidden_low)
    all_one = gather_relative(all_one, near_one, far)
    all_two = gather_relative(all_two, near_two, far)
    hidden_far = [gather_relative(part, far, []).reshape(-1, width) for part in hidden_low]
    all_one, all_two, *hidden_far = tie(all_one, all_two, *hidden_far)
    hidden_near = [
        jnp.stack([part, xor_trade(part, 1 << near[0])])
        for part, near in zip(hidden_far, (near_one, near_two))
    ]
    own_packs = [part.reshape((dp_count, rows, side)) for part in (all_one, all_two)]
    other_packs = [core_trade(part) for part in own_packs]
    packs = (own_packs[0], other_packs[0], own_packs[1], other_packs[1])
    far_count = dp_count // 4
    hidden_rows = far_count * up_cols
    wide_side, out_side = (devices * qkv_cols, side), (devices * out_cols, side)
    if exact:
        projected_low, *sides, vec_full, up_bias = run_kernel(
            unpack_body,
            [((tok_rows, 3 * width), LOW), (wide_side, LOW), (wide_side, LOW)]
            + [(out_side, LOW), (out_side, LOW), ((16, width), WIDE), ((8, hidden_rows), WIDE)],
            (index, *packs, tokens_in),
            [((devices, up_cols), WIDE)],
            scalars=1,
            room=18,
        )
        qkv_sides, out_sides = sides[:2], sides[2:]
    else:
        natural = [
            xor_order(pair(own, other, core, 1), rank, bits).reshape(devices, rows, side)
            for own, other in zip(own_packs, other_packs)
        ]
        qkv_sides = [part[:, :qkv_cols].reshape(wide_side) for part in natural]
        out_sides = [part[:, split : split + out_cols].reshape(out_side) for part in natural]
        vec_full = jnp.concatenate(natural, axis=2).astype(WIDE)
        vec_full = jnp.concatenate([vec_full[:, split - 8 : split], vec_full[:, rows - 8 :]], axis=1)
        vec_full = jnp.sum(vec_full, axis=0)
        qkv_bias = jnp.concatenate([vec_full[4], jnp.zeros((width,), WIDE), vec_full[5]])
        projected = rows_by_cols(tokens_in[:, :side], qkv_sides[0])
        projected = projected + rows_by_cols(tokens_in[:, side:], qkv_sides[1])
        projected_low = (projected + qkv_bias).astype(LOW)
        up_bias = xor_order(vec_full[8:12].reshape(dp_count, 2, up_cols), rank, bits)
        up_bias = up_bias.reshape(far_count, 2, 2, 2, up_cols).transpose(3, 1, 2, 0, 4)
        up_bias = up_bias.reshape(2, 4, hidden_rows)
        up_bias = jnp.where(core == 0, up_bias, up_bias[::-1]).reshape(8, hidden_rows)
    own_kv = projected_low[:, width:]
    other_kv = core_trade(own_kv)
    square = (tok_rows, width)
    context_low, normed, normed_low, unit, scale, probs = run_kernel(
        attend_body,
        [(square, LOW), (square, WIDE), (square, LOW), (square, WIDE), ((tok_rows, 1), WIDE)]
        + [((width // HD, tok_rows, 2 * tok_rows), WIDE)],
        (index, seq_lengths, projected_low, other_kv, *out_sides, tokens_in, vec_full),
        scalars=2,
    )
    hidden_got = [xor_trade(part, 1 << near[1]) for part, near in zip(hidden_near, (near_one, near_two))]
    hidden_got = gate(hidden_got, scale)
    pieces = []
    for part, got in zip(hidden_near, hidden_got):
        pieces += [part, got, core_trade(part), core_trade(got)]
    piece = hidden_near[0].shape
    output, d_normed, g_bias_up, rows_two, *grads = run_kernel(
        hidden_body,
        [(square, LOW), (square, WIDE), ((8, hidden_rows), WIDE), ((3, width), WIDE)]
        + [(piece, LOW)] * 8,
        (index, seq_lengths, normed, normed_low, cotangent, vec_full, up_bias, *pieces),
        [((8, tok_rows, hidden_rows), LOW), ((8, tok_rows, hidden_rows), WIDE)],
        room=18,
        scalars=2,
    )
    hidden_orders = (up_order, [1] + up_order[2:] + [0])
    hidden_left = [[bits] + up_order[2:], up_order[2:] + [bits]]
    mark = jnp.zeros(*MARK)
    hidden_sent, mark = summed(
        (grads[1], grads[5]), (core_trade(grads[3]), core_trade(grads[7])), mark, LOW
    )
    hidden_kept, _ = summed(
        (grads[0], grads[4]), (core_trade(grads[2]), core_trade(grads[6])), mark, WIDE
    )
    d_resid_one, d_attended, d_query, own_grad, other_grad, rows_one = run_kernel(
        attend_back_body,
        [(square, WIDE), (square, LOW), (square, LOW)]
        + [((tok_rows, 2 * width), WIDE), ((tok_rows, 2 * width), LOW), ((3, width), WIDE)],
        (d_normed, projected_low, other_kv, probs, *out_sides, unit, scale, vec_full),
    )
    (other_grad,) = gate((other_grad,), mark)
    got_grad = core_trade(other_grad)
    if exact:
        block = ((dp_count, rows, side), LOW)
        d_qkv, *g_sides = run_kernel(
            pack_body,
            [((tok_rows, 3 * width), LOW), block, block, block, block],
            (index, d_query, own_grad, got_grad, tokens_in, d_attended, context_low)
            + (rows_one, rows_two, g_bias_up),
            [(wide_side, WIDE), (out_side, WIDE), ((devices, up_cols), WIDE), ((16, width), WIDE)],
            scalars=1,
            room=20,
        )
    else:
        d_kv = own_grad + got_grad.astype(WIDE)
        d_qkv = jnp.concatenate([d_query, d_kv.astype(LOW)], axis=1)
        sums = jnp.sum(d_qkv.astype(WIDE), axis=0, keepdims=True)
        g_bias_up = g_bias_up.reshape(2, 4, hidden_rows)
        g_bias_up = jnp.where(core == 0, g_bias_up, g_bias_up[::-1])
        g_bias_up = g_bias_up.reshape(2, 2, 2, far_count, up_cols).transpose(3, 1, 2, 0, 4)
        g_bias_up = xor_order(g_bias_up.reshape(dp_count, 2, up_cols), rank, bits)
        g_rows = [rows_one[:2], rows_two[:2], sums[:, :width], sums[:, 2 * width :]]
        g_rows += [rows_one[2:], rows_two[2:], g_bias_up.reshape(-1, width)]
        g_rows = jnp.concatenate(g_rows + [jnp.zeros((4, width), WIDE)], axis=0).astype(LOW)
        g_sides = []
        for part in range(2):
            at = slice(part * side, (part + 1) * side)
            whole = jnp.broadcast_to(g_rows[None, :, at], (devices, 16, side))
            g_qkv = over_tokens(d_qkv, tokens_in[:, at]).reshape(devices, qkv_cols, side)
            g_out = over_tokens(d_attended, context_low[:, at]).reshape(devices, out_cols, side)
            whole = jnp.concatenate(
                [
                    jnp.pad(g_qkv, ((0, 0), (0, split - 8 - qkv_cols), (0, 0))),
                    whole[:, :8],
                    jnp.pad(g_out, ((0, 0), (0, rows - split - 8 - out_cols), (0, 0))),
                    whole[:, 8:],
                ],
                axis=1,
            )
            whole = xor_order(whole.reshape(dp_count, 2, rows, side), rank, bits)
            g_sides += [pick(whole, core, 1), pick(whole, 1 - core, 1)]
    attn_orders = (up_order, [2, 0, 1] + up_order[3:])
    attn_kept = g_sides[::2]
    attn_got = [core_trade(part) for part in g_sides[1::2]]
    for step in range(bits):
        left = [order[step:] for order in attn_orders]
        attn_kept, attn_sent, mark = stepped(attn_kept, attn_got, mark, left, (rows, side))
        attn_got = [
            xor_trade(sent, 1 << order[step]) for sent, order in zip(attn_sent, attn_orders)
        ]
        got = [xor_trade(sent, 1 << order[step]) for sent, order in zip(hidden_sent, hidden_orders)]
        if step < bits - 1:
            left = [order[step:] for order in hidden_left]
            hidden_kept, hidden_sent, mark = stepped(hidden_kept, got, mark, left, (up_cols, width))
    last = [part.reshape(rows, side) for part in (*attn_kept, *attn_got)]
    last += [part.reshape(up_cols, width) for part in (*hidden_kept, *got)]
    d_tokens = d_resid_one + jnp.concatenate([plain(d_qkv, part) for part in qkv_sides], axis=1)

    piece_rows = max(qkv_cols, up_cols)
    moments = (mom_qkv.T, mom_out.T, mom_up.T, mom_down)
    if exact:
        shapes = [(moment.shape, WIDE) for moment in moments]
        results = run_kernel(
            moment_body,
            [((piece_rows, width), LOW)] * PLANES + shapes + shapes + [((16, width), WIDE)],
            (index, *last, *moments),
            [((PLANES, piece_rows, width), LOW)],
            scalars=1,
        )
        pieces = results[:PLANES]
        grads_t, moments_t = results[PLANES : 2 * PLANES], results[2 * PLANES : 3 * PLANES]
        vec_sums = results[-1]
    else:
        attn = [kept.astype(WIDE) + part.astype(WIDE) for kept, part in zip(last[:2], last[2:4])]
        attn = jnp.concatenate(attn, axis=1)
        grads_t = [attn[:qkv_cols], attn[split : split + out_cols]]
        grads_t += [kept + part.astype(WIDE) for kept, part in zip(last[4:6], last[6:8])]
        vec_sums = jnp.concatenate([attn[split - 8 : split], attn[rows - 8 :]], axis=0)
        moments_t = [momentum_decay * moment + grad for moment, grad in zip(moments, grads_t)]
        stacked = [
            jnp.pad(moment.astype(LOW), ((0, piece_rows - moment.shape[0]), (0, 0)))
            for moment in moments_t
        ]
        stacked = jnp.stack(stacked)
        pieces = [pick(stacked, plane ^ offset, 0) for offset in range(PLANES)]
    grad_qkv_t, grad_out_t, grad_up_t, grad_down = grads_t
    grad_vectors = lax.dynamic_slice(vec_sums, (top, first_col), (vec_rows, vec_cols))
    new_mom_qkv, new_mom_out, new_mom_up = [moment.T for moment in moments_t[:3]]
    new_mom_down = moments_t[3]
    mine = [pieces[0]]
    for offset in range(1, PLANES):
        mine.append(xor_trade(pieces[offset], masks[offset]))
    turned = orthogonal(mine, index, plane_bits)
    back = [turned[0]]
    for offset in range(1, PLANES):
        back.append(xor_trade(turned[offset], masks[offset]))
    hidden = up_cols * devices
    sizes = (3 * width, width, max(width, hidden), max(width, hidden))
    weights = (w_qkv.T, w_out.T, w_up.T, w_down)
    if exact:
        new_weights = run_kernel(
            functools.partial(update_body, sizes),
            [(weight.shape, WIDE) for weight in weights],
            (index, *back, *weights),
            [((PLANES, piece_rows, width), LOW)],
            scalars=1,
        )
    else:
        back = jnp.stack(back)
        new_weights = [
            weight_update(weight, pick(back, plane ^ place, 0)[: weight.shape[0]].astype(WIDE), longest)
            for place, (weight, longest) in enumerate(zip(weights, sizes))
        ]
    new_w_qkv, new_w_out, new_w_up = [weight.T for weight in new_weights[:3]]
    new_w_down = new_weights[3]

    new_first = beta_one * adam_first + (1.0 - beta_one) * grad_vectors
    new_second = beta_two * adam_second + (1.0 - beta_two) * grad_vectors * grad_vectors
    first_hat = new_first / (1.0 - beta_one**STEP)
    second_hat = new_second / (1.0 - beta_two**STEP)
    new_vectors = vectors - adam_rate * first_hat / (jnp.sqrt(second_hat) + adam_epsilon)
    return (
        output,
        d_tokens,
        grad_qkv_t.T,
        grad_out_t.T,
        grad_up_t.T,
        grad_down,
        grad_vectors,
        new_mom_qkv,
        new_mom_out,
        new_mom_up,
        new_mom_down,
        new_w_qkv,
        new_w_out,
        new_w_up,
        new_w_down,
        new_first,
        new_second,
        new_vectors,
    )


def solution(mesh):
    in_specs = (
        P(("dp", "fsdp"), None),
        P(("dp", "fsdp"), None),
        P("dp", None),
        P(None, ("dp", "fsdp")),
        P(None, ("dp", "fsdp")),
        P(None, ("dp", "fsdp")),
        P(("dp", "fsdp"), None),
        P(None, ("dp", "fsdp")),
        P(None, ("dp", "fsdp")),
        P(None, ("dp", "fsdp")),
        P(None, ("dp", "fsdp")),
        P(("dp", "fsdp"), None),
        P(None, ("dp", "fsdp")),
        P(None, ("dp", "fsdp")),
    )
    out_specs = (
        P(("dp", "fsdp"), None),
        P(("dp", "fsdp"), None),
        P(None, ("dp", "fsdp")),
        P(None, ("dp", "fsdp")),
        P(None, ("dp", "fsdp")),
        P(("dp", "fsdp"), None),
        P(None, ("dp", "fsdp")),
        P(None, ("dp", "fsdp")),
        P(None, ("dp", "fsdp")),
        P(None, ("dp", "fsdp")),
        P(("dp", "fsdp"), None),
        P(None, ("dp", "fsdp")),
        P(None, ("dp", "fsdp")),
        P(None, ("dp", "fsdp")),
        P(("dp", "fsdp"), None),
        P(None, ("dp", "fsdp")),
        P(None, ("dp", "fsdp")),
        P(None, ("dp", "fsdp")),
    )
    return jax.shard_map(
        per_device, mesh=mesh, in_specs=in_specs, out_specs=out_specs, check_vma=False
    )
```

```python
import functools
import math

import jax
import jax.numpy as jnp
from jax import lax
from jax.experimental import pallas as pl
from jax.experimental.pallas import tpu as pltpu
from jax.sharding import PartitionSpec as P

HD = 64
NS_ITERS = 2
STEP = 10

poly_one = 3.4445
poly_three = -4.775
poly_five = 2.0315
momentum_decay = 0.95
muon_rate = 0.3
muon_decay = 0.01
adam_rate = 0.2
beta_one = 0.9
beta_two = 0.999
adam_epsilon = 1e-08
norm_epsilon = 1e-05
ortho_epsilon = 1e-07
masked_score = -1e30
PLANES = 4
LOW = jnp.bfloat16
WIDE = jnp.float32


def xor_trade(block, distance):
    count = lax.axis_size("dp")
    return lax.ppermute(block, "dp", [(i, i ^ distance) for i in range(count)])


def core_trade(block):
    return lax.ppermute(block, "fsdp", [(0, 1), (1, 0)])


def bit_of(rank, place):
    return (rank >> place) & 1


def pick(block, index, axis):
    return lax.dynamic_index_in_dim(block, index, axis, keepdims=False)


def pair(mine, other, bit, axis):
    first = jnp.where(bit == 0, mine, other)
    second = jnp.where(bit == 0, other, mine)
    return jnp.stack([first, second], axis)


def higher(places, place):
    return sum(1 for other in places if other > place)


def gather_relative(block, order, done):
    for index, place in enumerate(order):
        axis = higher(done + order[:index], place)
        block = jnp.stack([block, xor_trade(block, 1 << place)], axis)
    return block


def tie(*values):
    return lax.optimization_barrier(values)


def xor_order(block, rank, bits):
    tail = block.shape[1:]
    block = block.reshape((2,) * bits + tail)
    for place in range(bits):
        axis = bits - 1 - place
        block = jnp.where(bit_of(rank, place) == 0, block, jnp.flip(block, axis))
    return block.reshape((-1,) + tail)


def nt(left, right):
    return lax.dot_general(left, right, (((1,), (1,)), ((), ())), preferred_element_type=WIDE)


def nn(left, right):
    return lax.dot_general(left, right, (((1,), (0,)), ((), ())), preferred_element_type=WIDE)


def tn(left, right):
    return lax.dot_general(left, right, (((0,), (0,)), ((), ())), preferred_element_type=WIDE)


def run_kernel(body, results, operands, scratch=(), scalars=0, room=10):
    places = [pltpu.SMEM] * scalars + [pltpu.VMEM] * (len(operands) - scalars)
    return pl.pallas_call(
        body,
        out_shape=[jax.ShapeDtypeStruct(shape, kind) for shape, kind in results],
        in_specs=[pl.BlockSpec(memory_space=place) for place in places],
        out_specs=[pl.BlockSpec(memory_space=pltpu.VMEM)] * len(results),
        scratch_shapes=[pltpu.VMEM(shape, kind) for shape, kind in scratch],
        compiler_params=pltpu.CompilerParams(vmem_limit_bytes=room * 1024 * 1024),
        cost_estimate=pl.CostEstimate(flops=1000, bytes_accessed=1000, transcendentals=0),
    )(*operands)


def gate(values, *needed):
    anywhere = pl.BlockSpec(memory_space=pl.ANY)
    return pl.pallas_call(
        lambda *refs: None,
        out_shape=[jax.ShapeDtypeStruct(value.shape, value.dtype) for value in values],
        in_specs=[anywhere] * (len(values) + len(needed)),
        out_specs=[anywhere] * len(values),
        input_output_aliases={place: place for place in range(len(values))},
        compiler_params=pltpu.CompilerParams(vmem_limit_bytes=1024 * 1024),
        cost_estimate=pl.CostEstimate(flops=0, bytes_accessed=0, transcendentals=0),
    )(*values, *needed)


MARK = ((8, 128), WIDE)


def step_body(count, splits, *refs):
    kept, got = refs[:count], refs[count : 2 * count]
    results = list(refs[2 * count + 1 :])
    results.pop()[...] = jnp.zeros(MARK[0], WIDE)
    for kept_ref, got_ref in zip(kept, got):
        if splits:
            for half in range(2):
                part = kept_ref[:, half].astype(WIDE) + got_ref[:, half].astype(WIDE)
                result = results.pop(0)
                result[...] = part.astype(result.dtype)
        else:
            result = results.pop(0)
            result[...] = (kept_ref[...].astype(WIDE) + got_ref[...].astype(WIDE)).astype(result.dtype)


def summed(kept, got, mark, kind):
    results = [(part.shape, kind) for part in kept] + [MARK]
    body = functools.partial(step_body, len(kept), False)
    *totals, mark = run_kernel(body, results, (*kept, *got, mark))
    return totals, mark


def stepped(kept, got, mark, orders, tail):
    results, operands = [], []
    for part, order in zip(kept, orders):
        above = higher(order, order[0])
        shape = (2**above, 2 ** (len(order) - 1 - above)) + tail
        operands.append((shape[0], 2) + shape[1:])
        results += [(shape, WIDE), (shape, LOW)]
    body = functools.partial(step_body, len(kept), True)
    parts = [part.reshape(shape) for part, shape in zip((*kept, *got), operands * 2)]
    *halves, mark = run_kernel(body, results + [MARK], (*parts, mark))
    return halves[::2], halves[1::2], mark


def mean_of(values):
    return jnp.sum(values, axis=-1, keepdims=True) * (1.0 / values.shape[-1])


def normalized(values):
    center = values - mean_of(values)
    scale = lax.rsqrt(mean_of(center * center) + norm_epsilon)
    return center * scale, scale


def norm_back(grad, unit, scale, gain):
    inner = grad * gain
    return scale * (inner - mean_of(inner) - unit * mean_of(inner * unit))


def head_probs(query, keys, allowed):
    scores = nt(query, keys) * (HD ** (-0.5))
    scores = jnp.where(allowed, scores, masked_score)
    exp_scores = jnp.exp(scores - jnp.max(scores, axis=-1, keepdims=True))
    return exp_scores / jnp.sum(exp_scores, axis=-1, keepdims=True)


def head_parts(head, width, own_ref, other_ref):
    at = slice(head * HD, (head + 1) * HD)
    keys = jnp.concatenate([own_ref[:, width:][:, at], other_ref[:, :width][:, at]], axis=0)
    values = jnp.concatenate([own_ref[:, 2 * width :][:, at], other_ref[:, width:][:, at]], axis=0)
    return own_ref[:, at], keys, values


def segments(index_ref, lengths_ref, places):
    half = places.size // 2 if places.shape[0] == 1 else places.shape[0]
    places = jnp.where(index_ref[1] == 0, places, (places + half) & (2 * half - 1))
    result, bound = jnp.zeros(places.shape, jnp.int32), 0
    for entry in range(lengths_ref.shape[1]):
        bound = bound + lengths_ref[0, entry]
        result = result + jnp.where(places >= bound, 1, 0)
    return result


def own_segments(index_ref, lengths_ref, tok_rows):
    return segments(index_ref, lengths_ref, lax.broadcasted_iota(jnp.int32, (tok_rows, 1), 0))


def allowed_pairs(index_ref, lengths_ref, tok_rows):
    every = lax.broadcasted_iota(jnp.int32, (1, 2 * tok_rows), 1)
    return own_segments(index_ref, lengths_ref, tok_rows) == segments(index_ref, lengths_ref, every)


def attend_body(
    index_ref, lengths_ref, own_ref, other_ref, one_ref, two_ref, tokens_ref, vec_ref,
    context_ref, normed_ref, low_ref, unit_ref, scale_ref, probs_ref,
):
    width = tokens_ref.shape[1]
    side = width // 2
    allowed = allowed_pairs(index_ref, lengths_ref, tokens_ref.shape[0])
    for start in range(0, width // HD, 2):
        found = []
        for head in (start, start + 1):
            query, keys, values = head_parts(head, width, own_ref, other_ref)
            probs = head_probs(query, keys, allowed)
            probs_ref[head] = probs
            found.append(nn(probs.astype(LOW), values))
        context_ref[:, start * HD : (start + 2) * HD] = jnp.concatenate(found, axis=1).astype(LOW)
    attended = (
        nt(context_ref[:, :side], one_ref[...])
        + nt(context_ref[:, side:], two_ref[...])
        + vec_ref[6:7, :]
    )
    unit, scale = normalized(tokens_ref[...].astype(WIDE) + attended)
    normed = unit * vec_ref[0:1, :] + vec_ref[1:2, :]
    normed_ref[...] = normed
    low_ref[...] = normed.astype(LOW)
    unit_ref[...] = unit
    scale_ref[...] = scale


def attend_back_body(
    d_normed_ref, own_ref, other_ref, probs_ref, one_ref, two_ref, unit_ref, scale_ref, vec_ref,
    resid_ref, attended_ref, query_ref, own_grad_ref, other_grad_ref, rows_ref,
):
    tok_rows, width = d_normed_ref.shape
    grad, unit = d_normed_ref[...], unit_ref[...]
    resid = norm_back(grad, unit, scale_ref[...], vec_ref[0:1, :])
    low = resid.astype(LOW)
    resid_ref[...] = resid
    attended_ref[...] = low
    rows_ref[0:1, :] = jnp.sum(grad * unit, axis=0, keepdims=True)
    rows_ref[1:2, :] = jnp.sum(grad, axis=0, keepdims=True)
    rows_ref[2:3, :] = jnp.sum(low.astype(WIDE), axis=0, keepdims=True)
    d_context = jnp.concatenate([nn(low, one_ref[...]), nn(low, two_ref[...])], axis=1).astype(LOW)
    factor = HD ** (-0.5)
    for start in range(0, width // HD, 2):
        found = []
        for head in (start, start + 1):
            query, keys, values = head_parts(head, width, own_ref, other_ref)
            grad_head = d_context[:, head * HD : (head + 1) * HD]
            probs = probs_ref[head]
            d_probs = nt(grad_head, values)
            inner = jnp.sum(probs * d_probs, axis=-1, keepdims=True)
            d_scores = (probs * (d_probs - inner)).astype(LOW)
            found.append(
                (nn(d_scores, keys) * factor, tn(d_scores, query) * factor,
                 tn(probs.astype(LOW), grad_head))
            )
        d_query, d_keys, d_values = [
            jnp.concatenate([first, second], axis=1) for first, second in zip(*found)
        ]
        at = slice(start * HD, (start + 2) * HD)
        shifted = slice(width + start * HD, width + (start + 2) * HD)
        query_ref[:, at] = d_query.astype(LOW)
        own_grad_ref[:, at] = d_keys[:tok_rows]
        own_grad_ref[:, shifted] = d_values[:tok_rows]
        other_grad_ref[:, at] = d_keys[tok_rows:].astype(LOW)
        other_grad_ref[:, shifted] = d_values[tok_rows:].astype(LOW)


def activate(low, matrix, bias):
    pre = nt(low, matrix) + bias
    cdf = 0.5 * (1.0 + lax.erf(pre * 0.7071067811865476))
    return (pre * cdf).astype(LOW), cdf + pre * jnp.exp(-0.5 * pre * pre) * 0.3989422804014327


def early_body(
    low_ref, bias_ref, up_own, down_own, act_ref, slope_ref, lowered_ref, mark_ref
):
    low = low_ref[...]
    for high in range(2):
        place = 2 * high
        act_ref[high], slope_ref[high] = activate(low, up_own[high], bias_ref[place : place + 1, :])
    lowered_ref[...] = nn(act_ref[0], down_own[0])
    mark_ref[...] = jnp.zeros(MARK[0], WIDE)


def own_body(
    low_ref, bias_ref, early_ref, sum_ref, up_got, down_near, down_got, act_ref, slope_ref, lowered_ref
):
    low = low_ref[...]
    lowered = sum_ref[...] + nn(early_ref[1], down_got[0])
    for high, down in enumerate((down_near, down_got)):
        place = 2 * high + 1
        act_ref[high], slope_ref[high] = activate(low, up_got[high], bias_ref[place : place + 1, :])
        lowered = lowered + nn(act_ref[high], down[1])
    lowered_ref[...] = lowered


def hidden_body(
    index_ref, lengths_ref, normed_ref, low_ref, cotangent_ref, vec_ref, bias_ref,
    sum_ref, early_act, early_slope, own_act, own_slope, *refs
):
    up, down = refs[:4], refs[4:8]
    output_ref, grad_ref, g_bias, rows_ref = refs[8:12]
    g_up, g_down = refs[12:16], refs[16:20]
    act_ref, slope_ref = refs[20:]
    low = low_ref[...]
    lowered = sum_ref[...] + vec_ref[7:8, :]
    for high in range(2):
        for lower in range(2):
            place, slot = 4 + 2 * high + lower, 2 * high + lower
            act_ref[slot], slope_ref[slot] = activate(
                low, up[2 + lower][high], bias_ref[place : place + 1, :]
            )
            lowered = lowered + nn(act_ref[slot], down[2 + high][lower])
    blocks = [(core, high, lower) for core in range(2) for high in range(2) for lower in range(2)]

    def kept(core, high, lower):
        if core == 1:
            return act_ref[2 * high + lower], slope_ref[2 * high + lower]
        if lower == 0:
            return early_act[high], early_slope[high]
        return own_act[high], own_slope[high]

    unit, scale = normalized(normed_ref[...] + lowered)
    output_ref[...] = (unit * vec_ref[2:3, :] + vec_ref[3:4, :]).astype(LOW)
    segment = own_segments(index_ref, lengths_ref, low.shape[0])
    live = jnp.where(segment < lengths_ref.shape[1], 1.0, 0.0)
    top = cotangent_ref[...].astype(WIDE) * live
    resid = norm_back(top, unit, scale, vec_ref[2:3, :])
    d_lowered = resid.astype(LOW)
    rows_ref[0:1, :] = jnp.sum(top * unit, axis=0, keepdims=True)
    rows_ref[1:2, :] = jnp.sum(top, axis=0, keepdims=True)
    rows_ref[2:3, :] = jnp.sum(d_lowered.astype(WIDE), axis=0, keepdims=True)
    total = resid
    for place, (core, high, lower) in enumerate(blocks):
        act, slope = kept(core, high, lower)
        g_down[2 * core + high][lower] = tn(act, d_lowered).astype(LOW)
        d_pre = (nt(d_lowered, down[2 * core + high][lower]) * slope).astype(LOW)
        g_bias[place : place + 1, :] = jnp.sum(d_pre.astype(WIDE), axis=0, keepdims=True)
        g_up[2 * core + lower][high] = tn(d_pre, low).astype(LOW)
        total = total + nn(d_pre, up[2 * core + lower][high])
    grad_ref[...] = total


def chunk_slot(rank, core, chunk, far):
    place = jnp.bitwise_xor(rank, chunk // 2)
    block = 4 * jnp.bitwise_xor(core, chunk % 2) + jnp.bitwise_and(place, 3)
    return far * block + lax.shift_right_logical(place, 2)


def unpack_body(
    index_ref, own_one, other_one, own_two, other_two, tokens_ref,
    projected_ref, qkv_one, qkv_two, out_one, out_two, vec_ref, bias_ref, chunk_ref,
):
    rank, core = index_ref[0], index_ref[1]
    count, rows, side = own_one.shape
    width = 2 * side
    qkv_cols = qkv_one.shape[0] // (2 * count)
    out_cols = out_one.shape[0] // (2 * count)
    split = qkv_cols + 8
    total = []
    for own, other, qkv, out in (
        (own_one, other_one, qkv_one, out_one), (own_two, other_two, qkv_two, out_two)
    ):
        vec = jnp.zeros((16, side), WIDE)
        for place in range(count):
            slot = jnp.bitwise_xor(rank, place)
            mine, theirs = own[slot].astype(WIDE), other[slot].astype(WIDE)
            first = jnp.where(core == 0, mine, theirs)
            second = jnp.where(core == 0, theirs, mine)
            both = jnp.concatenate([first[:qkv_cols], second[:qkv_cols]], axis=0)
            qkv[2 * qkv_cols * place : 2 * qkv_cols * (place + 1), :] = both.astype(LOW)
            both = [part[split : split + out_cols] for part in (first, second)]
            both = jnp.concatenate(both, axis=0)
            out[2 * out_cols * place : 2 * out_cols * (place + 1), :] = both.astype(LOW)
            vec = vec + jnp.concatenate(
                [mine[qkv_cols:split] + theirs[qkv_cols:split], mine[rows - 8 :] + theirs[rows - 8 :]],
                axis=0,
            )
        total.append(vec)
    vec = jnp.concatenate(total, axis=1)
    vec_ref[...] = vec
    far, cols = count // 4, chunk_ref.shape[1]
    per_row = width // cols
    for chunk in range(2 * count):
        at = slice((chunk % per_row) * cols, (chunk % per_row + 1) * cols)
        row = 8 + chunk // per_row
        chunk_ref[pl.ds(chunk_slot(rank, core, chunk, far), 1), :] = vec[row : row + 1, at]
    for block in range(8):
        parts = [chunk_ref[far * block + part : far * block + part + 1, :] for part in range(far)]
        bias_ref[block : block + 1, :] = jnp.concatenate(parts, axis=1)
    for part, bias in enumerate((vec[4:5], None, vec[5:6])):
        at = slice(part * width, (part + 1) * width)
        block = nt(tokens_ref[:, :side], qkv_one[at, :]) + nt(tokens_ref[:, side:], qkv_two[at, :])
        projected_ref[:, at] = (block if bias is None else block + bias).astype(LOW)


def pack_body(
    index_ref, query_ref, own_ref, got_ref, tokens_ref, attended_ref, context_ref,
    one_ref, two_ref, g_bias_ref,
    d_qkv_ref, kept_one, sent_one, kept_two, sent_two, wide_ref, out_ref, chunk_ref, rows_ref,
):
    rank, core = index_ref[0], index_ref[1]
    count, rows, side = kept_one.shape
    width = 2 * side
    qkv_cols = wide_ref.shape[0] // (2 * count)
    out_cols = out_ref.shape[0] // (2 * count)
    d_qkv_ref[:, :width] = query_ref[...]
    d_qkv_ref[:, width:] = (own_ref[...] + got_ref[...].astype(WIDE)).astype(LOW)
    far, cols = count // 4, chunk_ref.shape[1]
    for block in range(8):
        for part in range(far):
            at = slice(part * cols, (part + 1) * cols)
            chunk_ref[far * block + part : far * block + part + 1, :] = g_bias_ref[block : block + 1, at]
    rows_ref[...] = jnp.zeros(rows_ref.shape, WIDE)
    rows_ref[0:2, :] = one_ref[:2]
    rows_ref[2:4, :] = two_ref[:2]
    rows_ref[6:7, :] = one_ref[2:]
    rows_ref[7:8, :] = two_ref[2:]
    for part, row in ((0, 4), (2, 5)):
        block = slice(part * width, (part + 1) * width)
        rows_ref[row : row + 1, :] = jnp.sum(d_qkv_ref[:, block].astype(WIDE), axis=0, keepdims=True)
    per_row = width // cols
    for chunk in range(2 * count):
        at = slice((chunk % per_row) * cols, (chunk % per_row + 1) * cols)
        row = 8 + chunk // per_row
        rows_ref[row : row + 1, at] = chunk_ref[pl.ds(chunk_slot(rank, core, chunk, far), 1), :]
    for index, (kept, sent) in enumerate(((kept_one, sent_one), (kept_two, sent_two))):
        at = slice(index * side, (index + 1) * side)
        for part in range(3):
            block = slice(part * width, (part + 1) * width)
            wide_ref[block, :] = tn(d_qkv_ref[:, block], tokens_ref[:, at])
        out_ref[...] = tn(attended_ref[...], context_ref[:, at])
        low_rows = rows_ref[:8, at]
        high_rows = rows_ref[8:, at]
        for place in range(count):
            slot = jnp.bitwise_xor(rank, place)
            blocks = []
            for chunk in (2 * place, 2 * place + 1):
                blocks.append(
                    jnp.concatenate(
                        [
                            wide_ref[qkv_cols * chunk : qkv_cols * (chunk + 1), :],
                            low_rows,
                            out_ref[out_cols * chunk : out_cols * (chunk + 1), :],
                            high_rows,
                        ],
                        axis=0,
                    )
                )
            kept[slot] = jnp.where(core == 0, blocks[0], blocks[1]).astype(LOW)
            sent[slot] = jnp.where(core == 0, blocks[1], blocks[0]).astype(LOW)


def rows_by_cols(left, right):
    return jnp.einsum("td,fd->tf", left, right, preferred_element_type=WIDE)


def plain(left, right):
    return jnp.dot(left, right, preferred_element_type=WIDE)


def over_tokens(left, right):
    return jnp.einsum("ta,tb->ab", left, right, preferred_element_type=WIDE).astype(LOW)


def moment_body(index_ref, *refs):
    kept_one, kept_two, got_one, got_two, kept_up, kept_down, got_up, got_down = refs[:8]
    moments, pieces, grads, results = refs[8:12], refs[12:16], refs[16:20], refs[20:24]
    vec_ref, stack_ref = refs[24:]
    attn = jnp.concatenate(
        [kept_one[...] + got_one[...].astype(WIDE), kept_two[...] + got_two[...].astype(WIDE)], axis=1
    )
    qkv_cols, out_cols = moments[0].shape[0], moments[1].shape[0]
    split = qkv_cols + 8
    vec_ref[...] = jnp.concatenate([attn[qkv_cols:split], attn[split + out_cols :]], axis=0)
    sums = (
        attn[:qkv_cols],
        attn[split : split + out_cols],
        kept_up[...] + got_up[...].astype(WIDE),
        kept_down[...] + got_down[...].astype(WIDE),
    )
    for place, (moment, total, grad, result) in enumerate(zip(moments, sums, grads, results)):
        grad[...] = total
        updated = momentum_decay * moment[...] + total
        result[...] = updated
        missing = stack_ref.shape[1] - updated.shape[0]
        if missing:
            updated = jnp.concatenate([updated, jnp.zeros((missing, updated.shape[1]), WIDE)], axis=0)
        stack_ref[place] = updated.astype(LOW)
    plane = index_ref[2]
    for offset, piece in enumerate(pieces):
        piece[...] = stack_ref[jnp.bitwise_xor(plane, offset)]


def weight_update(weight, ortho, longest):
    return weight - muon_rate * (0.2 * math.sqrt(longest) * ortho + muon_decay * weight)


def update_body(sizes, index_ref, *refs):
    stack_ref = refs[-1]
    for offset in range(PLANES):
        stack_ref[offset] = refs[offset][...]
    for place, longest in enumerate(sizes):
        weight, result = refs[PLANES + place], refs[2 * PLANES + place]
        ortho = stack_ref[jnp.bitwise_xor(index_ref[2], place)].astype(WIDE)[: weight.shape[0]]
        result[...] = weight_update(weight[...], ortho, longest)


def gram_body(index_ref, *refs):
    rows, kept_ref, sent_ref = refs[:-2], refs[-2], refs[-1]
    gram = tn(rows[0][...], rows[0][...])
    for part in rows[1:]:
        gram = gram + tn(part[...], part[...])
    third = gram.shape[0] // 3
    first = gram[:third]
    second = jnp.concatenate([gram[third : 2 * third, third:], gram[2 * third :, 2 * third :]], axis=1)
    kept_ref[...] = jnp.where(index_ref[1] == 0, first, second)
    sent_ref[...] = jnp.where(index_ref[1] == 0, second, first).astype(LOW)


def share_body(kept_ref, got_ref, *results):
    half = kept_ref.shape[0] // 2
    for way in range(2):
        at = slice(way * half, (way + 1) * half)
        total = kept_ref[at, :] + got_ref[at, :].astype(WIDE)
        results[way][...] = total
        results[2 + way][...] = total.astype(LOW)


def add_body(*refs):
    for way in range(2):
        total = refs[way][...] + refs[2 + way][...].astype(WIDE)
        refs[4 + way][...] = total
        refs[6 + way][...] = total.astype(LOW)


def join_body(first, second, got_first, got_second, result):
    half = first.shape[0]
    result[:half, :] = (first[...] + got_first[...].astype(WIDE)).astype(LOW)
    result[half:, :] = (second[...] + got_second[...].astype(WIDE)).astype(LOW)


def orthogonal_body(index_ref, own_ref, other_ref, *refs):
    count = (len(refs) - 1) // 2
    rows, results, gram_ref = refs[:count], refs[count : 2 * count], refs[-1]
    third = own_ref.shape[0]
    own, other = own_ref[...].astype(WIDE), other_ref[...].astype(WIDE)
    first = jnp.where(index_ref[1] == 0, own, other)
    second = jnp.where(index_ref[1] == 0, other, own)
    gram_ref[:third, :] = first
    gram_ref[third : 2 * third, third:] = second[:, : 2 * third]
    gram_ref[2 * third :, 2 * third :] = second[:, 2 * third :]
    gram_ref[third : 2 * third, :third] = first[:, third : 2 * third].T
    gram_ref[2 * third :, :third] = first[:, 2 * third :].T
    gram_ref[2 * third :, third : 2 * third] = second[:, third : 2 * third].T
    trace = jnp.zeros((1, 1), WIDE)
    spot = lax.broadcasted_iota(jnp.int32, (third, third), 0)
    eye = spot == lax.broadcasted_iota(jnp.int32, (third, third), 1)
    for part in range(3):
        at = slice(part * third, (part + 1) * third)
        block = jnp.where(eye, gram_ref[at, at], 0.0)
        trace = trace + jnp.sum(jnp.sum(block, axis=1, keepdims=True), axis=0, keepdims=True)
    factor = 1.0 / (jnp.sqrt(trace) + ortho_epsilon)
    gram_mat = gram_ref[...] * (factor * factor)
    low_x = [part[...] for part in rows]
    current = [part.astype(WIDE) * factor for part in low_x]
    for iteration in range(NS_ITERS):
        low_gram = gram_mat.astype(LOW)
        low_mixing = (poly_three * gram_mat + poly_five * nn(low_gram, low_gram)).astype(LOW)
        scale = factor if iteration == 0 else 1.0
        current = [
            poly_one * part + nn(low, low_mixing) * scale for part, low in zip(current, low_x)
        ]
        low_x = [part.astype(LOW) for part in current]
        if iteration < NS_ITERS - 1:
            product = nn(low_mixing, low_gram)
            gram_mat = (
                (poly_one * poly_one) * gram_mat
                + (2.0 * poly_one) * product
                + nn(low_mixing, product.astype(LOW))
            )
    for result, part in zip(results, low_x):
        result[...] = part


def orthogonal(rows, index, low_bits):
    count, width = rows[0].shape
    third = width // 3
    kept, sent = run_kernel(
        gram_body, [((third, width), WIDE), ((third, width), LOW)], (index, *rows), scalars=1
    )
    half = (third // 2, width)
    both = [(half, WIDE)] * 2 + [(half, LOW)] * 2
    *parts, left, right = run_kernel(share_body, both, (kept, core_trade(sent)))
    for step in range(len(low_bits)):
        got = [
            xor_trade(part, 1 << low_bits[(step + way) % len(low_bits)])
            for way, part in enumerate((left, right))
        ]
        if step < len(low_bits) - 1:
            *parts, left, right = run_kernel(add_body, both, (*parts, *got))
    (own,) = run_kernel(join_body, [((third, width), LOW)], (*parts, *got))
    return run_kernel(
        orthogonal_body,
        [((count, width), LOW)] * len(rows),
        (index, own, core_trade(own), *rows),
        [((width, width), WIDE)],
        scalars=1,
        room=26,
    )


def per_device(
    tokens_in,
    cotangent,
    seq_lengths,
    w_qkv,
    w_out,
    w_up,
    w_down,
    vectors,
    mom_qkv,
    mom_out,
    mom_up,
    mom_down,
    adam_first,
    adam_second,
):
    tok_rows, width = tokens_in.shape
    side = width // 2
    dp_count = lax.axis_size("dp")
    bits = dp_count.bit_length() - 1
    rank, core = lax.axis_index("dp"), lax.axis_index("fsdp")
    up_order = list(range(bits))
    qkv_cols, out_cols, up_cols = w_qkv.shape[1], w_out.shape[1], w_up.shape[1]
    vec_rows, vec_cols = vectors.shape
    devices = 2 * dp_count

    masks = [(offset & 1) | (offset & 2) << 1 for offset in range(PLANES)]
    plane_bits = [place for place in range(bits) if place not in (0, 2)]
    plane = bit_of(rank, 0) + 2 * bit_of(rank, 2)
    index = jnp.stack([rank, core, plane]).astype(jnp.int32)
    first_col = (vec_cols * (2 * rank + core)).astype(jnp.uint32)
    top = jnp.uint32(0)
    vec_wide = lax.dynamic_update_slice(
        jnp.zeros((16, width), LOW), vectors.astype(LOW), (top, first_col)
    )
    split = -(-(qkv_cols + 8) // 16) * 16
    rows = split + -(-(out_cols + 8) // 16) * 16
    exact = qkv_cols % 8 == 0 and out_cols % 8 == 0 and split == qkv_cols + 8 and rows == split + out_cols + 8
    pack = jnp.concatenate(
        [
            jnp.pad(w_qkv.T.astype(LOW), ((0, split - 8 - qkv_cols), (0, 0))),
            vec_wide[:8],
            jnp.pad(w_out.T.astype(LOW), ((0, rows - split - 8 - out_cols), (0, 0))),
            vec_wide[8:],
        ],
        axis=0,
    )
    pack_one, pack_two = pack[:, :side], pack[:, side:]
    far = up_order[2:][::-1]
    near_one, near_two = [1, 0], [0, 1]
    all_one = gather_relative(pack_one, far, [])
    all_two = gather_relative(pack_two, far, [])
    hidden_low = (w_up.T.astype(LOW), w_down.astype(LOW))
    all_one, all_two, *hidden_low = tie(all_one, all_two, *hidden_low)
    all_one = gather_relative(all_one, near_one, far)
    all_two = gather_relative(all_two, near_two, far)
    hidden_far = [gather_relative(part, far, []).reshape(-1, width) for part in hidden_low]
    all_one, all_two, *hidden_far = tie(all_one, all_two, *hidden_far)
    hidden_near = [
        jnp.stack([part, xor_trade(part, 1 << near[0])])
        for part, near in zip(hidden_far, (near_one, near_two))
    ]
    own_packs = [part.reshape((dp_count, rows, side)) for part in (all_one, all_two)]
    other_packs = [core_trade(part) for part in own_packs]
    packs = (own_packs[0], other_packs[0], own_packs[1], other_packs[1])
    far_count = dp_count // 4
    hidden_rows = far_count * up_cols
    wide_side, out_side = (devices * qkv_cols, side), (devices * out_cols, side)
    if exact:
        projected_low, *sides, vec_full, up_bias = run_kernel(
            unpack_body,
            [((tok_rows, 3 * width), LOW), (wide_side, LOW), (wide_side, LOW)]
            + [(out_side, LOW), (out_side, LOW), ((16, width), WIDE), ((8, hidden_rows), WIDE)],
            (index, *packs, tokens_in),
            [((devices, up_cols), WIDE)],
            scalars=1,
            room=18,
        )
        qkv_sides, out_sides = sides[:2], sides[2:]
    else:
        natural = [
            xor_order(pair(own, other, core, 1), rank, bits).reshape(devices, rows, side)
            for own, other in zip(own_packs, other_packs)
        ]
        qkv_sides = [part[:, :qkv_cols].reshape(wide_side) for part in natural]
        out_sides = [part[:, split : split + out_cols].reshape(out_side) for part in natural]
        vec_full = jnp.concatenate(natural, axis=2).astype(WIDE)
        vec_full = jnp.concatenate([vec_full[:, split - 8 : split], vec_full[:, rows - 8 :]], axis=1)
        vec_full = jnp.sum(vec_full, axis=0)
        qkv_bias = jnp.concatenate([vec_full[4], jnp.zeros((width,), WIDE), vec_full[5]])
        projected = rows_by_cols(tokens_in[:, :side], qkv_sides[0])
        projected = projected + rows_by_cols(tokens_in[:, side:], qkv_sides[1])
        projected_low = (projected + qkv_bias).astype(LOW)
        up_bias = xor_order(vec_full[8:12].reshape(dp_count, 2, up_cols), rank, bits)
        up_bias = up_bias.reshape(far_count, 2, 2, 2, up_cols).transpose(3, 1, 2, 0, 4)
        up_bias = up_bias.reshape(2, 4, hidden_rows)
        up_bias = jnp.where(core == 0, up_bias, up_bias[::-1]).reshape(8, hidden_rows)
    own_kv = projected_low[:, width:]
    other_kv = core_trade(own_kv)
    square = (tok_rows, width)
    context_low, normed, normed_low, unit, scale, probs = run_kernel(
        attend_body,
        [(square, LOW), (square, WIDE), (square, LOW), (square, WIDE), ((tok_rows, 1), WIDE)]
        + [((width // HD, tok_rows, 2 * tok_rows), WIDE)],
        (index, seq_lengths, projected_low, other_kv, *out_sides, tokens_in, vec_full),
        scalars=2,
    )
    hidden_got = [xor_trade(part, 1 << near[1]) for part, near in zip(hidden_near, (near_one, near_two))]
    piece, block = hidden_near[0].shape, (tok_rows, hidden_rows)
    early_act, early_slope, lowered, early = run_kernel(
        early_body,
        [((2,) + block, LOW), ((2,) + block, WIDE), (square, WIDE), MARK],
        (normed_low, up_bias, *hidden_near),
    )
    hidden_got = gate(hidden_got, early)
    pieces = []
    for part, got in zip(hidden_near, hidden_got):
        pieces += [part, got, core_trade(part), core_trade(got)]
    own_act, own_slope, lowered = run_kernel(
        own_body,
        [((2,) + block, LOW), ((2,) + block, WIDE), (square, WIDE)],
        (normed_low, up_bias, early_act, lowered, hidden_got[0], hidden_near[1], hidden_got[1]),
    )
    output, d_normed, g_bias_up, rows_two, *grads = run_kernel(
        hidden_body,
        [(square, LOW), (square, WIDE), ((8, hidden_rows), WIDE), ((3, width), WIDE)]
        + [(piece, LOW)] * 8,
        (index, seq_lengths, normed, normed_low, cotangent, vec_full, up_bias)
        + (lowered, early_act, early_slope, own_act, own_slope, *pieces),
        [((4,) + block, LOW), ((4,) + block, WIDE)],
        room=18,
        scalars=2,
    )
    hidden_orders = (up_order, [1] + up_order[2:] + [0])
    hidden_left = [[bits] + up_order[2:], up_order[2:] + [bits]]
    mark = jnp.zeros(*MARK)
    hidden_sent, mark = summed(
        (grads[1], grads[5]), (core_trade(grads[3]), core_trade(grads[7])), mark, LOW
    )
    hidden_kept, _ = summed(
        (grads[0], grads[4]), (core_trade(grads[2]), core_trade(grads[6])), mark, WIDE
    )
    d_resid_one, d_attended, d_query, own_grad, other_grad, rows_one = run_kernel(
        attend_back_body,
        [(square, WIDE), (square, LOW), (square, LOW)]
        + [((tok_rows, 2 * width), WIDE), ((tok_rows, 2 * width), LOW), ((3, width), WIDE)],
        (d_normed, projected_low, other_kv, probs, *out_sides, unit, scale, vec_full),
    )
    (other_grad,) = gate((other_grad,), mark)
    got_grad = core_trade(other_grad)
    if exact:
        pack_block = ((dp_count, rows, side), LOW)
        d_qkv, *g_sides = run_kernel(
            pack_body,
            [((tok_rows, 3 * width), LOW)] + [pack_block] * 4,
            (index, d_query, own_grad, got_grad, tokens_in, d_attended, context_low)
            + (rows_one, rows_two, g_bias_up),
            [(wide_side, WIDE), (out_side, WIDE), ((devices, up_cols), WIDE), ((16, width), WIDE)],
            scalars=1,
            room=20,
        )
    else:
        d_kv = own_grad + got_grad.astype(WIDE)
        d_qkv = jnp.concatenate([d_query, d_kv.astype(LOW)], axis=1)
        sums = jnp.sum(d_qkv.astype(WIDE), axis=0, keepdims=True)
        g_bias_up = g_bias_up.reshape(2, 4, hidden_rows)
        g_bias_up = jnp.where(core == 0, g_bias_up, g_bias_up[::-1])
        g_bias_up = g_bias_up.reshape(2, 2, 2, far_count, up_cols).transpose(3, 1, 2, 0, 4)
        g_bias_up = xor_order(g_bias_up.reshape(dp_count, 2, up_cols), rank, bits)
        g_rows = [rows_one[:2], rows_two[:2], sums[:, :width], sums[:, 2 * width :]]
        g_rows += [rows_one[2:], rows_two[2:], g_bias_up.reshape(-1, width)]
        g_rows = jnp.concatenate(g_rows + [jnp.zeros((4, width), WIDE)], axis=0).astype(LOW)
        g_sides = []
        for part in range(2):
            at = slice(part * side, (part + 1) * side)
            whole = jnp.broadcast_to(g_rows[None, :, at], (devices, 16, side))
            g_qkv = over_tokens(d_qkv, tokens_in[:, at]).reshape(devices, qkv_cols, side)
            g_out = over_tokens(d_attended, context_low[:, at]).reshape(devices, out_cols, side)
            whole = jnp.concatenate(
                [
                    jnp.pad(g_qkv, ((0, 0), (0, split - 8 - qkv_cols), (0, 0))),
                    whole[:, :8],
                    jnp.pad(g_out, ((0, 0), (0, rows - split - 8 - out_cols), (0, 0))),
                    whole[:, 8:],
                ],
                axis=1,
            )
            whole = xor_order(whole.reshape(dp_count, 2, rows, side), rank, bits)
            g_sides += [pick(whole, core, 1), pick(whole, 1 - core, 1)]
    attn_orders = (up_order, [2, 0, 1] + up_order[3:])
    attn_kept = g_sides[::2]
    attn_got = [core_trade(part) for part in g_sides[1::2]]
    for step in range(bits):
        left = [order[step:] for order in attn_orders]
        attn_kept, attn_sent, mark = stepped(attn_kept, attn_got, mark, left, (rows, side))
        attn_got = [
            xor_trade(sent, 1 << order[step]) for sent, order in zip(attn_sent, attn_orders)
        ]
        got = [xor_trade(sent, 1 << order[step]) for sent, order in zip(hidden_sent, hidden_orders)]
        if step < bits - 1:
            left = [order[step:] for order in hidden_left]
            hidden_kept, hidden_sent, mark = stepped(hidden_kept, got, mark, left, (up_cols, width))
    last = [part.reshape(rows, side) for part in (*attn_kept, *attn_got)]
    last += [part.reshape(up_cols, width) for part in (*hidden_kept, *got)]
    d_tokens = d_resid_one + jnp.concatenate([plain(d_qkv, part) for part in qkv_sides], axis=1)

    piece_rows = max(qkv_cols, up_cols)
    moments = (mom_qkv.T, mom_out.T, mom_up.T, mom_down)
    if exact:
        shapes = [(moment.shape, WIDE) for moment in moments]
        results = run_kernel(
            moment_body,
            [((piece_rows, width), LOW)] * PLANES + shapes + shapes + [((16, width), WIDE)],
            (index, *last, *moments),
            [((PLANES, piece_rows, width), LOW)],
            scalars=1,
        )
        pieces = results[:PLANES]
        grads_t, moments_t = results[PLANES : 2 * PLANES], results[2 * PLANES : 3 * PLANES]
        vec_sums = results[-1]
    else:
        attn = [kept.astype(WIDE) + part.astype(WIDE) for kept, part in zip(last[:2], last[2:4])]
        attn = jnp.concatenate(attn, axis=1)
        grads_t = [attn[:qkv_cols], attn[split : split + out_cols]]
        grads_t += [kept + part.astype(WIDE) for kept, part in zip(last[4:6], last[6:8])]
        vec_sums = jnp.concatenate([attn[split - 8 : split], attn[rows - 8 :]], axis=0)
        moments_t = [momentum_decay * moment + grad for moment, grad in zip(moments, grads_t)]
        stacked = [
            jnp.pad(moment.astype(LOW), ((0, piece_rows - moment.shape[0]), (0, 0)))
            for moment in moments_t
        ]
        stacked = jnp.stack(stacked)
        pieces = [pick(stacked, plane ^ offset, 0) for offset in range(PLANES)]
    grad_qkv_t, grad_out_t, grad_up_t, grad_down = grads_t
    grad_vectors = lax.dynamic_slice(vec_sums, (top, first_col), (vec_rows, vec_cols))
    new_mom_qkv, new_mom_out, new_mom_up = [moment.T for moment in moments_t[:3]]
    new_mom_down = moments_t[3]
    mine = [pieces[0]]
    for offset in range(1, PLANES):
        mine.append(xor_trade(pieces[offset], masks[offset]))
    turned = orthogonal(mine, index, plane_bits)
    back = [turned[0]]
    for offset in range(1, PLANES):
        back.append(xor_trade(turned[offset], masks[offset]))
    hidden = up_cols * devices
    sizes = (3 * width, width, max(width, hidden), max(width, hidden))
    weights = (w_qkv.T, w_out.T, w_up.T, w_down)
    if exact:
        new_weights = run_kernel(
            functools.partial(update_body, sizes),
            [(weight.shape, WIDE) for weight in weights],
            (index, *back, *weights),
            [((PLANES, piece_rows, width), LOW)],
            scalars=1,
        )
    else:
        back = jnp.stack(back)
        new_weights = [
            weight_update(weight, pick(back, plane ^ place, 0)[: weight.shape[0]].astype(WIDE), longest)
            for place, (weight, longest) in enumerate(zip(weights, sizes))
        ]
    new_w_qkv, new_w_out, new_w_up = [weight.T for weight in new_weights[:3]]
    new_w_down = new_weights[3]

    new_first = beta_one * adam_first + (1.0 - beta_one) * grad_vectors
    new_second = beta_two * adam_second + (1.0 - beta_two) * grad_vectors * grad_vectors
    first_hat = new_first / (1.0 - beta_one**STEP)
    second_hat = new_second / (1.0 - beta_two**STEP)
    new_vectors = vectors - adam_rate * first_hat / (jnp.sqrt(second_hat) + adam_epsilon)
    return (
        output,
        d_tokens,
        grad_qkv_t.T,
        grad_out_t.T,
        grad_up_t.T,
        grad_down,
        grad_vectors,
        new_mom_qkv,
        new_mom_out,
        new_mom_up,
        new_mom_down,
        new_w_qkv,
        new_w_out,
        new_w_up,
        new_w_down,
        new_first,
        new_second,
        new_vectors,
    )


def solution(mesh):
    in_specs = (
        P(("dp", "fsdp"), None),
        P(("dp", "fsdp"), None),
        P("dp", None),
        P(None, ("dp", "fsdp")),
        P(None, ("dp", "fsdp")),
        P(None, ("dp", "fsdp")),
        P(("dp", "fsdp"), None),
        P(None, ("dp", "fsdp")),
        P(None, ("dp", "fsdp")),
        P(None, ("dp", "fsdp")),
        P(None, ("dp", "fsdp")),
        P(("dp", "fsdp"), None),
        P(None, ("dp", "fsdp")),
        P(None, ("dp", "fsdp")),
    )
    out_specs = (
        P(("dp", "fsdp"), None),
        P(("dp", "fsdp"), None),
        P(None, ("dp", "fsdp")),
        P(None, ("dp", "fsdp")),
        P(None, ("dp", "fsdp")),
        P(("dp", "fsdp"), None),
        P(None, ("dp", "fsdp")),
        P(None, ("dp", "fsdp")),
        P(None, ("dp", "fsdp")),
        P(None, ("dp", "fsdp")),
        P(("dp", "fsdp"), None),
        P(None, ("dp", "fsdp")),
        P(None, ("dp", "fsdp")),
        P(None, ("dp", "fsdp")),
        P(("dp", "fsdp"), None),
        P(None, ("dp", "fsdp")),
        P(None, ("dp", "fsdp")),
        P(None, ("dp", "fsdp")),
    )
    return jax.shard_map(
        per_device, mesh=mesh, in_specs=in_specs, out_specs=out_specs, check_vma=False
    )
```

```python
import functools
import math

import jax
import jax.numpy as jnp
from jax import lax
from jax.experimental import pallas as pl
from jax.experimental.pallas import tpu as pltpu
from jax.sharding import PartitionSpec as P

HD = 64
NS_ITERS = 2
STEP = 10

poly_one = 3.4445
poly_three = -4.775
poly_five = 2.0315
momentum_decay = 0.95
muon_rate = 0.3
muon_decay = 0.01
adam_rate = 0.2
beta_one = 0.9
beta_two = 0.999
adam_epsilon = 1e-08
norm_epsilon = 1e-05
ortho_epsilon = 1e-07
masked_score = -1e30
PLANES = 4
LOW = jnp.bfloat16
WIDE = jnp.float32


def xor_trade(block, distance):
    count = lax.axis_size("dp")
    return lax.ppermute(block, "dp", [(i, i ^ distance) for i in range(count)])


def core_trade(block):
    return lax.ppermute(block, "fsdp", [(0, 1), (1, 0)])


def bit_of(rank, place):
    return (rank >> place) & 1


def pick(block, index, axis):
    return lax.dynamic_index_in_dim(block, index, axis, keepdims=False)


def pair(mine, other, bit, axis):
    first = jnp.where(bit == 0, mine, other)
    second = jnp.where(bit == 0, other, mine)
    return jnp.stack([first, second], axis)


def higher(places, place):
    return sum(1 for other in places if other > place)


def gather_relative(block, order, done):
    for index, place in enumerate(order):
        axis = higher(done + order[:index], place)
        block = jnp.stack([block, xor_trade(block, 1 << place)], axis)
    return block


def tie(*values):
    return lax.optimization_barrier(values)


def xor_order(block, rank, bits):
    tail = block.shape[1:]
    block = block.reshape((2,) * bits + tail)
    for place in range(bits):
        axis = bits - 1 - place
        block = jnp.where(bit_of(rank, place) == 0, block, jnp.flip(block, axis))
    return block.reshape((-1,) + tail)


def nt(left, right):
    return lax.dot_general(left, right, (((1,), (1,)), ((), ())), preferred_element_type=WIDE)


def nn(left, right):
    return lax.dot_general(left, right, (((1,), (0,)), ((), ())), preferred_element_type=WIDE)


def tn(left, right):
    return lax.dot_general(left, right, (((0,), (0,)), ((), ())), preferred_element_type=WIDE)


def run_kernel(body, results, operands, scratch=(), scalars=0, room=10):
    places = [pltpu.SMEM] * scalars + [pltpu.VMEM] * (len(operands) - scalars)
    return pl.pallas_call(
        body,
        out_shape=[jax.ShapeDtypeStruct(shape, kind) for shape, kind in results],
        in_specs=[pl.BlockSpec(memory_space=place) for place in places],
        out_specs=[pl.BlockSpec(memory_space=pltpu.VMEM)] * len(results),
        scratch_shapes=[pltpu.VMEM(shape, kind) for shape, kind in scratch],
        compiler_params=pltpu.CompilerParams(vmem_limit_bytes=room * 1024 * 1024),
        cost_estimate=pl.CostEstimate(flops=1000, bytes_accessed=1000, transcendentals=0),
    )(*operands)


def gate(values, *needed):
    anywhere = pl.BlockSpec(memory_space=pl.ANY)
    return pl.pallas_call(
        lambda *refs: None,
        out_shape=[jax.ShapeDtypeStruct(value.shape, value.dtype) for value in values],
        in_specs=[anywhere] * (len(values) + len(needed)),
        out_specs=[anywhere] * len(values),
        input_output_aliases={place: place for place in range(len(values))},
        compiler_params=pltpu.CompilerParams(vmem_limit_bytes=1024 * 1024),
        cost_estimate=pl.CostEstimate(flops=0, bytes_accessed=0, transcendentals=0),
    )(*values, *needed)


MARK = ((8, 128), WIDE)


def step_body(count, splits, *refs):
    kept, got = refs[:count], refs[count : 2 * count]
    results = list(refs[2 * count + 1 :])
    results.pop()[...] = jnp.zeros(MARK[0], WIDE)
    for kept_ref, got_ref in zip(kept, got):
        if splits:
            for half in range(2):
                part = kept_ref[:, half].astype(WIDE) + got_ref[:, half].astype(WIDE)
                result = results.pop(0)
                result[...] = part.astype(result.dtype)
        else:
            result = results.pop(0)
            result[...] = (kept_ref[...].astype(WIDE) + got_ref[...].astype(WIDE)).astype(result.dtype)


def summed(kept, got, mark, kind):
    results = [(part.shape, kind) for part in kept] + [MARK]
    body = functools.partial(step_body, len(kept), False)
    *totals, mark = run_kernel(body, results, (*kept, *got, mark))
    return totals, mark


def stepped(kept, got, mark, orders, tail):
    results, operands = [], []
    for part, order in zip(kept, orders):
        above = higher(order, order[0])
        shape = (2**above, 2 ** (len(order) - 1 - above)) + tail
        operands.append((shape[0], 2) + shape[1:])
        results += [(shape, WIDE), (shape, LOW)]
    body = functools.partial(step_body, len(kept), True)
    parts = [part.reshape(shape) for part, shape in zip((*kept, *got), operands * 2)]
    *halves, mark = run_kernel(body, results + [MARK], (*parts, mark))
    return halves[::2], halves[1::2], mark


def mean_of(values):
    return jnp.sum(values, axis=-1, keepdims=True) * (1.0 / values.shape[-1])


def normalized(values):
    center = values - mean_of(values)
    scale = lax.rsqrt(mean_of(center * center) + norm_epsilon)
    return center * scale, scale


def norm_back(grad, unit, scale, gain):
    inner = grad * gain
    return scale * (inner - mean_of(inner) - unit * mean_of(inner * unit))


def head_probs(query, keys, allowed):
    scores = nt(query, keys) * (HD ** (-0.5))
    scores = jnp.where(allowed, scores, masked_score)
    exp_scores = jnp.exp(scores - jnp.max(scores, axis=-1, keepdims=True))
    return exp_scores / jnp.sum(exp_scores, axis=-1, keepdims=True)


def head_parts(head, width, own_ref, other_ref):
    at = slice(head * HD, (head + 1) * HD)
    keys = jnp.concatenate([own_ref[:, width:][:, at], other_ref[:, :width][:, at]], axis=0)
    values = jnp.concatenate([own_ref[:, 2 * width :][:, at], other_ref[:, width:][:, at]], axis=0)
    return own_ref[:, at], keys, values


def segments(index_ref, lengths_ref, places):
    half = places.size // 2 if places.shape[0] == 1 else places.shape[0]
    places = jnp.where(index_ref[1] == 0, places, (places + half) & (2 * half - 1))
    result, bound = jnp.zeros(places.shape, jnp.int32), 0
    for entry in range(lengths_ref.shape[1]):
        bound = bound + lengths_ref[0, entry]
        result = result + jnp.where(places >= bound, 1, 0)
    return result


def own_segments(index_ref, lengths_ref, tok_rows):
    return segments(index_ref, lengths_ref, lax.broadcasted_iota(jnp.int32, (tok_rows, 1), 0))


def allowed_pairs(index_ref, lengths_ref, tok_rows):
    every = lax.broadcasted_iota(jnp.int32, (1, 2 * tok_rows), 1)
    return own_segments(index_ref, lengths_ref, tok_rows) == segments(index_ref, lengths_ref, every)


def attend_body(
    index_ref, lengths_ref, own_ref, other_ref, one_ref, two_ref, tokens_ref, vec_ref,
    context_ref, normed_ref, low_ref, unit_ref, scale_ref, probs_ref,
):
    width = tokens_ref.shape[1]
    side = width // 2
    allowed = allowed_pairs(index_ref, lengths_ref, tokens_ref.shape[0])
    for start in range(0, width // HD, 2):
        found = []
        for head in (start, start + 1):
            query, keys, values = head_parts(head, width, own_ref, other_ref)
            probs = head_probs(query, keys, allowed)
            probs_ref[head] = probs
            found.append(nn(probs.astype(LOW), values))
        context_ref[:, start * HD : (start + 2) * HD] = jnp.concatenate(found, axis=1).astype(LOW)
    attended = (
        nt(context_ref[:, :side], one_ref[...])
        + nt(context_ref[:, side:], two_ref[...])
        + vec_ref[6:7, :]
    )
    unit, scale = normalized(tokens_ref[...].astype(WIDE) + attended)
    normed = unit * vec_ref[0:1, :] + vec_ref[1:2, :]
    normed_ref[...] = normed
    low_ref[...] = normed.astype(LOW)
    unit_ref[...] = unit
    scale_ref[...] = scale


def attend_back_body(
    d_normed_ref, own_ref, other_ref, probs_ref, one_ref, two_ref, unit_ref, scale_ref, vec_ref,
    resid_ref, attended_ref, query_ref, own_grad_ref, other_grad_ref, rows_ref,
):
    tok_rows, width = d_normed_ref.shape
    grad, unit = d_normed_ref[...], unit_ref[...]
    resid = norm_back(grad, unit, scale_ref[...], vec_ref[0:1, :])
    low = resid.astype(LOW)
    resid_ref[...] = resid
    attended_ref[...] = low
    rows_ref[0:1, :] = jnp.sum(grad * unit, axis=0, keepdims=True)
    rows_ref[1:2, :] = jnp.sum(grad, axis=0, keepdims=True)
    rows_ref[2:3, :] = jnp.sum(low.astype(WIDE), axis=0, keepdims=True)
    d_context = jnp.concatenate([nn(low, one_ref[...]), nn(low, two_ref[...])], axis=1).astype(LOW)
    factor = HD ** (-0.5)
    for start in range(0, width // HD, 2):
        found = []
        for head in (start, start + 1):
            query, keys, values = head_parts(head, width, own_ref, other_ref)
            grad_head = d_context[:, head * HD : (head + 1) * HD]
            probs = probs_ref[head]
            d_probs = nt(grad_head, values)
            inner = jnp.sum(probs * d_probs, axis=-1, keepdims=True)
            d_scores = (probs * (d_probs - inner)).astype(LOW)
            found.append(
                (nn(d_scores, keys) * factor, tn(d_scores, query) * factor,
                 tn(probs.astype(LOW), grad_head))
            )
        d_query, d_keys, d_values = [
            jnp.concatenate([first, second], axis=1) for first, second in zip(*found)
        ]
        at = slice(start * HD, (start + 2) * HD)
        shifted = slice(width + start * HD, width + (start + 2) * HD)
        query_ref[:, at] = d_query.astype(LOW)
        own_grad_ref[:, at] = d_keys[:tok_rows]
        own_grad_ref[:, shifted] = d_values[:tok_rows]
        other_grad_ref[:, at] = d_keys[tok_rows:].astype(LOW)
        other_grad_ref[:, shifted] = d_values[tok_rows:].astype(LOW)


def activate(low, matrix, bias):
    pre = nt(low, matrix) + bias
    cdf = 0.5 * (1.0 + lax.erf(pre * 0.7071067811865476))
    return (pre * cdf).astype(LOW), cdf + pre * jnp.exp(-0.5 * pre * pre) * 0.3989422804014327


def early_body(
    low_ref, bias_ref, up_own, down_own, act_ref, slope_ref, lowered_ref, mark_ref
):
    low = low_ref[...]
    for high in range(2):
        place = 2 * high
        act_ref[high], slope_ref[high] = activate(low, up_own[high], bias_ref[place : place + 1, :])
    lowered_ref[...] = nn(act_ref[0], down_own[0])
    mark_ref[...] = jnp.zeros(MARK[0], WIDE)


def own_body(
    low_ref, bias_ref, early_ref, sum_ref, up_got, down_near, down_got, act_ref, slope_ref, lowered_ref
):
    low = low_ref[...]
    lowered = sum_ref[...] + nn(early_ref[1], down_got[0])
    for high, down in enumerate((down_near, down_got)):
        place = 2 * high + 1
        act_ref[high], slope_ref[high] = activate(low, up_got[high], bias_ref[place : place + 1, :])
        lowered = lowered + nn(act_ref[high], down[1])
    lowered_ref[...] = lowered


def hidden_body(
    index_ref, lengths_ref, normed_ref, low_ref, cotangent_ref, vec_ref, bias_ref,
    sum_ref, early_act, early_slope, own_act, own_slope, *refs
):
    up, down = refs[:4], refs[4:8]
    output_ref, grad_ref, g_bias, rows_ref = refs[8:12]
    g_up, g_down = refs[12:16], refs[16:20]
    act_ref, slope_ref = refs[20:]
    low = low_ref[...]
    lowered = sum_ref[...] + vec_ref[7:8, :]
    for high in range(2):
        for lower in range(2):
            place, slot = 4 + 2 * high + lower, 2 * high + lower
            act_ref[slot], slope_ref[slot] = activate(
                low, up[2 + lower][high], bias_ref[place : place + 1, :]
            )
            lowered = lowered + nn(act_ref[slot], down[2 + high][lower])
    blocks = [(core, high, lower) for core in range(2) for high in range(2) for lower in range(2)]

    def kept(core, high, lower):
        if core == 1:
            return act_ref[2 * high + lower], slope_ref[2 * high + lower]
        if lower == 0:
            return early_act[high], early_slope[high]
        return own_act[high], own_slope[high]

    unit, scale = normalized(normed_ref[...] + lowered)
    output_ref[...] = (unit * vec_ref[2:3, :] + vec_ref[3:4, :]).astype(LOW)
    segment = own_segments(index_ref, lengths_ref, low.shape[0])
    live = jnp.where(segment < lengths_ref.shape[1], 1.0, 0.0)
    top = cotangent_ref[...].astype(WIDE) * live
    resid = norm_back(top, unit, scale, vec_ref[2:3, :])
    d_lowered = resid.astype(LOW)
    rows_ref[0:1, :] = jnp.sum(top * unit, axis=0, keepdims=True)
    rows_ref[1:2, :] = jnp.sum(top, axis=0, keepdims=True)
    rows_ref[2:3, :] = jnp.sum(d_lowered.astype(WIDE), axis=0, keepdims=True)
    total = resid
    for place, (core, high, lower) in enumerate(blocks):
        act, slope = kept(core, high, lower)
        g_down[2 * core + high][lower] = tn(act, d_lowered).astype(LOW)
        d_pre = (nt(d_lowered, down[2 * core + high][lower]) * slope).astype(LOW)
        g_bias[place : place + 1, :] = jnp.sum(d_pre.astype(WIDE), axis=0, keepdims=True)
        g_up[2 * core + lower][high] = tn(d_pre, low).astype(LOW)
        total = total + nn(d_pre, up[2 * core + lower][high])
    grad_ref[...] = total


def chunk_slot(rank, core, chunk, far):
    place = jnp.bitwise_xor(rank, chunk // 2)
    block = 4 * jnp.bitwise_xor(core, chunk % 2) + jnp.bitwise_and(place, 3)
    return far * block + lax.shift_right_logical(place, 2)


def unpack_body(
    index_ref, own_one, other_one, own_two, other_two, tokens_ref,
    projected_ref, qkv_one, qkv_two, out_one, out_two, vec_ref, bias_ref, chunk_ref,
):
    rank, core = index_ref[0], index_ref[1]
    count, rows, side = own_one.shape
    width = 2 * side
    qkv_cols = qkv_one.shape[0] // (2 * count)
    out_cols = out_one.shape[0] // (2 * count)
    split = qkv_cols + 8
    total = []
    for own, other, qkv, out in (
        (own_one, other_one, qkv_one, out_one), (own_two, other_two, qkv_two, out_two)
    ):
        vec = jnp.zeros((16, side), WIDE)
        for place in range(count):
            slot = jnp.bitwise_xor(rank, place)
            mine, theirs = own[slot].astype(WIDE), other[slot].astype(WIDE)
            first = jnp.where(core == 0, mine, theirs)
            second = jnp.where(core == 0, theirs, mine)
            both = jnp.concatenate([first[:qkv_cols], second[:qkv_cols]], axis=0)
            qkv[2 * qkv_cols * place : 2 * qkv_cols * (place + 1), :] = both.astype(LOW)
            both = [part[split : split + out_cols] for part in (first, second)]
            both = jnp.concatenate(both, axis=0)
            out[2 * out_cols * place : 2 * out_cols * (place + 1), :] = both.astype(LOW)
            vec = vec + jnp.concatenate(
                [mine[qkv_cols:split] + theirs[qkv_cols:split], mine[rows - 8 :] + theirs[rows - 8 :]],
                axis=0,
            )
        total.append(vec)
    vec = jnp.concatenate(total, axis=1)
    vec_ref[...] = vec
    far, cols = count // 4, chunk_ref.shape[1]
    per_row = width // cols
    for chunk in range(2 * count):
        at = slice((chunk % per_row) * cols, (chunk % per_row + 1) * cols)
        row = 8 + chunk // per_row
        chunk_ref[pl.ds(chunk_slot(rank, core, chunk, far), 1), :] = vec[row : row + 1, at]
    for block in range(8):
        parts = [chunk_ref[far * block + part : far * block + part + 1, :] for part in range(far)]
        bias_ref[block : block + 1, :] = jnp.concatenate(parts, axis=1)
    for part, bias in enumerate((vec[4:5], None, vec[5:6])):
        at = slice(part * width, (part + 1) * width)
        block = nt(tokens_ref[:, :side], qkv_one[at, :]) + nt(tokens_ref[:, side:], qkv_two[at, :])
        projected_ref[:, at] = (block if bias is None else block + bias).astype(LOW)


def pack_body(
    index_ref, query_ref, own_ref, got_ref, tokens_ref, attended_ref, context_ref,
    one_ref, two_ref, g_bias_ref,
    d_qkv_ref, kept_one, sent_one, kept_two, sent_two, wide_ref, out_ref, chunk_ref, rows_ref,
):
    rank, core = index_ref[0], index_ref[1]
    count, rows, side = kept_one.shape
    width = 2 * side
    qkv_cols = wide_ref.shape[0] // (2 * count)
    out_cols = out_ref.shape[0] // (2 * count)
    d_qkv_ref[:, :width] = query_ref[...]
    d_qkv_ref[:, width:] = (own_ref[...] + got_ref[...].astype(WIDE)).astype(LOW)
    far, cols = count // 4, chunk_ref.shape[1]
    for block in range(8):
        for part in range(far):
            at = slice(part * cols, (part + 1) * cols)
            chunk_ref[far * block + part : far * block + part + 1, :] = g_bias_ref[block : block + 1, at]
    rows_ref[...] = jnp.zeros(rows_ref.shape, WIDE)
    rows_ref[0:2, :] = one_ref[:2]
    rows_ref[2:4, :] = two_ref[:2]
    rows_ref[6:7, :] = one_ref[2:]
    rows_ref[7:8, :] = two_ref[2:]
    for part, row in ((0, 4), (2, 5)):
        block = slice(part * width, (part + 1) * width)
        rows_ref[row : row + 1, :] = jnp.sum(d_qkv_ref[:, block].astype(WIDE), axis=0, keepdims=True)
    per_row = width // cols
    for chunk in range(2 * count):
        at = slice((chunk % per_row) * cols, (chunk % per_row + 1) * cols)
        row = 8 + chunk // per_row
        rows_ref[row : row + 1, at] = chunk_ref[pl.ds(chunk_slot(rank, core, chunk, far), 1), :]
    for index, (kept, sent) in enumerate(((kept_one, sent_one), (kept_two, sent_two))):
        at = slice(index * side, (index + 1) * side)
        for part in range(3):
            block = slice(part * width, (part + 1) * width)
            wide_ref[block, :] = tn(d_qkv_ref[:, block], tokens_ref[:, at])
        out_ref[...] = tn(attended_ref[...], context_ref[:, at])
        low_rows = rows_ref[:8, at]
        high_rows = rows_ref[8:, at]
        for place in range(count):
            slot = jnp.bitwise_xor(rank, place)
            blocks = []
            for chunk in (2 * place, 2 * place + 1):
                blocks.append(
                    jnp.concatenate(
                        [
                            wide_ref[qkv_cols * chunk : qkv_cols * (chunk + 1), :],
                            low_rows,
                            out_ref[out_cols * chunk : out_cols * (chunk + 1), :],
                            high_rows,
                        ],
                        axis=0,
                    )
                )
            kept[slot] = jnp.where(core == 0, blocks[0], blocks[1]).astype(LOW)
            sent[slot] = jnp.where(core == 0, blocks[1], blocks[0]).astype(LOW)


def rows_by_cols(left, right):
    return jnp.einsum("td,fd->tf", left, right, preferred_element_type=WIDE)


def plain(left, right):
    return jnp.dot(left, right, preferred_element_type=WIDE)


def over_tokens(left, right):
    return jnp.einsum("ta,tb->ab", left, right, preferred_element_type=WIDE).astype(LOW)


def moment_body(index_ref, *refs):
    kept_one, kept_two, got_one, got_two, kept_up, kept_down, got_up, got_down = refs[:8]
    moments, pieces, grads, results = refs[8:12], refs[12:16], refs[16:20], refs[20:24]
    vec_ref, stack_ref = refs[24:]
    attn = jnp.concatenate(
        [kept_one[...] + got_one[...].astype(WIDE), kept_two[...] + got_two[...].astype(WIDE)], axis=1
    )
    qkv_cols, out_cols = moments[0].shape[0], moments[1].shape[0]
    split = qkv_cols + 8
    vec_ref[...] = jnp.concatenate([attn[qkv_cols:split], attn[split + out_cols :]], axis=0)
    sums = (
        attn[:qkv_cols],
        attn[split : split + out_cols],
        kept_up[...] + got_up[...].astype(WIDE),
        kept_down[...] + got_down[...].astype(WIDE),
    )
    for place, (moment, total, grad, result) in enumerate(zip(moments, sums, grads, results)):
        grad[...] = total
        updated = momentum_decay * moment[...] + total
        result[...] = updated
        missing = stack_ref.shape[1] - updated.shape[0]
        if missing:
            updated = jnp.concatenate([updated, jnp.zeros((missing, updated.shape[1]), WIDE)], axis=0)
        stack_ref[place] = updated.astype(LOW)
    plane = index_ref[2]
    for offset, piece in enumerate(pieces):
        piece[...] = stack_ref[jnp.bitwise_xor(plane, offset)]


def weight_update(weight, ortho, longest):
    return weight - muon_rate * (0.2 * math.sqrt(longest) * ortho + muon_decay * weight)


def update_body(sizes, index_ref, *refs):
    stack_ref = refs[-1]
    for offset in range(PLANES):
        stack_ref[offset] = refs[offset][...]
    for place, longest in enumerate(sizes):
        weight, result = refs[PLANES + place], refs[2 * PLANES + place]
        ortho = stack_ref[jnp.bitwise_xor(index_ref[2], place)].astype(WIDE)[: weight.shape[0]]
        result[...] = weight_update(weight[...], ortho, longest)


def together(parts):
    parts = [part[...] for part in parts]
    if parts[0].shape[0] % 16:
        return parts
    return [jnp.concatenate(parts, axis=0)]


def gram_body(index_ref, *refs):
    rows, kept_ref, sent_ref = refs[:-2], refs[-2], refs[-1]
    blocks = together(rows)
    gram = tn(blocks[0], blocks[0])
    for part in blocks[1:]:
        gram = gram + tn(part, part)
    third = gram.shape[0] // 3
    first = gram[:third]
    second = jnp.concatenate([gram[third : 2 * third, third:], gram[2 * third :, 2 * third :]], axis=1)
    kept_ref[...] = jnp.where(index_ref[1] == 0, first, second)
    sent_ref[...] = jnp.where(index_ref[1] == 0, second, first).astype(LOW)


def share_body(kept_ref, got_ref, *results):
    half = kept_ref.shape[0] // 2
    for way in range(2):
        at = slice(way * half, (way + 1) * half)
        total = kept_ref[at, :] + got_ref[at, :].astype(WIDE)
        results[way][...] = total
        results[2 + way][...] = total.astype(LOW)


def add_body(*refs):
    for way in range(2):
        total = refs[way][...] + refs[2 + way][...].astype(WIDE)
        refs[4 + way][...] = total
        refs[6 + way][...] = total.astype(LOW)


def join_body(first, second, got_first, got_second, result):
    half = first.shape[0]
    result[:half, :] = (first[...] + got_first[...].astype(WIDE)).astype(LOW)
    result[half:, :] = (second[...] + got_second[...].astype(WIDE)).astype(LOW)


def orthogonal_body(index_ref, own_ref, other_ref, *refs):
    count = (len(refs) - 1) // 2
    rows, results, gram_ref = refs[:count], refs[count : 2 * count], refs[-1]
    third = own_ref.shape[0]
    own, other = own_ref[...].astype(WIDE), other_ref[...].astype(WIDE)
    first = jnp.where(index_ref[1] == 0, own, other)
    second = jnp.where(index_ref[1] == 0, other, own)
    gram_ref[:third, :] = first
    gram_ref[third : 2 * third, third:] = second[:, : 2 * third]
    gram_ref[2 * third :, 2 * third :] = second[:, 2 * third :]
    gram_ref[third : 2 * third, :third] = first[:, third : 2 * third].T
    gram_ref[2 * third :, :third] = first[:, 2 * third :].T
    gram_ref[2 * third :, third : 2 * third] = second[:, third : 2 * third].T
    trace = jnp.zeros((1, 1), WIDE)
    spot = lax.broadcasted_iota(jnp.int32, (third, third), 0)
    eye = spot == lax.broadcasted_iota(jnp.int32, (third, third), 1)
    for part in range(3):
        at = slice(part * third, (part + 1) * third)
        block = jnp.where(eye, gram_ref[at, at], 0.0)
        trace = trace + jnp.sum(jnp.sum(block, axis=1, keepdims=True), axis=0, keepdims=True)
    factor = 1.0 / (jnp.sqrt(trace) + ortho_epsilon)
    gram_mat = gram_ref[...] * (factor * factor)
    low_x = together(rows)
    current = [part.astype(WIDE) * factor for part in low_x]
    for iteration in range(NS_ITERS):
        low_gram = gram_mat.astype(LOW)
        low_mixing = (poly_three * gram_mat + poly_five * nn(low_gram, low_gram)).astype(LOW)
        scale = factor if iteration == 0 else 1.0
        current = [
            poly_one * part + nn(low, low_mixing) * scale for part, low in zip(current, low_x)
        ]
        low_x = [part.astype(LOW) for part in current]
        if iteration < NS_ITERS - 1:
            product = nn(low_mixing, low_gram)
            gram_mat = (
                (poly_one * poly_one) * gram_mat
                + (2.0 * poly_one) * product
                + nn(low_mixing, product.astype(LOW))
            )
    size = results[0].shape[0]
    for place, result in enumerate(results):
        if len(low_x) == 1:
            result[...] = low_x[0][place * size : (place + 1) * size]
        else:
            result[...] = low_x[place]


def orthogonal(rows, index, low_bits):
    count, width = rows[0].shape
    third = width // 3
    kept, sent = run_kernel(
        gram_body, [((third, width), WIDE), ((third, width), LOW)], (index, *rows), scalars=1
    )
    half = (third // 2, width)
    both = [(half, WIDE)] * 2 + [(half, LOW)] * 2
    *parts, left, right = run_kernel(share_body, both, (kept, core_trade(sent)))
    for step in range(len(low_bits)):
        got = [
            xor_trade(part, 1 << low_bits[(step + way) % len(low_bits)])
            for way, part in enumerate((left, right))
        ]
        if step < len(low_bits) - 1:
            *parts, left, right = run_kernel(add_body, both, (*parts, *got))
    (own,) = run_kernel(join_body, [((third, width), LOW)], (*parts, *got))
    return run_kernel(
        orthogonal_body,
        [((count, width), LOW)] * len(rows),
        (index, own, core_trade(own), *rows),
        [((width, width), WIDE)],
        scalars=1,
        room=26,
    )


def per_device(
    tokens_in,
    cotangent,
    seq_lengths,
    w_qkv,
    w_out,
    w_up,
    w_down,
    vectors,
    mom_qkv,
    mom_out,
    mom_up,
    mom_down,
    adam_first,
    adam_second,
):
    tok_rows, width = tokens_in.shape
    side = width // 2
    dp_count = lax.axis_size("dp")
    bits = dp_count.bit_length() - 1
    rank, core = lax.axis_index("dp"), lax.axis_index("fsdp")
    up_order = list(range(bits))
    qkv_cols, out_cols, up_cols = w_qkv.shape[1], w_out.shape[1], w_up.shape[1]
    vec_rows, vec_cols = vectors.shape
    devices = 2 * dp_count

    masks = [(offset & 1) | (offset & 2) << 1 for offset in range(PLANES)]
    plane_bits = [place for place in range(bits) if place not in (0, 2)]
    plane = bit_of(rank, 0) + 2 * bit_of(rank, 2)
    index = jnp.stack([rank, core, plane]).astype(jnp.int32)
    first_col = (vec_cols * (2 * rank + core)).astype(jnp.uint32)
    top = jnp.uint32(0)
    vec_wide = lax.dynamic_update_slice(
        jnp.zeros((16, width), LOW), vectors.astype(LOW), (top, first_col)
    )
    split = -(-(qkv_cols + 8) // 16) * 16
    rows = split + -(-(out_cols + 8) // 16) * 16
    exact = qkv_cols % 8 == 0 and out_cols % 8 == 0 and split == qkv_cols + 8 and rows == split + out_cols + 8
    pack = jnp.concatenate(
        [
            jnp.pad(w_qkv.T.astype(LOW), ((0, split - 8 - qkv_cols), (0, 0))),
            vec_wide[:8],
            jnp.pad(w_out.T.astype(LOW), ((0, rows - split - 8 - out_cols), (0, 0))),
            vec_wide[8:],
        ],
        axis=0,
    )
    pack_one, pack_two = pack[:, :side], pack[:, side:]
    far = up_order[2:][::-1]
    near_one, near_two = [1, 0], [0, 1]
    all_one = gather_relative(pack_one, far, [])
    all_two = gather_relative(pack_two, far, [])
    hidden_low = (w_up.T.astype(LOW), w_down.astype(LOW))
    all_one, all_two, *hidden_low = tie(all_one, all_two, *hidden_low)
    all_one = gather_relative(all_one, near_one, far)
    all_two = gather_relative(all_two, near_two, far)
    hidden_far = [gather_relative(part, far, []).reshape(-1, width) for part in hidden_low]
    all_one, all_two, *hidden_far = tie(all_one, all_two, *hidden_far)
    hidden_near = [
        jnp.stack([part, xor_trade(part, 1 << near[0])])
        for part, near in zip(hidden_far, (near_one, near_two))
    ]
    own_packs = [part.reshape((dp_count, rows, side)) for part in (all_one, all_two)]
    other_packs = [core_trade(part) for part in own_packs]
    packs = (own_packs[0], other_packs[0], own_packs[1], other_packs[1])
    far_count = dp_count // 4
    hidden_rows = far_count * up_cols
    wide_side, out_side = (devices * qkv_cols, side), (devices * out_cols, side)
    if exact:
        projected_low, *sides, vec_full, up_bias = run_kernel(
            unpack_body,
            [((tok_rows, 3 * width), LOW), (wide_side, LOW), (wide_side, LOW)]
            + [(out_side, LOW), (out_side, LOW), ((16, width), WIDE), ((8, hidden_rows), WIDE)],
            (index, *packs, tokens_in),
            [((devices, up_cols), WIDE)],
            scalars=1,
            room=18,
        )
        qkv_sides, out_sides = sides[:2], sides[2:]
    else:
        natural = [
            xor_order(pair(own, other, core, 1), rank, bits).reshape(devices, rows, side)
            for own, other in zip(own_packs, other_packs)
        ]
        qkv_sides = [part[:, :qkv_cols].reshape(wide_side) for part in natural]
        out_sides = [part[:, split : split + out_cols].reshape(out_side) for part in natural]
        vec_full = jnp.concatenate(natural, axis=2).astype(WIDE)
        vec_full = jnp.concatenate([vec_full[:, split - 8 : split], vec_full[:, rows - 8 :]], axis=1)
        vec_full = jnp.sum(vec_full, axis=0)
        qkv_bias = jnp.concatenate([vec_full[4], jnp.zeros((width,), WIDE), vec_full[5]])
        projected = rows_by_cols(tokens_in[:, :side], qkv_sides[0])
        projected = projected + rows_by_cols(tokens_in[:, side:], qkv_sides[1])
        projected_low = (projected + qkv_bias).astype(LOW)
        up_bias = xor_order(vec_full[8:12].reshape(dp_count, 2, up_cols), rank, bits)
        up_bias = up_bias.reshape(far_count, 2, 2, 2, up_cols).transpose(3, 1, 2, 0, 4)
        up_bias = up_bias.reshape(2, 4, hidden_rows)
        up_bias = jnp.where(core == 0, up_bias, up_bias[::-1]).reshape(8, hidden_rows)
    own_kv = projected_low[:, width:]
    other_kv = core_trade(own_kv)
    square = (tok_rows, width)
    context_low, normed, normed_low, unit, scale, probs = run_kernel(
        attend_body,
        [(square, LOW), (square, WIDE), (square, LOW), (square, WIDE), ((tok_rows, 1), WIDE)]
        + [((width // HD, tok_rows, 2 * tok_rows), WIDE)],
        (index, seq_lengths, projected_low, other_kv, *out_sides, tokens_in, vec_full),
        scalars=2,
    )
    hidden_got = [xor_trade(part, 1 << near[1]) for part, near in zip(hidden_near, (near_one, near_two))]
    piece, block = hidden_near[0].shape, (tok_rows, hidden_rows)
    early_act, early_slope, lowered, early = run_kernel(
        early_body,
        [((2,) + block, LOW), ((2,) + block, WIDE), (square, WIDE), MARK],
        (normed_low, up_bias, *hidden_near),
    )
    hidden_got = gate(hidden_got, early)
    pieces = []
    for part, got in zip(hidden_near, hidden_got):
        pieces += [part, got, core_trade(part), core_trade(got)]
    own_act, own_slope, lowered = run_kernel(
        own_body,
        [((2,) + block, LOW), ((2,) + block, WIDE), (square, WIDE)],
        (normed_low, up_bias, early_act, lowered, hidden_got[0], hidden_near[1], hidden_got[1]),
    )
    output, d_normed, g_bias_up, rows_two, *grads = run_kernel(
        hidden_body,
        [(square, LOW), (square, WIDE), ((8, hidden_rows), WIDE), ((3, width), WIDE)]
        + [(piece, LOW)] * 8,
        (index, seq_lengths, normed, normed_low, cotangent, vec_full, up_bias)
        + (lowered, early_act, early_slope, own_act, own_slope, *pieces),
        [((4,) + block, LOW), ((4,) + block, WIDE)],
        room=18,
        scalars=2,
    )
    hidden_orders = (up_order, [1] + up_order[2:] + [0])
    hidden_left = [[bits] + up_order[2:], up_order[2:] + [bits]]
    mark = jnp.zeros(*MARK)
    hidden_sent, mark = summed(
        (grads[1], grads[5]), (core_trade(grads[3]), core_trade(grads[7])), mark, LOW
    )
    hidden_kept, _ = summed(
        (grads[0], grads[4]), (core_trade(grads[2]), core_trade(grads[6])), mark, WIDE
    )
    d_resid_one, d_attended, d_query, own_grad, other_grad, rows_one = run_kernel(
        attend_back_body,
        [(square, WIDE), (square, LOW), (square, LOW)]
        + [((tok_rows, 2 * width), WIDE), ((tok_rows, 2 * width), LOW), ((3, width), WIDE)],
        (d_normed, projected_low, other_kv, probs, *out_sides, unit, scale, vec_full),
    )
    (other_grad,) = gate((other_grad,), mark)
    got_grad = core_trade(other_grad)
    if exact:
        pack_block = ((dp_count, rows, side), LOW)
        d_qkv, *g_sides = run_kernel(
            pack_body,
            [((tok_rows, 3 * width), LOW)] + [pack_block] * 4,
            (index, d_query, own_grad, got_grad, tokens_in, d_attended, context_low)
            + (rows_one, rows_two, g_bias_up),
            [(wide_side, WIDE), (out_side, WIDE), ((devices, up_cols), WIDE), ((16, width), WIDE)],
            scalars=1,
            room=20,
        )
    else:
        d_kv = own_grad + got_grad.astype(WIDE)
        d_qkv = jnp.concatenate([d_query, d_kv.astype(LOW)], axis=1)
        sums = jnp.sum(d_qkv.astype(WIDE), axis=0, keepdims=True)
        g_bias_up = g_bias_up.reshape(2, 4, hidden_rows)
        g_bias_up = jnp.where(core == 0, g_bias_up, g_bias_up[::-1])
        g_bias_up = g_bias_up.reshape(2, 2, 2, far_count, up_cols).transpose(3, 1, 2, 0, 4)
        g_bias_up = xor_order(g_bias_up.reshape(dp_count, 2, up_cols), rank, bits)
        g_rows = [rows_one[:2], rows_two[:2], sums[:, :width], sums[:, 2 * width :]]
        g_rows += [rows_one[2:], rows_two[2:], g_bias_up.reshape(-1, width)]
        g_rows = jnp.concatenate(g_rows + [jnp.zeros((4, width), WIDE)], axis=0).astype(LOW)
        g_sides = []
        for part in range(2):
            at = slice(part * side, (part + 1) * side)
            whole = jnp.broadcast_to(g_rows[None, :, at], (devices, 16, side))
            g_qkv = over_tokens(d_qkv, tokens_in[:, at]).reshape(devices, qkv_cols, side)
            g_out = over_tokens(d_attended, context_low[:, at]).reshape(devices, out_cols, side)
            whole = jnp.concatenate(
                [
                    jnp.pad(g_qkv, ((0, 0), (0, split - 8 - qkv_cols), (0, 0))),
                    whole[:, :8],
                    jnp.pad(g_out, ((0, 0), (0, rows - split - 8 - out_cols), (0, 0))),
                    whole[:, 8:],
                ],
                axis=1,
            )
            whole = xor_order(whole.reshape(dp_count, 2, rows, side), rank, bits)
            g_sides += [pick(whole, core, 1), pick(whole, 1 - core, 1)]
    attn_orders = (up_order, [2, 0, 1] + up_order[3:])
    attn_kept = g_sides[::2]
    attn_got = [core_trade(part) for part in g_sides[1::2]]
    for step in range(bits):
        left = [order[step:] for order in attn_orders]
        attn_kept, attn_sent, mark = stepped(attn_kept, attn_got, mark, left, (rows, side))
        attn_got = [
            xor_trade(sent, 1 << order[step]) for sent, order in zip(attn_sent, attn_orders)
        ]
        got = [xor_trade(sent, 1 << order[step]) for sent, order in zip(hidden_sent, hidden_orders)]
        if step < bits - 1:
            left = [order[step:] for order in hidden_left]
            hidden_kept, hidden_sent, mark = stepped(hidden_kept, got, mark, left, (up_cols, width))
    last = [part.reshape(rows, side) for part in (*attn_kept, *attn_got)]
    last += [part.reshape(up_cols, width) for part in (*hidden_kept, *got)]
    d_tokens = d_resid_one + jnp.concatenate([plain(d_qkv, part) for part in qkv_sides], axis=1)

    piece_rows = max(qkv_cols, up_cols)
    moments = (mom_qkv.T, mom_out.T, mom_up.T, mom_down)
    if exact:
        shapes = [(moment.shape, WIDE) for moment in moments]
        results = run_kernel(
            moment_body,
            [((piece_rows, width), LOW)] * PLANES + shapes + shapes + [((16, width), WIDE)],
            (index, *last, *moments),
            [((PLANES, piece_rows, width), LOW)],
            scalars=1,
        )
        pieces = results[:PLANES]
        grads_t, moments_t = results[PLANES : 2 * PLANES], results[2 * PLANES : 3 * PLANES]
        vec_sums = results[-1]
    else:
        attn = [kept.astype(WIDE) + part.astype(WIDE) for kept, part in zip(last[:2], last[2:4])]
        attn = jnp.concatenate(attn, axis=1)
        grads_t = [attn[:qkv_cols], attn[split : split + out_cols]]
        grads_t += [kept + part.astype(WIDE) for kept, part in zip(last[4:6], last[6:8])]
        vec_sums = jnp.concatenate([attn[split - 8 : split], attn[rows - 8 :]], axis=0)
        moments_t = [momentum_decay * moment + grad for moment, grad in zip(moments, grads_t)]
        stacked = [
            jnp.pad(moment.astype(LOW), ((0, piece_rows - moment.shape[0]), (0, 0)))
            for moment in moments_t
        ]
        stacked = jnp.stack(stacked)
        pieces = [pick(stacked, plane ^ offset, 0) for offset in range(PLANES)]
    grad_qkv_t, grad_out_t, grad_up_t, grad_down = grads_t
    grad_vectors = lax.dynamic_slice(vec_sums, (top, first_col), (vec_rows, vec_cols))
    new_mom_qkv, new_mom_out, new_mom_up = [moment.T for moment in moments_t[:3]]
    new_mom_down = moments_t[3]
    mine = [pieces[0]]
    for offset in range(1, PLANES):
        mine.append(xor_trade(pieces[offset], masks[offset]))
    turned = orthogonal(mine, index, plane_bits)
    back = [turned[0]]
    for offset in range(1, PLANES):
        back.append(xor_trade(turned[offset], masks[offset]))
    hidden = up_cols * devices
    sizes = (3 * width, width, max(width, hidden), max(width, hidden))
    weights = (w_qkv.T, w_out.T, w_up.T, w_down)
    if exact:
        new_weights = run_kernel(
            functools.partial(update_body, sizes),
            [(weight.shape, WIDE) for weight in weights],
            (index, *back, *weights),
            [((PLANES, piece_rows, width), LOW)],
            scalars=1,
        )
    else:
        back = jnp.stack(back)
        new_weights = [
            weight_update(weight, pick(back, plane ^ place, 0)[: weight.shape[0]].astype(WIDE), longest)
            for place, (weight, longest) in enumerate(zip(weights, sizes))
        ]
    new_w_qkv, new_w_out, new_w_up = [weight.T for weight in new_weights[:3]]
    new_w_down = new_weights[3]

    new_first = beta_one * adam_first + (1.0 - beta_one) * grad_vectors
    new_second = beta_two * adam_second + (1.0 - beta_two) * grad_vectors * grad_vectors
    first_hat = new_first / (1.0 - beta_one**STEP)
    second_hat = new_second / (1.0 - beta_two**STEP)
    new_vectors = vectors - adam_rate * first_hat / (jnp.sqrt(second_hat) + adam_epsilon)
    return (
        output,
        d_tokens,
        grad_qkv_t.T,
        grad_out_t.T,
        grad_up_t.T,
        grad_down,
        grad_vectors,
        new_mom_qkv,
        new_mom_out,
        new_mom_up,
        new_mom_down,
        new_w_qkv,
        new_w_out,
        new_w_up,
        new_w_down,
        new_first,
        new_second,
        new_vectors,
    )


def solution(mesh):
    in_specs = (
        P(("dp", "fsdp"), None),
        P(("dp", "fsdp"), None),
        P("dp", None),
        P(None, ("dp", "fsdp")),
        P(None, ("dp", "fsdp")),
        P(None, ("dp", "fsdp")),
        P(("dp", "fsdp"), None),
        P(None, ("dp", "fsdp")),
        P(None, ("dp", "fsdp")),
        P(None, ("dp", "fsdp")),
        P(None, ("dp", "fsdp")),
        P(("dp", "fsdp"), None),
        P(None, ("dp", "fsdp")),
        P(None, ("dp", "fsdp")),
    )
    out_specs = (
        P(("dp", "fsdp"), None),
        P(("dp", "fsdp"), None),
        P(None, ("dp", "fsdp")),
        P(None, ("dp", "fsdp")),
        P(None, ("dp", "fsdp")),
        P(("dp", "fsdp"), None),
        P(None, ("dp", "fsdp")),
        P(None, ("dp", "fsdp")),
        P(None, ("dp", "fsdp")),
        P(None, ("dp", "fsdp")),
        P(("dp", "fsdp"), None),
        P(None, ("dp", "fsdp")),
        P(None, ("dp", "fsdp")),
        P(None, ("dp", "fsdp")),
        P(("dp", "fsdp"), None),
        P(None, ("dp", "fsdp")),
        P(None, ("dp", "fsdp")),
        P(None, ("dp", "fsdp")),
    )
    return jax.shard_map(
        per_device, mesh=mesh, in_specs=in_specs, out_specs=out_specs, check_vma=False
    )
```
